32 devices in a mesh: row: 8 (over y, x, core), col: 4 (over z).
Axes of the slice: x: 2, y: 2, z: 4, core: 2. Of those that a mesh axis runs over, the one named last changes fastest.
Arguments:
- pair: bfloat16 [128, 128, 128], P('row', 'col'), may hold values from -6 to 6
- targets: int32 [128, 128], P('row', 'col'), may hold values from 0 to 63, as said below
- w_gate: bfloat16 [128, 512], replicated, may hold values from -0.5 to 0.5
- w_up: bfloat16 [128, 512], replicated, may hold values from -0.5 to 0.5
- w_out: bfloat16 [512, 128], replicated, may hold values from -0.25 to 0.25
- w_head: bfloat16 [128, 64], replicated, may hold values from -16 to 16
Outputs:
- d_pair: bfloat16 [128, 128, 128], P('row', 'col')
- grad_gate: float32 [128, 512], P('row', 'col')
- grad_up: float32 [128, 512], P('row', 'col')
- grad_out: float32 [512, 128], P('row', 'col')
- grad_head: float32 [128, 64], P('row', 'col')
The draws below stay inside these ranges and needn't reach their ends.
Inputs may be any that keep to these rules, and one draw needn't show every extreme that they name: symmetric: targets[i, j] equals targets[j, i].
All inputs are finite; a program needn't handle non-finite values.
Results may differ from the reference program's by a relative error of at most 0.015.
Values may be sent and summed in bfloat16 or wider, within the bound.
No kernel may reach another device: no remote copies, remote signals or barrier semaphores. Data moves between devices by JAX's collectives and lax.ppermute only.
A program may use at most 64 MiB of HBM per device.

```python
import jax
import jax.numpy as jnp
from jax import lax

C = 128
F = 512
BINS = 64
L = 128


def draw_targets(key, part):
    full = jax.random.randint(key, (L, L), 0, BINS, dtype=jnp.int32)
    first = lax.broadcasted_iota(jnp.int32, (L, L), 0)
    second = lax.broadcasted_iota(jnp.int32, (L, L), 1)
    return jnp.where(first <= second, full, full.T)


def draw_w_head(key, part):
    base = jax.random.normal(jax.random.fold_in(key, 3), (C, BINS), jnp.float32) * 0.2
    return jnp.clip(base, -16.0, 16.0).astype(jnp.bfloat16)


def strengthened(values, key, source, target, parts, factor):
    def block_of(position):
        return (jnp.arange(values.shape[position]) // (values.shape[position] // parts)).reshape((-1,) + (1,) * (values.ndim - 1 - position))

    near = jax.random.permutation(key, parts)[block_of(target)]
    other_side = (block_of(target) + parts // 2) % parts
    return jnp.where((block_of(source) == near) | (block_of(source) == other_side), factor * values, values)


def level_of(stream_key, shape, shards, low, top_value):
    gain, own = 1.0, jax.random.fold_in(stream_key, 6)
    for position, blocks in shards:
        heights = jnp.exp(jax.random.uniform(jax.random.fold_in(own, position), (blocks,), jnp.float32, low / len(shards), top_value / len(shards)))
        gain = gain * jnp.repeat(heights, shape[position] // blocks).reshape([-1 if axis == position else 1 for axis in range(len(shape))])
    return gain


def normal_values(key, shape, spread, most, shards=(), kind=jnp.bfloat16):
    drawn = jax.random.normal(key, shape, jnp.float32) * spread
    if len(shards) > 0:
        drawn = level_of(key, shape, shards, -0.22, 0.18) * drawn
    return jnp.clip(drawn, min=-most, max=most).astype(kind)


def heavy_noise(own_key, extent, spread, bound, split, heavy, kind=jnp.bfloat16):
    array = spread * jax.random.normal(own_key, extent, jnp.float32)
    if split:
        array = array * level_of(own_key, extent, split, -0.22, 0.18)
    return jnp.clip(strengthened(array, jax.random.fold_in(own_key, 3), *heavy), -bound, bound).astype(kind)


def setup_inputs(seed: int = 0) -> dict:
    splits = jax.random.split(jax.random.key(seed), 7)
    return {
        "pair": heavy_noise(splits[0], (L, L, C), 1.0, 6.0, ((0, 8), (1, 4)), (0, 2, 8, 2.0)),
        "targets": draw_targets(jax.random.fold_in(splits[6], 71), 0),
        "w_gate": normal_values(splits[2], (C, F), C ** -0.5, 0.5),
        "w_up": normal_values(splits[3], (C, F), C ** -0.5, 0.5),
        "w_out": normal_values(splits[4], (F, C), F ** -0.5, 0.25),
        "w_head": draw_w_head(jax.random.fold_in(splits[6], 71), 0),
    }


eps = 1e-05

def normalize(flat):
    values = flat.astype(jnp.float32)
    centre = values - lax.optimization_barrier(jnp.mean(values, axis=-1, keepdims=True))
    scale_inv = lax.rsqrt(lax.optimization_barrier(jnp.mean(centre * centre, axis=-1, keepdims=True)) + eps)
    return (centre * scale_inv, scale_inv)

def forward_block(flat, w_gate, w_up, w_out, w_head):
    normed, scale_inv = normalize(flat)
    inputs = normed.astype(jnp.bfloat16)
    gate = jnp.dot(inputs, w_gate, preferred_element_type=jnp.float32)
    upper = jnp.dot(inputs, w_up, preferred_element_type=jnp.float32)
    hidden = (jax.nn.silu(gate) * upper).astype(jnp.bfloat16)
    updated = (flat.astype(jnp.float32) + jnp.dot(hidden, w_out, preferred_element_type=jnp.float32)).astype(jnp.bfloat16)
    logits = jnp.dot(updated, w_head, preferred_element_type=jnp.float32).astype(jnp.bfloat16)
    return (updated, logits)

def backward_block(flat, updated, cotangent, w_gate, w_up, w_out, w_head):
    normed, scale_inv = normalize(flat)
    inputs = normed.astype(jnp.bfloat16)
    gate = jnp.dot(inputs, w_gate, preferred_element_type=jnp.float32)
    upper = jnp.dot(inputs, w_up, preferred_element_type=jnp.float32)
    sigma = jax.nn.sigmoid(gate)
    swish = jax.nn.silu(gate)
    hidden = (swish * upper).astype(jnp.bfloat16)
    d_updated = jnp.dot(cotangent, w_head.T, preferred_element_type=jnp.float32)
    d_upd_b = d_updated.astype(jnp.bfloat16)
    d_hidden = jnp.dot(d_upd_b, w_out.T, preferred_element_type=jnp.float32)
    d_gate = (d_hidden * upper * sigma * (1.0 + gate * (1.0 - sigma))).astype(jnp.bfloat16)
    d_up = (d_hidden * swish).astype(jnp.bfloat16)
    d_inputs = jnp.dot(d_gate, w_gate.T, preferred_element_type=jnp.float32) + jnp.dot(d_up, w_up.T, preferred_element_type=jnp.float32)
    d_norm = (d_inputs - lax.optimization_barrier(jnp.mean(d_inputs, axis=-1, keepdims=True)) - normed * lax.optimization_barrier(jnp.mean(d_inputs * normed, axis=-1, keepdims=True))) * scale_inv
    d_block = (d_updated + d_norm).astype(jnp.bfloat16)
    terms = (jnp.dot(inputs.T, d_gate, preferred_element_type=jnp.float32), jnp.dot(inputs.T, d_up, preferred_element_type=jnp.float32), jnp.dot(hidden.T, d_upd_b, preferred_element_type=jnp.float32), jnp.dot(updated.T, cotangent, preferred_element_type=jnp.float32))
    return (terms, d_block)

def reference(pair, targets, w_gate, w_up, w_out, w_head):
    length = pair.shape[0]
    width = pair.shape[2]
    bins = w_head.shape[1]
    rows_step = 8
    nblocks = length // rows_step
    blocks = pair.reshape(nblocks, rows_step * length, width)
    updated, logits = lax.map(lambda blk: forward_block(blk, w_gate, w_up, w_out, w_head), blocks)
    logits = logits.reshape(length, length, bins)
    summed = logits.astype(jnp.float32) + jnp.transpose(logits, (1, 0, 2)).astype(jnp.float32)
    probs = jax.nn.softmax(summed, axis=-1)
    onehot = (targets[:, :, None] == jnp.arange(bins, dtype=jnp.int32)[None, None, :]).astype(jnp.float32)
    grad_sym = (probs - onehot).astype(jnp.bfloat16)
    cotangent = (grad_sym.astype(jnp.float32) + jnp.transpose(grad_sym, (1, 0, 2)).astype(jnp.float32)).astype(jnp.bfloat16)
    cotangent = cotangent.reshape(nblocks, rows_step * length, bins)

    def accumulate(carry, items):
        flat, upd, cot = items
        terms, d_block = backward_block(flat, upd, cot, w_gate, w_up, w_out, w_head)
        return (tuple((c + t for c, t in zip(carry, terms))), d_block)
    start = (jnp.zeros(w_gate.shape, jnp.float32), jnp.zeros(w_up.shape, jnp.float32), jnp.zeros(w_out.shape, jnp.float32), jnp.zeros(w_head.shape, jnp.float32))
    totals, d_blocks = lax.scan(accumulate, start, (blocks, updated, cotangent))
    d_pair = d_blocks.reshape(length, length, width)
    factor = 1.0 / length
    return (d_pair, totals[0] * factor, totals[1] * factor, totals[2] * factor, totals[3] * factor)
```

```python
import functools

import jax
import jax.numpy as jnp
from jax import lax
from jax.experimental import pallas as pl
from jax.experimental.pallas import tpu as pltpu
from jax.sharding import PartitionSpec as P

eps = 1e-05
f32 = jnp.float32
bf16 = jnp.bfloat16
SMEM = pl.BlockSpec(memory_space=pltpu.SMEM)
VMEM = pl.BlockSpec(memory_space=pltpu.VMEM)


def nn(a, b):
    return lax.dot_general(a, b, (((1,), (0,)), ((), ())), preferred_element_type=f32)


def nt(a, b):
    return lax.dot_general(a, b, (((1,), (1,)), ((), ())), preferred_element_type=f32)


def tn(a, b):
    return lax.dot_general(a, b, (((0,), (0,)), ((), ())), preferred_element_type=f32)


def normalize(flat):
    values = flat.astype(f32)
    centre = values - jnp.mean(values, axis=-1, keepdims=True)
    scale_inv = lax.rsqrt(jnp.mean(centre * centre, axis=-1, keepdims=True) + eps)
    return centre * scale_inv, scale_inv


def sigmoid(v):
    return 1.0 / (1.0 + jnp.exp(-v))


def chunks_of(size, most):
    step = most if size % most == 0 else size
    return [(at, step) for at in range(0, size, step)]


def forward_kernel(q, place, pair, w_gate, w_up, w_out, w_head, updated, logits, *rest):
    sends, halves = rest[:q], rest[q]
    count, width = pair.shape
    hidden_units = w_gate.shape[1]
    side = halves.shape[1]
    flat = pair[...]
    inputs = normalize(flat)[0].astype(bf16)
    total = flat.astype(f32)
    for at, step in chunks_of(hidden_units, 256):
        gate = nn(inputs, w_gate[:, at : at + step])
        upper = nn(inputs, w_up[:, at : at + step])
        hidden = (gate * sigmoid(gate) * upper).astype(bf16)
        total = total + nn(hidden, w_out[at : at + step, :])
    upd = total.astype(bf16)
    updated[...] = upd
    logit = nn(upd, w_head[...]).astype(bf16)
    logits[...] = logit
    edge = 1
    while edge * edge < side:
        edge *= 2
    out_row = lax.broadcasted_iota(jnp.int32, (side, side), 0)
    in_row = lax.broadcasted_iota(jnp.int32, (side, side), 1)
    shift = edge.bit_length() - 1
    wanted = ((out_row & (edge - 1)) << shift) | (out_row >> shift)
    swap = jnp.where(in_row == wanted, 1.0, 0.0).astype(bf16)
    blocks = logit.reshape(edge, q, edge, logit.shape[-1])
    for k in range(q):
        piece = blocks[:, k].reshape(side, logit.shape[-1])
        halves[k] = nn(swap, piece).astype(bf16)
    first = place[0]
    for p in range(q):
        sends[p][...] = halves[lax.rem(first + p, q)]


def backward_kernel(q, packed, place, pair, updated, logits, onehot, w_gate, w_up, w_out, w_head, *rest):
    got, rest = rest[:q], rest[q:]
    d_pair, rest = rest[0], rest[1:]
    mirrored, hot = rest[-2], rest[:-2]
    count, width = pair.shape
    units = w_gate.shape[1]
    bins = w_head.shape[1]
    edge = mirrored.shape[0]
    for p in range(q):
        h = lax.rem(place[0] + q - p, q)
        mirrored[:, h] = got[p][...].reshape(edge, edge, bins)
    summed = logits[...].astype(f32) + mirrored[...].reshape(count, bins).astype(f32)
    powers = jnp.exp(summed - jnp.max(summed, axis=-1, keepdims=True))
    probs = powers / jnp.sum(powers, axis=-1, keepdims=True)
    grad_sym = (probs - onehot[...].astype(f32)).astype(bf16)
    cotangent = (grad_sym.astype(f32) * 2.0).astype(bf16)
    d_updated = nt(cotangent, w_head[...])
    d_upd_b = d_updated.astype(bf16)
    normed, scale_inv = normalize(pair[...])
    inputs = normed.astype(bf16)
    head_term = tn(updated[...], cotangent)
    d_inputs = jnp.zeros((count, width), f32)
    gate_terms, up_terms, out_terms = [], [], []
    for at, step in chunks_of(units, 256):
        gate_w, up_w, out_w = w_gate[:, at : at + step], w_up[:, at : at + step], w_out[at : at + step, :]
        gate = nn(inputs, gate_w)
        upper = nn(inputs, up_w)
        sigma = sigmoid(gate)
        swish = gate * sigma
        hidden = (swish * upper).astype(bf16)
        d_hidden = nt(d_upd_b, out_w)
        d_gate = (d_hidden * upper * sigma * (1.0 + gate * (1.0 - sigma))).astype(bf16)
        d_up = (d_hidden * swish).astype(bf16)
        d_inputs = d_inputs + nt(d_gate, gate_w) + nt(d_up, up_w)
        gate_terms.append(tn(inputs, d_gate))
        up_terms.append(tn(inputs, d_up))
        out_terms.append(tn(hidden, d_upd_b))
    d_norm = (
        d_inputs
        - jnp.mean(d_inputs, axis=-1, keepdims=True)
        - normed * jnp.mean(d_inputs * normed, axis=-1, keepdims=True)
    ) * scale_inv
    d_pair[...] = (d_updated + d_norm).astype(bf16)
    terms = (
        jnp.concatenate(gate_terms, axis=1),
        jnp.concatenate(up_terms, axis=1),
        jnp.concatenate(out_terms, axis=0),
        head_term,
    )
    if not packed:
        for ref, term in zip(hot, terms):
            ref[...] = term.astype(bf16)
        return
    nrow, ncol = packed
    slots = rest[-1]
    lanes = units // ncol
    part, tall = width // nrow, units // nrow
    for d in range(nrow):
        for n in range(2):
            for c in range(ncol):
                at = (n * ncol + c) * part
                slots[d, at : at + part, :] = terms[n][d * part : (d + 1) * part, c * lanes : (c + 1) * lanes].astype(bf16)
        at = 2 * ncol * part
        slots[d, at : at + tall, :] = terms[2][d * tall : (d + 1) * tall, :].astype(bf16)
        piece = terms[3][d * part : (d + 1) * part, :]
        piece = jnp.concatenate([piece, jnp.zeros((part, lanes - bins), f32)], axis=1)
        slots[d, at + tall : at + tall + part, :] = piece.astype(bf16)
    for p in range(nrow):
        hot[p][...] = slots[lax.rem(place[1] + p, nrow)]


def row_sum_kernel(shapes, place, *rest):
    nrow, ncol, width, units, bins = shapes
    terms, hot, slots = rest[:nrow], rest[nrow:-1], rest[-1]
    lanes, part, tall = units // ncol, width // nrow, units // nrow
    total = terms[0][...].astype(f32)
    for term in terms[1:]:
        total = total + term[...].astype(f32)
    narrow, few = width // ncol, bins // ncol
    group = lanes // narrow
    at = 2 * ncol * part
    out = total[at : at + tall]
    head = total[at + tall : at + tall + part]
    deep = tall // group
    for c in range(ncol):
        slots[c, 0:part] = total[c * part : (c + 1) * part].astype(bf16)
        slots[c, part : 2 * part] = total[(ncol + c) * part : (ncol + c + 1) * part].astype(bf16)
        pieces = [out[k * deep : (k + 1) * deep, c * narrow : (c + 1) * narrow] for k in range(group)]
        slots[c, 2 * part : 2 * part + deep] = jnp.concatenate(pieces, axis=1).astype(bf16)
        piece = head[:, c * few : (c + 1) * few]
        piece = jnp.concatenate([piece, jnp.zeros((part, lanes - few), f32)], axis=1)
        slots[c, 2 * part + deep : 3 * part + deep] = piece.astype(bf16)
    for p in range(ncol):
        hot[p][...] = slots[lax.rem(place[2] + p, ncol)]


def col_sum_kernel(shapes, factor, *rest):
    nrow, ncol, width, units, bins = shapes
    terms, (gate, up, out, head) = rest[:ncol], rest[ncol:]
    lanes, part, tall = units // ncol, width // nrow, units // nrow
    total = terms[0][...].astype(f32)
    for term in terms[1:]:
        total = total + term[...].astype(f32)
    total = total * factor
    narrow, few = width // ncol, bins // ncol
    group = lanes // narrow
    deep = tall // group
    gate[...] = total[0:part]
    up[...] = total[part : 2 * part]
    for k in range(group):
        out[k * deep : (k + 1) * deep, :] = total[2 * part : 2 * part + deep, k * narrow : (k + 1) * narrow]
    head[...] = total[2 * part + deep : 3 * part + deep, 0:few]


def shaped(shape, kind):
    return jax.ShapeDtypeStruct(shape, kind)


def ring_permutes(values, axis, size):
    return [
        lax.ppermute(value, axis, [(s, (s + p) % size) for s in range(size)])
        for p, value in enumerate(values, start=1)
    ]


def body(pair, targets, w_gate, w_up, w_out, w_head):
    rows, cols, width = pair.shape
    units = w_gate.shape[1]
    bins = w_head.shape[1]
    count = rows * cols
    nrow, ncol = lax.axis_size("row"), lax.axis_size("col")
    q = nrow // ncol
    side = count // q
    row, col = lax.axis_index("row"), lax.axis_index("col")
    place = jnp.stack([lax.rem(row, q), row, col]).astype(jnp.int32)
    flat = pair.reshape(count, width)
    params = pltpu.CompilerParams(vmem_limit_bytes=40 * 1024 * 1024)

    updated, logits, *sends = pl.pallas_call(
        functools.partial(forward_kernel, q),
        out_shape=[shaped((count, width), bf16), shaped((count, bins), bf16)] + [shaped((side, bins), bf16)] * q,
        in_specs=[SMEM] + [VMEM] * 5,
        out_specs=[VMEM] * (2 + q),
        scratch_shapes=[pltpu.VMEM((q, side, bins), bf16)],
        compiler_params=params,
        name="forward",
    )(place, flat, w_gate, w_up, w_out, w_head)

    got = []
    for p in range(q):
        pairs = [
            (r * ncol + c, (q * c + (r % q + p) % q) * ncol + r // q) for r in range(nrow) for c in range(ncol)
        ]
        got.append(lax.ppermute(sends[p], ("row", "col"), pairs))
    onehot = (targets.reshape(count)[:, None] == jnp.arange(bins, dtype=jnp.int32)[None, :]).astype(bf16)

    part, tall = width // nrow, units // nrow
    lanes = units // ncol
    fits = (
        part % 16 == 0 and lanes == width and width % 128 == 0 and bins <= lanes
        and lanes % (width // ncol) == 0 and (tall // (lanes // (width // ncol))) % 16 == 0
    )
    height = 2 * ncol * part + tall + part
    if fits:
        hot_shapes = [shaped((height, lanes), bf16)] * nrow
        slots = pltpu.VMEM((nrow, height, lanes), bf16)
    else:
        hot_shapes = [shaped(w.shape, bf16) for w in (w_gate, w_up, w_out, w_head)]
        slots = pltpu.VMEM((16, 128), bf16)
    d_pair, *hot = pl.pallas_call(
        functools.partial(backward_kernel, q, (nrow, ncol) if fits else None),
        out_shape=[shaped((count, width), bf16)] + hot_shapes,
        in_specs=[SMEM] + [VMEM] * (8 + q),
        out_specs=[VMEM] * (1 + len(hot_shapes)),
        scratch_shapes=[pltpu.VMEM((rows, q, rows, bins), bf16), slots],
        compiler_params=params,
        name="backward",
    )(place, flat, updated, logits, onehot, w_gate, w_up, w_out, w_head, *got)
    d_pair = d_pair.reshape(rows, cols, width)
    factor = 1.0 / (rows * nrow)
    if not fits:
        owned = []
        for term in hot:
            mine = lax.psum_scatter(term, "row", scatter_dimension=0, tiled=True).astype(f32)
            owned.append(lax.psum_scatter(mine, "col", scatter_dimension=1, tiled=True) * factor)
        return (d_pair, *owned)

    shapes = (nrow, ncol, width, units, bins)
    short = 3 * part + tall // (lanes // (width // ncol))
    terms = [hot[0]] + ring_permutes(hot[1:], "row", nrow)
    hot = pl.pallas_call(
        functools.partial(row_sum_kernel, shapes),
        out_shape=[shaped((short, lanes), bf16)] * ncol,
        in_specs=[SMEM] + [VMEM] * nrow,
        out_specs=[VMEM] * ncol,
        scratch_shapes=[pltpu.VMEM((ncol, short, lanes), bf16)],
        compiler_params=params,
        name="row_sum",
    )(place, *terms)
    terms = [hot[0]] + ring_permutes(hot[1:], "col", ncol)
    owned = pl.pallas_call(
        functools.partial(col_sum_kernel, shapes, factor),
        out_shape=[
            shaped((part, lanes), f32),
            shaped((part, lanes), f32),
            shaped((tall, width // ncol), f32),
            shaped((part, bins // ncol), f32),
        ],
        in_specs=[VMEM] * ncol,
        out_specs=[VMEM] * 4,
        compiler_params=params,
        name="col_sum",
    )(*terms)
    return (d_pair, *owned)


def solution(mesh):
    placed = (P("row", "col", None), P("row", "col"), P(), P(), P(), P())
    return jax.shard_map(
        body,
        mesh=mesh,
        in_specs=placed,
        out_specs=(P("row", "col", None), P("row", "col"), P("row", "col"), P("row", "col"), P("row", "col")),
        check_vma=False,
    )
```

```python
import functools

import jax
import jax.numpy as jnp
from jax import lax
from jax.experimental import pallas as pl
from jax.experimental.pallas import tpu as pltpu
from jax.sharding import PartitionSpec as P

eps = 1e-05
f32 = jnp.float32
bf16 = jnp.bfloat16
HBM = pl.BlockSpec(memory_space=pltpu.HBM)
VMEM = pl.BlockSpec(memory_space=pltpu.VMEM)
PARAMS = pltpu.CompilerParams(vmem_limit_bytes=24 * 1024 * 1024)


def nn(a, b):
    return lax.dot_general(a, b, (((1,), (0,)), ((), ())), preferred_element_type=f32)


def nt(a, b):
    return lax.dot_general(a, b, (((1,), (1,)), ((), ())), preferred_element_type=f32)


def tn(a, b):
    return lax.dot_general(a, b, (((0,), (0,)), ((), ())), preferred_element_type=f32)


def normalize(flat):
    values = flat.astype(f32)
    centre = values - jnp.mean(values, axis=-1, keepdims=True)
    scale_inv = lax.rsqrt(jnp.mean(centre * centre, axis=-1, keepdims=True) + eps)
    return centre * scale_inv, scale_inv


def sigmoid(v):
    return 0.5 * jnp.tanh(0.5 * v) + 0.5


def chunks_of(size, most):
    step = most if size % most == 0 else size
    return [(at, step) for at in range(0, size, step)]


def partner(s, p, n):
    if n & (n - 1) == 0:
        return s ^ p
    return (s + p) % n if isinstance(s, int) else lax.rem(s + p, n)


def lane_packs(bins, side):
    packs = max(1, 128 // bins)
    return packs if (side // packs) % 16 == 0 else 1


def forward_kernel(q, pair_hbm, gate_hbm, up_hbm, out_hbm, head_hbm, updated, logits, *rest):
    sends, (pair, w_gate, w_up, w_out, w_head, halves, sems) = rest[:q], rest[q:]
    copies = [
        pltpu.make_async_copy(source, target, sems.at[i])
        for i, (source, target) in enumerate(
            ((pair_hbm, pair), (gate_hbm, w_gate), (up_hbm, w_up), (out_hbm, w_out), (head_hbm, w_head))
        )
    ]
    for copy in copies:
        copy.start()
    count, width = pair.shape
    bins = w_head.shape[0]
    side = count // q
    edge = 1
    while edge * edge < side:
        edge *= 2
    shift = edge.bit_length() - 1
    out_row = lax.broadcasted_iota(jnp.int32, (side, side), 0)
    in_row = lax.broadcasted_iota(jnp.int32, (side, side), 1)
    wanted = ((out_row & (edge - 1)) << shift) | (out_row >> shift)
    swap = jnp.where(in_row == wanted, 1.0, 0.0).astype(bf16)
    copies[0].wait()
    flat = pair[...]
    inputs = normalize(flat)[0].astype(bf16)
    total = flat.astype(f32)
    copies[1].wait()
    copies[2].wait()
    copies[3].wait()
    for at, step in chunks_of(w_gate.shape[1], 256):
        gate = nn(inputs, w_gate[:, at : at + step])
        upper = nn(inputs, w_up[:, at : at + step])
        hidden = (gate * sigmoid(gate) * upper).astype(bf16)
        total = total + nn(hidden, w_out[at : at + step, :])
    upd = total.astype(bf16)
    updated[...] = upd
    copies[4].wait()
    logit = nt(upd, w_head[...]).astype(bf16)
    logits[...] = logit
    blocks = logit.reshape(edge, q, edge, bins)
    packs = lane_packs(bins, side)
    deep = side // packs
    for k in range(q):
        piece = nn(swap, blocks[:, k].reshape(side, bins))
        if packs > 1:
            piece = jnp.concatenate([piece[u * deep : (u + 1) * deep] for u in range(packs)], axis=1)
        halves[k] = piece.astype(bf16)
    first = lax.rem(lax.axis_index("row"), q)
    for p in range(q):
        sends[p][...] = halves[lax.rem(first + p, q)]


def prepare_kernel(pair, updated, w_gate, w_up, inputs_t, updated_t, hidden, slope, swish, normed, scale):
    normal, scale_inv = normalize(pair[...])
    normed[...] = normal
    scale[...] = jnp.broadcast_to(scale_inv, scale.shape)
    inputs = normal.astype(bf16)
    inputs_t[...] = inputs.T
    updated_t[...] = updated[...].T
    for at, step in chunks_of(w_gate.shape[1], 256):
        span = slice(at, at + step)
        gate = nn(inputs, w_gate[:, span])
        upper = nn(inputs, w_up[:, span])
        sigma = sigmoid(gate)
        swished = gate * sigma
        swish[:, span] = swished
        hidden[:, span] = (swished * upper).astype(bf16)
        slope[:, span] = upper * sigma * (1.0 + gate * (1.0 - sigma))


def backward_kernel(q, packed, inputs_t, updated_t, hidden, slope, swish, logits, onehot, w_out, w_head, *rest):
    got, (d_updated, d_gate, d_up, *hot), mirrored, slots = rest[:q], rest[q:-2], rest[-2], rest[-1]
    count, bins = logits.shape
    width, units = inputs_t.shape[0], hidden.shape[1]
    edge = mirrored.shape[0]
    side = count // q
    packs = lane_packs(bins, side)
    own = lax.rem(lax.axis_index("row"), q)
    for p in range(q):
        h = lax.rem(own + q - p, q)
        piece = got[p][...]
        for u in range(packs):
            mirrored[u * (edge // packs) : (u + 1) * (edge // packs), h] = (
                piece[:, u * bins : (u + 1) * bins].astype(f32).reshape(edge // packs, edge, bins)
            )
    summed = logits[...].astype(f32) + mirrored[...].reshape(count, bins)
    powers = jnp.exp(summed - jnp.max(summed, axis=-1, keepdims=True))
    probs = powers / jnp.sum(powers, axis=-1, keepdims=True)
    grad_sym = (probs - onehot[...].astype(f32)).astype(bf16)
    cotangent = (grad_sym.astype(f32) * 2.0).astype(bf16)
    d_upd = nn(cotangent, w_head[...])
    d_updated[...] = d_upd
    d_upd_b = d_upd.astype(bf16)
    d_upd_t = d_upd_b.T
    gate_terms, up_terms, out_terms = [], [], []
    for at, step in chunks_of(units, 256):
        span = slice(at, at + step)
        d_hidden = nt(d_upd_b, w_out[span, :])
        d_gate_part = (d_hidden * slope[:, span]).astype(bf16)
        d_up_part = (d_hidden * swish[:, span]).astype(bf16)
        d_gate[:, span] = d_gate_part
        d_up[:, span] = d_up_part
        gate_terms.append(nn(inputs_t[...], d_gate_part))
        up_terms.append(nn(inputs_t[...], d_up_part))
        out_terms.append(nn(d_upd_t, hidden[:, span]))
    gate_term, up_term, out_term = (jnp.concatenate(t, axis=1) for t in (gate_terms, up_terms, out_terms))
    head_term = nn(updated_t[...], cotangent)
    if not packed:
        for ref, term in zip(hot, (gate_term, up_term, out_term, head_term)):
            ref[...] = term.astype(bf16)
        return
    nrow, ncol = packed
    groups = nrow // q
    lanes, part, tall = units // ncol, width // nrow, units // nrow
    deep = width // q
    for k in range(q):
        for a in range(groups):
            r = a * q + k
            at = 0
            for term in (gate_term, up_term):
                for c in range(ncol):
                    piece = term[r * part : (r + 1) * part, c * lanes : (c + 1) * lanes]
                    slots[k, a, at : at + part] = piece.astype(bf16)
                    at += part
            pieces = [out_term[u * deep : (u + 1) * deep, r * tall : (r + 1) * tall] for u in range(q)]
            slots[k, a, at : at + deep] = jnp.concatenate(pieces, axis=1).astype(bf16)
            at += deep
            piece = head_term[r * part : (r + 1) * part, :]
            piece = jnp.concatenate([piece, jnp.zeros((part, lanes - bins), f32)], axis=1)
            slots[k, a, at : at + part] = piece.astype(bf16)
    for p in range(q):
        hot[p][...] = slots[partner(own, p, q)]


def input_kernel(d_gate, d_up, d_updated, normed, scale, w_gate, w_up, d_pair):
    d_inputs = nt(d_gate[...], w_gate[...]) + nt(d_up[...], w_up[...])
    normal = normed[...]
    d_norm = (
        d_inputs
        - jnp.mean(d_inputs, axis=-1, keepdims=True)
        - normal * jnp.mean(d_inputs * normal, axis=-1, keepdims=True)
    ) * scale[...]
    d_pair[...] = (d_updated[...] + d_norm).astype(bf16)


def core_sum_kernel(q, groups, *rest):
    terms, hot = rest[:q], rest[q:]
    mine = lax.axis_index("row") // q
    for p in range(groups):
        a = partner(mine, p, groups)
        total = terms[0][a].astype(f32)
        for term in terms[1:]:
            total = total + term[a].astype(f32)
        hot[p][...] = total.astype(bf16)


def chip_sum_kernel(q, groups, ncol, shapes, *rest):
    terms, hot, slots = rest[:groups], rest[groups:-1], rest[-1]
    part, lanes, deep, tall, few = shapes
    total = terms[0][...].astype(f32)
    for term in terms[1:]:
        total = total + term[...].astype(f32)
    at = 2 * ncol * part
    out = total[at : at + deep]
    head = total[at + deep : at + deep + part]
    narrow = deep * q // ncol
    fold = lanes // tall
    short = narrow // fold
    for c in range(ncol):
        slots[c, 0:part] = total[c * part : (c + 1) * part].astype(bf16)
        slots[c, part : 2 * part] = total[(ncol + c) * part : (ncol + c + 1) * part].astype(bf16)
        u, top = (c * narrow) // deep, (c * narrow) % deep
        block = out[top : top + narrow, u * tall : (u + 1) * tall]
        block = jnp.concatenate([block[v * short : (v + 1) * short] for v in range(fold)], axis=1)
        slots[c, 2 * part : 2 * part + short] = block.astype(bf16)
        piece = jnp.concatenate([head[:, c * few : (c + 1) * few], jnp.zeros((part, lanes - few), f32)], axis=1)
        slots[c, 2 * part + short : 3 * part + short] = piece.astype(bf16)
    for p in range(ncol):
        hot[p][...] = slots[partner(lax.axis_index("col"), p, ncol)]


def col_sum_kernel(shapes, factor, *rest):
    terms, (gate, up, out, head) = rest[:-4], rest[-4:]
    part, lanes, tall, few = shapes
    total = terms[0][...].astype(f32)
    for term in terms[1:]:
        total = total + term[...].astype(f32)
    total = total * factor
    fold = lanes // tall
    short = out.shape[0] // fold
    gate[...] = total[0:part]
    up[...] = total[part : 2 * part]
    for v in range(fold):
        out[v * short : (v + 1) * short, :] = total[2 * part : 2 * part + short, v * tall : (v + 1) * tall]
    head[...] = total[2 * part + short : 3 * part + short, 0:few]


def shaped(shape, kind):
    return jax.ShapeDtypeStruct(shape, kind)


def cost(flops, moved):
    return pl.CostEstimate(flops=flops, bytes_accessed=moved, transcendentals=0)


def body(pair, targets, w_gate, w_up, w_out, w_head):
    rows, cols, width = pair.shape
    units = w_gate.shape[1]
    bins = w_head.shape[1]
    count = rows * cols
    nrow, ncol = lax.axis_size("row"), lax.axis_size("col")
    q = nrow // ncol
    groups = nrow // q
    side = count // q
    packs = lane_packs(bins, side)
    flat = pair.reshape(count, width)
    head_t = w_head.T
    piece = (side // packs, bins * packs)

    updated, logits, *sends = pl.pallas_call(
        functools.partial(forward_kernel, q),
        out_shape=[shaped((count, width), bf16), shaped((count, bins), bf16)] + [shaped(piece, bf16)] * q,
        in_specs=[HBM] * 5,
        out_specs=[VMEM] * (2 + q),
        scratch_shapes=[
            pltpu.VMEM((count, width), bf16),
            pltpu.VMEM(w_gate.shape, bf16),
            pltpu.VMEM(w_up.shape, bf16),
            pltpu.VMEM(w_out.shape, bf16),
            pltpu.VMEM(head_t.shape, bf16),
            pltpu.VMEM((q, *piece), bf16),
            pltpu.SemaphoreType.DMA((5,)),
        ],
        compiler_params=PARAMS,
        name="forward",
    )(*(pltpu.with_memory_space_constraint(x, pltpu.HBM) for x in (flat, w_gate, w_up, w_out, head_t)))

    got = []
    for p in range(q):
        pairs = [
            (r * ncol + c, (q * c + (r % q + p) % q) * ncol + r // q) for r in range(nrow) for c in range(ncol)
        ]
        got.append(lax.ppermute(sends[p], ("row", "col"), pairs))
    onehot = (targets.reshape(count)[:, None] == jnp.arange(bins, dtype=jnp.int32)[None, :]).astype(bf16)
    inputs_t, updated_t, hidden, slope, swish, normed, scale = pl.pallas_call(
        prepare_kernel,
        out_shape=[
            shaped((width, count), bf16),
            shaped((width, count), bf16),
            shaped((count, units), bf16),
            shaped((count, units), f32),
            shaped((count, units), f32),
            shaped((count, width), f32),
            shaped((count, width), f32),
        ],
        in_specs=[VMEM] * 4,
        out_specs=[VMEM] * 7,
        compiler_params=PARAMS,
        cost_estimate=cost(4 * count * width * units, 4 * count * units),
        name="prepare",
    )(flat, updated, w_gate, w_up)

    part, tall, few = width // nrow, units // nrow, bins // ncol
    lanes, deep = units // ncol, width // q
    fits = (
        part % 16 == 0 and lanes == 128 and tall * q == lanes and bins <= lanes and deep % (width // ncol) == 0
        and (width // ncol * tall // lanes) % 16 == 0
    )
    height = 2 * ncol * part + deep + part
    if fits:
        hot_shapes = [shaped((groups, height, lanes), bf16)] * q
        slots = pltpu.VMEM((q, groups, height, lanes), bf16)
    else:
        hot_shapes = [shaped((width, n), bf16) for n in (units, units, units, bins)]
        slots = pltpu.VMEM((16, 128), bf16)
    d_updated, d_gate, d_up, *hot = pl.pallas_call(
        functools.partial(backward_kernel, q, (nrow, ncol) if fits else None),
        out_shape=[shaped((count, width), f32)] + [shaped((count, units), bf16)] * 2 + hot_shapes,
        in_specs=[VMEM] * (9 + q),
        out_specs=[VMEM] * (3 + len(hot_shapes)),
        scratch_shapes=[pltpu.VMEM((rows, q, cols // q, bins), f32), slots],
        compiler_params=PARAMS,
        cost_estimate=cost(8 * count * width * units, 4 * count * units),
        name="backward",
    )(inputs_t, updated_t, hidden, slope, swish, logits, onehot, w_out, head_t, *got)

    d_pair = pl.pallas_call(
        input_kernel,
        out_shape=shaped((count, width), bf16),
        in_specs=[VMEM] * 7,
        out_specs=VMEM,
        compiler_params=PARAMS,
        cost_estimate=cost(4 * count * width * units, 4 * count * units),
        name="d_inputs",
    )(d_gate, d_up, d_updated, normed, scale, w_gate, w_up)
    d_pair = d_pair.reshape(rows, cols, width)
    factor = 1.0 / (rows * nrow)
    if not fits:
        owned = []
        hot[2] = hot[2].T
        for term in hot:
            mine = lax.psum_scatter(term, "row", scatter_dimension=0, tiled=True).astype(f32)
            owned.append(lax.psum_scatter(mine, "col", scatter_dimension=1, tiled=True) * factor)
        return (d_pair, *owned)

    terms = [hot[0]]
    for p in range(1, q):
        terms.append(lax.ppermute(hot[p], "row", [(s, s - s % q + partner(s % q, p, q)) for s in range(nrow)]))
    hot = pl.pallas_call(
        functools.partial(core_sum_kernel, q, groups),
        out_shape=[shaped((height, lanes), bf16)] * groups,
        in_specs=[VMEM] * q,
        out_specs=[VMEM] * groups,
        compiler_params=PARAMS,
        name="core_sum",
    )(*terms)
    terms = [hot[0]]
    for p in range(1, groups):
        terms.append(lax.ppermute(hot[p], "row", [(s, partner(s // q, p, groups) * q + s % q) for s in range(nrow)]))
    short = 3 * part + width // ncol * tall // lanes
    hot = pl.pallas_call(
        functools.partial(chip_sum_kernel, q, groups, ncol, (part, lanes, deep, tall, few)),
        out_shape=[shaped((short, lanes), bf16)] * ncol,
        in_specs=[VMEM] * groups,
        out_specs=[VMEM] * ncol,
        scratch_shapes=[pltpu.VMEM((ncol, short, lanes), bf16)],
        compiler_params=PARAMS,
        name="chip_sum",
    )(*terms)
    terms = [hot[0]]
    for p in range(1, ncol):
        terms.append(lax.ppermute(hot[p], "col", [(s, partner(s, p, ncol)) for s in range(ncol)]))
    gate, up, out, head = pl.pallas_call(
        functools.partial(col_sum_kernel, (part, lanes, tall, few), factor),
        out_shape=[
            shaped((part, lanes), f32),
            shaped((part, lanes), f32),
            shaped((width // ncol, tall), f32),
            shaped((part, few), f32),
        ],
        in_specs=[VMEM] * ncol,
        out_specs=[VMEM] * 4,
        compiler_params=PARAMS,
        name="col_sum",
    )(*terms)
    return d_pair, gate, up, out.T, head


def solution(mesh):
    placed = (P("row", "col", None), P("row", "col"), P(), P(), P(), P())
    return jax.shard_map(
        body,
        mesh=mesh,
        in_specs=placed,
        out_specs=(P("row", "col", None), P("row", "col"), P("row", "col"), P("row", "col"), P("row", "col")),
        check_vma=False,
    )
```

```python
import functools

import jax
import jax.numpy as jnp
from jax import lax
from jax.experimental import pallas as pl
from jax.experimental.pallas import tpu as pltpu
from jax.sharding import PartitionSpec as P

eps = 1e-05
f32 = jnp.float32
bf16 = jnp.bfloat16
HBM = pl.BlockSpec(memory_space=pltpu.HBM)
VMEM = pl.BlockSpec(memory_space=pltpu.VMEM)
PARAMS = pltpu.CompilerParams(vmem_limit_bytes=24 * 1024 * 1024)


def nn(a, b):
    return lax.dot_general(a, b, (((1,), (0,)), ((), ())), preferred_element_type=f32)


def nt(a, b):
    return lax.dot_general(a, b, (((1,), (1,)), ((), ())), preferred_element_type=f32)


def tn(a, b):
    return lax.dot_general(a, b, (((0,), (0,)), ((), ())), preferred_element_type=f32)


def normalize(flat):
    values = flat.astype(f32)
    centre = values - jnp.mean(values, axis=-1, keepdims=True)
    scale_inv = lax.rsqrt(jnp.mean(centre * centre, axis=-1, keepdims=True) + eps)
    return centre * scale_inv, scale_inv


def sigmoid(v):
    return 0.5 * jnp.tanh(0.5 * v) + 0.5


def chunks_of(size, most):
    step = most if size % most == 0 else size
    return [(at, step) for at in range(0, size, step)]


def partner(s, p, n):
    if n & (n - 1) == 0:
        return s ^ p
    return (s + p) % n if isinstance(s, int) else lax.rem(s + p, n)


def lane_packs(bins, side):
    packs = max(1, 128 // bins)
    return packs if (side // packs) % 16 == 0 else 1


def forward_kernel(q, *refs):
    sources, kept, (updated, logits) = refs[:6], refs[6:12], refs[12:14]
    sends, (halves, sems) = refs[14 : 14 + q], refs[14 + q :]
    pair, w_gate, w_up, w_out, w_head, _ = kept
    copies = [
        pltpu.make_async_copy(source, target, sems.at[i]) for i, (source, target) in enumerate(zip(sources, kept))
    ]
    for copy in copies:
        copy.start()
    count, width = pair.shape
    bins = w_head.shape[0]
    side = count // q
    edge = 1
    while edge * edge < side:
        edge *= 2
    shift = edge.bit_length() - 1
    out_row = lax.broadcasted_iota(jnp.int32, (side, side), 0)
    in_row = lax.broadcasted_iota(jnp.int32, (side, side), 1)
    wanted = ((out_row & (edge - 1)) << shift) | (out_row >> shift)
    swap = jnp.where(in_row == wanted, 1.0, 0.0).astype(bf16)
    copies[0].wait()
    flat = pair[...]
    inputs = normalize(flat)[0].astype(bf16)
    total = flat.astype(f32)
    copies[1].wait()
    copies[2].wait()
    copies[3].wait()
    for at, step in chunks_of(w_gate.shape[1], 256):
        gate = nn(inputs, w_gate[:, at : at + step])
        upper = nn(inputs, w_up[:, at : at + step])
        hidden = (gate * sigmoid(gate) * upper).astype(bf16)
        total = total + nn(hidden, w_out[at : at + step, :])
    upd = total.astype(bf16)
    updated[...] = upd
    copies[4].wait()
    logit = nt(upd, w_head[...]).astype(bf16)
    logits[...] = logit
    blocks = logit.reshape(edge, q, edge, bins)
    packs = lane_packs(bins, side)
    deep = side // packs
    for k in range(q):
        piece = nn(swap, blocks[:, k].reshape(side, bins))
        if packs > 1:
            piece = jnp.concatenate([piece[u * deep : (u + 1) * deep] for u in range(packs)], axis=1)
        halves[k] = piece.astype(bf16)
    first = lax.rem(lax.axis_index("row"), q)
    for p in range(q):
        sends[p][...] = halves[lax.rem(first + p, q)]
    copies[5].wait()


def prepare_kernel(pair, updated, w_gate, w_up, inputs_t, updated_t, hidden, slope, swish, normed, scale):
    normal, scale_inv = normalize(pair[...])
    normed[...] = normal
    scale[...] = jnp.broadcast_to(scale_inv, scale.shape)
    inputs = normal.astype(bf16)
    inputs_t[...] = inputs.T
    updated_t[...] = updated[...].T
    for at, step in chunks_of(w_gate.shape[1], 256):
        span = slice(at, at + step)
        gate = nn(inputs, w_gate[:, span])
        upper = nn(inputs, w_up[:, span])
        sigma = sigmoid(gate)
        swished = gate * sigma
        swish[:, span] = swished
        hidden[:, span] = (swished * upper).astype(bf16)
        slope[:, span] = upper * sigma * (1.0 + gate * (1.0 - sigma))


def backward_kernel(q, packed, inputs_t, updated_t, hidden, slope, swish, logits, onehot, w_out, w_head, *rest):
    got, (d_updated, d_gate, d_up, *hot), mirrored, slots = rest[:q], rest[q:-2], rest[-2], rest[-1]
    count, bins = logits.shape
    width, units = inputs_t.shape[0], hidden.shape[1]
    edge = mirrored.shape[0]
    side = count // q
    packs = lane_packs(bins, side)
    own = lax.rem(lax.axis_index("row"), q)
    for p in range(q):
        h = lax.rem(own + q - p, q)
        piece = got[p][...]
        for u in range(packs):
            mirrored[u * (edge // packs) : (u + 1) * (edge // packs), h] = (
                piece[:, u * bins : (u + 1) * bins].astype(f32).reshape(edge // packs, edge, bins)
            )
    summed = logits[...].astype(f32) + mirrored[...].reshape(count, bins)
    powers = jnp.exp(summed - jnp.max(summed, axis=-1, keepdims=True))
    probs = powers / jnp.sum(powers, axis=-1, keepdims=True)
    grad_sym = (probs - onehot[...].astype(f32)).astype(bf16)
    cotangent = (grad_sym.astype(f32) * 2.0).astype(bf16)
    d_upd = nn(cotangent, w_head[...])
    d_updated[...] = d_upd
    d_upd_b = d_upd.astype(bf16)
    d_upd_t = d_upd_b.T
    gate_terms, up_terms, out_terms = [], [], []
    for at, step in chunks_of(units, 256):
        span = slice(at, at + step)
        d_hidden = nt(d_upd_b, w_out[span, :])
        d_gate_part = (d_hidden * slope[:, span]).astype(bf16)
        d_up_part = (d_hidden * swish[:, span]).astype(bf16)
        d_gate[:, span] = d_gate_part
        d_up[:, span] = d_up_part
        gate_terms.append(nn(inputs_t[...], d_gate_part))
        up_terms.append(nn(inputs_t[...], d_up_part))
        out_terms.append(nn(d_upd_t, hidden[:, span]))
    gate_term, up_term, out_term = (jnp.concatenate(t, axis=1) for t in (gate_terms, up_terms, out_terms))
    head_term = nn(updated_t[...], cotangent)
    if not packed:
        for ref, term in zip(hot, (gate_term, up_term, out_term, head_term)):
            ref[...] = term.astype(bf16)
        return
    nrow, ncol = packed
    groups = nrow // q
    lanes, part, tall = units // ncol, width // nrow, units // nrow
    deep = width // q
    for k in range(q):
        for a in range(groups):
            r = a * q + k
            at = 0
            for term in (gate_term, up_term):
                for c in range(ncol):
                    piece = term[r * part : (r + 1) * part, c * lanes : (c + 1) * lanes]
                    slots[k, a, at : at + part] = piece.astype(bf16)
                    at += part
            pieces = [out_term[u * deep : (u + 1) * deep, r * tall : (r + 1) * tall] for u in range(q)]
            slots[k, a, at : at + deep] = jnp.concatenate(pieces, axis=1).astype(bf16)
            at += deep
            piece = head_term[r * part : (r + 1) * part, :]
            piece = jnp.concatenate([piece, jnp.zeros((part, lanes - bins), f32)], axis=1)
            slots[k, a, at : at + part] = piece.astype(bf16)
    for p in range(q):
        hot[p][...] = slots[partner(own, p, q)]


def input_kernel(d_gate, d_up, d_updated, normed, scale, w_gate, w_up, d_pair):
    d_inputs = nt(d_gate[...], w_gate[...]) + nt(d_up[...], w_up[...])
    normal = normed[...]
    d_norm = (
        d_inputs
        - jnp.mean(d_inputs, axis=-1, keepdims=True)
        - normal * jnp.mean(d_inputs * normal, axis=-1, keepdims=True)
    ) * scale[...]
    d_pair[...] = (d_updated[...] + d_norm).astype(bf16)


def core_sum_kernel(q, groups, *rest):
    terms, hot = rest[:q], rest[q:]
    mine = lax.axis_index("row") // q
    for p in range(groups):
        a = partner(mine, p, groups)
        total = terms[0][a].astype(f32)
        for term in terms[1:]:
            total = total + term[a].astype(f32)
        hot[p][...] = total.astype(bf16)


def chip_sum_kernel(q, groups, ncol, shapes, *rest):
    terms, hot, slots = rest[:groups], rest[groups:-1], rest[-1]
    part, lanes, deep, tall, few = shapes
    total = terms[0][...].astype(f32)
    for term in terms[1:]:
        total = total + term[...].astype(f32)
    at = 2 * ncol * part
    out = total[at : at + deep]
    head = total[at + deep : at + deep + part]
    narrow = deep * q // ncol
    fold = lanes // tall
    short = narrow // fold
    for c in range(ncol):
        slots[c, 0:part] = total[c * part : (c + 1) * part].astype(bf16)
        slots[c, part : 2 * part] = total[(ncol + c) * part : (ncol + c + 1) * part].astype(bf16)
        u, top = (c * narrow) // deep, (c * narrow) % deep
        block = out[top : top + narrow, u * tall : (u + 1) * tall]
        block = jnp.concatenate([block[v * short : (v + 1) * short] for v in range(fold)], axis=1)
        slots[c, 2 * part : 2 * part + short] = block.astype(bf16)
        piece = jnp.concatenate([head[:, c * few : (c + 1) * few], jnp.zeros((part, lanes - few), f32)], axis=1)
        slots[c, 2 * part + short : 3 * part + short] = piece.astype(bf16)
    for p in range(ncol):
        hot[p][...] = slots[partner(lax.axis_index("col"), p, ncol)]


def col_sum_kernel(shapes, factor, *rest):
    terms, (gate, up, out, head) = rest[:-4], rest[-4:]
    part, lanes, tall, few = shapes
    total = terms[0][...].astype(f32)
    for term in terms[1:]:
        total = total + term[...].astype(f32)
    total = total * factor
    fold = lanes // tall
    short = out.shape[0] // fold
    gate[...] = total[0:part]
    up[...] = total[part : 2 * part]
    for v in range(fold):
        out[v * short : (v + 1) * short, :] = total[2 * part : 2 * part + short, v * tall : (v + 1) * tall]
    head[...] = total[2 * part + short : 3 * part + short, 0:few]


def shaped(shape, kind):
    return jax.ShapeDtypeStruct(shape, kind)


def cost(flops, moved):
    return pl.CostEstimate(flops=flops, bytes_accessed=moved, transcendentals=0)


def body(pair, targets, w_gate, w_up, w_out, w_head):
    rows, cols, width = pair.shape
    units = w_gate.shape[1]
    bins = w_head.shape[1]
    count = rows * cols
    nrow, ncol = lax.axis_size("row"), lax.axis_size("col")
    q = nrow // ncol
    groups = nrow // q
    side = count // q
    packs = lane_packs(bins, side)
    flat = pair.reshape(count, width)
    head_t = w_head.T
    piece = (side // packs, bins * packs)

    sources = (flat, w_gate, w_up, w_out, head_t, targets)
    kept = [shaped(x.shape, x.dtype) for x in sources]
    flat, w_gate, w_up, w_out, head_t, targets, updated, logits, *sends = pl.pallas_call(
        functools.partial(forward_kernel, q),
        out_shape=kept + [shaped((count, width), bf16), shaped((count, bins), bf16)] + [shaped(piece, bf16)] * q,
        in_specs=[HBM] * 6,
        out_specs=[VMEM] * (8 + q),
        scratch_shapes=[pltpu.VMEM((q, *piece), bf16), pltpu.SemaphoreType.DMA((6,))],
        compiler_params=PARAMS,
        name="forward",
    )(*(pltpu.with_memory_space_constraint(x, pltpu.HBM) for x in sources))

    got = []
    for p in range(q):
        pairs = [
            (r * ncol + c, (q * c + (r % q + p) % q) * ncol + r // q) for r in range(nrow) for c in range(ncol)
        ]
        got.append(lax.ppermute(sends[p], ("row", "col"), pairs))
    onehot = (targets.reshape(count)[:, None] == jnp.arange(bins, dtype=jnp.int32)[None, :]).astype(bf16)
    inputs_t, updated_t, hidden, slope, swish, normed, scale = pl.pallas_call(
        prepare_kernel,
        out_shape=[
            shaped((width, count), bf16),
            shaped((width, count), bf16),
            shaped((count, units), bf16),
            shaped((count, units), f32),
            shaped((count, units), f32),
            shaped((count, width), f32),
            shaped((count, width), f32),
        ],
        in_specs=[VMEM] * 4,
        out_specs=[VMEM] * 7,
        compiler_params=PARAMS,
        cost_estimate=cost(4 * count * width * units, 4 * count * units),
        name="prepare",
    )(flat, updated, w_gate, w_up)

    part, tall, few = width // nrow, units // nrow, bins // ncol
    lanes, deep = units // ncol, width // q
    fits = (
        part % 16 == 0 and lanes == 128 and tall * q == lanes and bins <= lanes and deep % (width // ncol) == 0
        and (width // ncol * tall // lanes) % 16 == 0
    )
    height = 2 * ncol * part + deep + part
    if fits:
        hot_shapes = [shaped((groups, height, lanes), bf16)] * q
        slots = pltpu.VMEM((q, groups, height, lanes), bf16)
    else:
        hot_shapes = [shaped((width, n), bf16) for n in (units, units, units, bins)]
        slots = pltpu.VMEM((16, 128), bf16)
    d_updated, d_gate, d_up, *hot = pl.pallas_call(
        functools.partial(backward_kernel, q, (nrow, ncol) if fits else None),
        out_shape=[shaped((count, width), f32)] + [shaped((count, units), bf16)] * 2 + hot_shapes,
        in_specs=[VMEM] * (9 + q),
        out_specs=[VMEM] * (3 + len(hot_shapes)),
        scratch_shapes=[pltpu.VMEM((rows, q, cols // q, bins), f32), slots],
        compiler_params=PARAMS,
        cost_estimate=cost(8 * count * width * units, 4 * count * units),
        name="backward",
    )(inputs_t, updated_t, hidden, slope, swish, logits, onehot, w_out, head_t, *got)

    d_pair = pl.pallas_call(
        input_kernel,
        out_shape=shaped((count, width), bf16),
        in_specs=[VMEM] * 7,
        out_specs=VMEM,
        compiler_params=PARAMS,
        cost_estimate=cost(4 * count * width * units, 4 * count * units),
        name="d_inputs",
    )(d_gate, d_up, d_updated, normed, scale, w_gate, w_up)
    d_pair = d_pair.reshape(rows, cols, width)
    factor = 1.0 / (rows * nrow)
    if not fits:
        owned = []
        hot[2] = hot[2].T
        for term in hot:
            mine = lax.psum_scatter(term, "row", scatter_dimension=0, tiled=True).astype(f32)
            owned.append(lax.psum_scatter(mine, "col", scatter_dimension=1, tiled=True) * factor)
        return (d_pair, *owned)

    terms = [hot[0]]
    for p in range(1, q):
        terms.append(lax.ppermute(hot[p], "row", [(s, s - s % q + partner(s % q, p, q)) for s in range(nrow)]))
    hot = pl.pallas_call(
        functools.partial(core_sum_kernel, q, groups),
        out_shape=[shaped((height, lanes), bf16)] * groups,
        in_specs=[VMEM] * q,
        out_specs=[VMEM] * groups,
        compiler_params=PARAMS,
        name="core_sum",
    )(*terms)
    terms = [hot[0]]
    for p in range(groups - 1, 0, -1):
        terms.append(lax.ppermute(hot[p], "row", [(s, partner(s // q, p, groups) * q + s % q) for s in range(nrow)]))
    short = 3 * part + width // ncol * tall // lanes
    hot = pl.pallas_call(
        functools.partial(chip_sum_kernel, q, groups, ncol, (part, lanes, deep, tall, few)),
        out_shape=[shaped((short, lanes), bf16)] * ncol,
        in_specs=[VMEM] * groups,
        out_specs=[VMEM] * ncol,
        scratch_shapes=[pltpu.VMEM((ncol, short, lanes), bf16)],
        compiler_params=PARAMS,
        name="chip_sum",
    )(*terms)
    terms = [hot[0]]
    for p in range(ncol - 1, 0, -1):
        terms.append(lax.ppermute(hot[p], "col", [(s, partner(s, p, ncol)) for s in range(ncol)]))
    gate, up, out, head = pl.pallas_call(
        functools.partial(col_sum_kernel, (part, lanes, tall, few), factor),
        out_shape=[
            shaped((part, lanes), f32),
            shaped((part, lanes), f32),
            shaped((width // ncol, tall), f32),
            shaped((part, few), f32),
        ],
        in_specs=[VMEM] * ncol,
        out_specs=[VMEM] * 4,
        compiler_params=PARAMS,
        name="col_sum",
    )(*terms)
    return d_pair, gate, up, out.T, head


def solution(mesh):
    placed = (P("row", "col", None), P("row", "col"), P(), P(), P(), P())
    return jax.shard_map(
        body,
        mesh=mesh,
        in_specs=placed,
        out_specs=(P("row", "col", None), P("row", "col"), P("row", "col"), P("row", "col"), P("row", "col")),
        check_vma=False,
    )
```

```python
import functools

import jax
import jax.numpy as jnp
from jax import lax
from jax.experimental import pallas as pl
from jax.experimental.pallas import tpu as pltpu
from jax.sharding import PartitionSpec as P

eps = 1e-05
f32 = jnp.float32
bf16 = jnp.bfloat16
HBM = pl.BlockSpec(memory_space=pltpu.HBM)
VMEM = pl.BlockSpec(memory_space=pltpu.VMEM)
PARAMS = pltpu.CompilerParams(vmem_limit_bytes=24 * 1024 * 1024)


def nn(a, b):
    return lax.dot_general(a, b, (((1,), (0,)), ((), ())), preferred_element_type=f32)


def nt(a, b):
    return lax.dot_general(a, b, (((1,), (1,)), ((), ())), preferred_element_type=f32)


def tn(a, b):
    return lax.dot_general(a, b, (((0,), (0,)), ((), ())), preferred_element_type=f32)


def normalize(flat):
    values = flat.astype(f32)
    centre = values - jnp.mean(values, axis=-1, keepdims=True)
    scale_inv = lax.rsqrt(jnp.mean(centre * centre, axis=-1, keepdims=True) + eps)
    return centre * scale_inv, scale_inv


def sigmoid(v):
    return 0.5 * jnp.tanh(0.5 * v) + 0.5


def chunks_of(size, most):
    step = most if size % most == 0 else size
    return [(at, step) for at in range(0, size, step)]


def partner(s, p, n):
    if n & (n - 1) == 0:
        return s ^ p
    return (s + p) % n if isinstance(s, int) else lax.rem(s + p, n)


def lane_packs(bins, side):
    packs = max(1, 128 // bins)
    return packs if (side // packs) % 16 == 0 else 1


def forward_kernel(q, *refs):
    sources, kept, (updated, logits, sends, halves, sems) = refs[:6], refs[6:12], refs[12:]
    pair, w_gate, w_up, w_out, w_head, _ = kept
    _, side, width = pair.shape
    edge = sources[0].shape[0]
    bins = w_head.shape[0]
    copies = [
        pltpu.make_async_copy(source, target, sems.at[i]) for i, (source, target) in enumerate(zip(sources[1:], kept[1:]))
    ]
    pieces = [
        pltpu.make_async_copy(
            sources[0].at[:, h * edge : (h + 1) * edge, :], pair.reshape(q, edge, edge, width).at[h], sems.at[5 + h]
        )
        for h in range(q)
    ]
    for copy in pieces + copies:
        copy.start()
    shift = edge.bit_length() - 1
    out_row = lax.broadcasted_iota(jnp.int32, (side, side), 0)
    in_row = lax.broadcasted_iota(jnp.int32, (side, side), 1)
    wanted = ((out_row & (edge - 1)) << shift) | (out_row >> shift)
    swap = jnp.where(in_row == wanted, 1.0, 0.0).astype(bf16)
    for copy in pieces:
        copy.wait()
    flat = pair[...].reshape(q * side, width)
    inputs = normalize(flat)[0].astype(bf16)
    total = flat.astype(f32)
    for copy in copies[:4]:
        copy.wait()
    for at, step in chunks_of(w_gate.shape[1], 256):
        gate = nn(inputs, w_gate[:, at : at + step])
        upper = nn(inputs, w_up[:, at : at + step])
        hidden = (gate * sigmoid(gate) * upper).astype(bf16)
        total = total + nn(hidden, w_out[at : at + step, :])
    upd = total.astype(bf16)
    updated[...] = upd.reshape(updated.shape)
    logit = nt(upd, w_head[...]).astype(bf16)
    logits[...] = logit.reshape(logits.shape)
    packs = lane_packs(bins, side)
    deep = side // packs
    for h in range(q):
        piece = nn(swap, logit[h * side : (h + 1) * side])
        if packs > 1:
            piece = jnp.concatenate([piece[u * deep : (u + 1) * deep] for u in range(packs)], axis=1)
        halves[h] = piece.astype(bf16)
    own = lax.rem(lax.axis_index("row"), q)
    for p in range(q):
        sends[p] = halves[partner(own, p, q)]
    copies[4].wait()


def prepare_kernel(pair, updated, w_gate, w_up, inputs_t, updated_t, hidden, slope, swish, normed, scale):
    q, side, width = pair.shape
    units = w_gate.shape[1]
    normal, scale_inv = normalize(pair[...].reshape(q * side, width))
    normed[...] = normal.reshape(normed.shape)
    scale[...] = jnp.broadcast_to(scale_inv, normal.shape).reshape(scale.shape)
    inputs = normal.astype(bf16)
    for h in range(q):
        inputs_t[h] = inputs[h * side : (h + 1) * side].T
        updated_t[h] = updated[h].T
    for at, step in chunks_of(units, 256):
        span = slice(at, at + step)
        gate = nn(inputs, w_gate[:, span])
        upper = nn(inputs, w_up[:, span])
        sigma = sigmoid(gate)
        swished = gate * sigma
        swish[:, :, span] = swished.reshape(q, side, step)
        hidden[:, :, span] = (swished * upper).astype(bf16).reshape(q, side, step)
        slope[:, :, span] = (upper * sigma * (1.0 + gate * (1.0 - sigma))).reshape(q, side, step)


def backward_kernel(q, p, packed, inputs_t, updated_t, hidden, slope, swish, logits, onehot, w_out, w_head, *rest):
    piece, before, rest = rest[0], rest[1:5] if p else (), rest[5 if p else 1 :]
    d_updated, d_gate, d_up, *hot = rest
    _, side, bins = logits.shape
    width, units = inputs_t.shape[1], hidden.shape[2]
    packs = lane_packs(bins, side)
    own = lax.rem(lax.axis_index("row"), q)
    h = partner(own, p, q)
    mirrored = piece[...] if p else piece[0]
    if packs > 1:
        mirrored = jnp.concatenate([mirrored[:, u * bins : (u + 1) * bins] for u in range(packs)], axis=0)
    summed = logits[h].astype(f32) + mirrored.astype(f32)
    powers = jnp.exp(summed - jnp.max(summed, axis=-1, keepdims=True))
    probs = powers / jnp.sum(powers, axis=-1, keepdims=True)
    grad_sym = (probs - onehot[h].astype(f32)).astype(bf16)
    cotangent = (grad_sym.astype(f32) * 2.0).astype(bf16)
    d_upd = nn(cotangent, w_head[...])
    d_updated[...] = d_upd
    d_upd_b = d_upd.astype(bf16)
    d_upd_t = d_upd_b.T
    terms = [[], [], []]
    for at, step in chunks_of(units, 256):
        span = slice(at, at + step)
        d_hidden = nt(d_upd_b, w_out[span, :])
        d_gate_part = (d_hidden * slope[h, :, span]).astype(bf16)
        d_up_part = (d_hidden * swish[h, :, span]).astype(bf16)
        d_gate[:, span] = d_gate_part
        d_up[:, span] = d_up_part
        terms[0].append(nn(inputs_t[h], d_gate_part))
        terms[1].append(nn(inputs_t[h], d_up_part))
        terms[2].append(nn(d_upd_t, hidden[h, :, span]))
    terms = [jnp.concatenate(term, axis=1) for term in terms] + [nn(updated_t[h], cotangent)]
    if p:
        terms = [term + ref[...] for term, ref in zip(terms, before)]
    if p < q - 1 or not packed:
        for ref, term in zip(hot, terms):
            ref[...] = term.astype(ref.dtype)
        return
    gate_term, up_term, out_term, head_term = terms
    hot, slots = hot[:-1], hot[-1]
    nrow, ncol = packed
    groups = nrow // q
    lanes, part, tall = units // ncol, width // nrow, units // nrow
    deep = width // q
    for k in range(q):
        for a in range(groups):
            r = a * q + k
            at = 0
            for term in (gate_term, up_term):
                for c in range(ncol):
                    block = term[r * part : (r + 1) * part, c * lanes : (c + 1) * lanes]
                    slots[k, a, at : at + part] = block.astype(bf16)
                    at += part
            blocks = [out_term[u * deep : (u + 1) * deep, r * tall : (r + 1) * tall] for u in range(q)]
            slots[k, a, at : at + deep] = jnp.concatenate(blocks, axis=1).astype(bf16)
            at += deep
            block = head_term[r * part : (r + 1) * part, :]
            block = jnp.concatenate([block, jnp.zeros((part, lanes - bins), f32)], axis=1)
            slots[k, a, at : at + part] = block.astype(bf16)
    for n in range(q):
        hot[n][...] = slots[partner(own, n, q)]


def input_kernel(q, *refs):
    terms, (normed, scale, w_gate, w_up, d_pair) = refs[: 3 * q], refs[3 * q :]
    own = lax.rem(lax.axis_index("row"), q)
    for p in range(q):
        d_updated, d_gate, d_up = terms[3 * p : 3 * p + 3]
        h = partner(own, p, q)
        d_inputs = nt(d_gate[...], w_gate[...]) + nt(d_up[...], w_up[...])
        normal = normed[h]
        d_norm = (
            d_inputs
            - jnp.mean(d_inputs, axis=-1, keepdims=True)
            - normal * jnp.mean(d_inputs * normal, axis=-1, keepdims=True)
        ) * scale[h]
        result = (d_updated[...] + d_norm).astype(bf16)
        d_pair[:, h] = result.reshape(d_pair.shape[0], d_pair.shape[2], d_pair.shape[3])


def core_sum_kernel(q, groups, *rest):
    terms, hot = rest[:q], rest[q:]
    mine = lax.axis_index("row") // q
    for p in range(groups):
        a = partner(mine, p, groups)
        total = terms[0][a].astype(f32)
        for term in terms[1:]:
            total = total + term[a].astype(f32)
        hot[p][...] = total.astype(bf16)


def chip_sum_kernel(q, groups, ncol, shapes, *rest):
    terms, hot, slots = rest[:groups], rest[groups:-1], rest[-1]
    part, lanes, deep, tall, few = shapes
    total = terms[0][...].astype(f32)
    for term in terms[1:]:
        total = total + term[...].astype(f32)
    at = 2 * ncol * part
    out = total[at : at + deep]
    head = total[at + deep : at + deep + part]
    narrow = deep * q // ncol
    fold = lanes // tall
    short = narrow // fold
    for c in range(ncol):
        slots[c, 0:part] = total[c * part : (c + 1) * part].astype(bf16)
        slots[c, part : 2 * part] = total[(ncol + c) * part : (ncol + c + 1) * part].astype(bf16)
        u, top = (c * narrow) // deep, (c * narrow) % deep
        block = out[top : top + narrow, u * tall : (u + 1) * tall]
        block = jnp.concatenate([block[v * short : (v + 1) * short] for v in range(fold)], axis=1)
        slots[c, 2 * part : 2 * part + short] = block.astype(bf16)
        piece = jnp.concatenate([head[:, c * few : (c + 1) * few], jnp.zeros((part, lanes - few), f32)], axis=1)
        slots[c, 2 * part + short : 3 * part + short] = piece.astype(bf16)
    for p in range(ncol):
        hot[p][...] = slots[partner(lax.axis_index("col"), p, ncol)]


def col_sum_kernel(shapes, factor, *rest):
    terms, (gate, up, out, head) = rest[:-4], rest[-4:]
    part, lanes, tall, few = shapes
    total = terms[0][...].astype(f32)
    for term in terms[1:]:
        total = total + term[...].astype(f32)
    total = total * factor
    fold = lanes // tall
    short = out.shape[0] // fold
    gate[...] = total[0:part]
    up[...] = total[part : 2 * part]
    for v in range(fold):
        out[v * short : (v + 1) * short, :] = total[2 * part : 2 * part + short, v * tall : (v + 1) * tall]
    head[...] = total[2 * part + short : 3 * part + short, 0:few]


def core_pairs(nrow, q, p):
    return [(s, s - s % q + partner(s % q, p, q)) for s in range(nrow)]


def shaped(shape, kind):
    return jax.ShapeDtypeStruct(shape, kind)


def cost(flops, moved):
    return pl.CostEstimate(flops=flops, bytes_accessed=moved, transcendentals=0)


def body(pair, targets, w_gate, w_up, w_out, w_head):
    rows, cols, width = pair.shape
    units = w_gate.shape[1]
    bins = w_head.shape[1]
    nrow, ncol = lax.axis_size("row"), lax.axis_size("col")
    q = nrow // ncol
    groups = nrow // q
    side = rows * cols // q
    packs = lane_packs(bins, side)
    head_t = w_head.T
    piece = (side // packs, bins * packs)

    sources = (pair, w_gate, w_up, w_out, head_t, targets)
    kept = [shaped(x.shape, x.dtype) for x in sources]
    kept[0] = shaped((q, side, width), bf16)
    pair, w_gate, w_up, w_out, head_t, targets, updated, logits, sends = pl.pallas_call(
        functools.partial(forward_kernel, q),
        out_shape=kept + [shaped((q, side, width), bf16), shaped((q, side, bins), bf16), shaped((q, *piece), bf16)],
        in_specs=[HBM] * 6,
        out_specs=[VMEM] * 9,
        scratch_shapes=[pltpu.VMEM((q, *piece), bf16), pltpu.SemaphoreType.DMA((5 + q,))],
        compiler_params=PARAMS,
        name="forward",
    )(*(pltpu.with_memory_space_constraint(x, pltpu.HBM) for x in sources))

    pairs = [(r * ncol + c, (q * c + r % q) * ncol + r // q) for r in range(nrow) for c in range(ncol)]
    got = lax.ppermute(sends, ("row", "col"), pairs)
    targets = jnp.swapaxes(targets.reshape(rows, q, rows), 0, 1).reshape(q, side)
    onehot = (targets[:, :, None] == jnp.arange(bins, dtype=jnp.int32)[None, None, :]).astype(bf16)
    inputs_t, updated_t, hidden, slope, swish, normed, scale = pl.pallas_call(
        prepare_kernel,
        out_shape=[
            shaped((q, width, side), bf16),
            shaped((q, width, side), bf16),
            shaped((q, side, units), bf16),
            shaped((q, side, units), f32),
            shaped((q, side, units), f32),
            shaped((q, side, width), f32),
            shaped((q, side, width), f32),
        ],
        in_specs=[VMEM] * 4,
        out_specs=[VMEM] * 7,
        compiler_params=PARAMS,
        cost_estimate=cost(4 * q * side * width * units, 4 * q * side * units),
        name="prepare",
    )(pair, updated, w_gate, w_up)
    got, onehot, inputs_t = lax.optimization_barrier((got, onehot, inputs_t))
    got = [got] + [lax.ppermute(got[p], "row", core_pairs(nrow, q, p)) for p in range(1, q)]

    part, tall, few = width // nrow, units // nrow, bins // ncol
    lanes, deep = units // ncol, width // q
    fits = (
        part % 16 == 0 and lanes == 128 and tall * q == lanes and bins <= lanes and deep % (width // ncol) == 0
        and (width // ncol * tall // lanes) % 16 == 0
    )
    height = 2 * ncol * part + deep + part
    grads = [(width, n) for n in (units, units, units, bins)]
    hot, d_terms = [], []
    for p in range(q):
        scratch = []
        if p < q - 1 or not fits:
            hot_shapes = [shaped(shape, f32 if p < q - 1 else bf16) for shape in grads]
        else:
            hot_shapes = [shaped((groups, height, lanes), bf16)] * q
            scratch = [pltpu.VMEM((q, groups, height, lanes), bf16)]
        results = pl.pallas_call(
            functools.partial(backward_kernel, q, p, (nrow, ncol) if fits else None),
            out_shape=[shaped((side, width), f32)] + [shaped((side, units), bf16)] * 2 + hot_shapes,
            in_specs=[VMEM] * (10 + len(hot)),
            out_specs=[VMEM] * (3 + len(hot_shapes)),
            scratch_shapes=scratch,
            compiler_params=PARAMS,
            cost_estimate=cost(8 * side * width * units, 4 * side * units),
            name="backward",
        )(inputs_t, updated_t, hidden, slope, swish, logits, onehot, w_out, head_t, got[p], *hot)
        d_terms += results[:3]
        hot = list(results[3:])

    d_pair = pl.pallas_call(
        functools.partial(input_kernel, q),
        out_shape=shaped((rows, q, cols // q, width), bf16),
        in_specs=[VMEM] * (3 * q + 4),
        out_specs=VMEM,
        compiler_params=PARAMS,
        cost_estimate=cost(4 * q * side * width * units, 4 * q * side * units),
        name="d_inputs",
    )(*d_terms, normed, scale, w_gate, w_up)
    factor = 1.0 / (rows * nrow)
    if not fits:
        owned = []
        hot[2] = hot[2].T
        for term in hot:
            mine = lax.psum_scatter(term, "row", scatter_dimension=0, tiled=True).astype(f32)
            owned.append(lax.psum_scatter(mine, "col", scatter_dimension=1, tiled=True) * factor)
        return (d_pair.reshape(rows, cols, width), *owned)

    terms = [hot[0]]
    for p in range(1, q):
        terms.append(lax.ppermute(hot[p], "row", core_pairs(nrow, q, p)))
    hot = pl.pallas_call(
        functools.partial(core_sum_kernel, q, groups),
        out_shape=[shaped((height, lanes), bf16)] * groups,
        in_specs=[VMEM] * q,
        out_specs=[VMEM] * groups,
        compiler_params=PARAMS,
        name="core_sum",
    )(*terms)
    terms = [hot[0]]
    for p in range(groups - 1, 0, -1):
        terms.append(lax.ppermute(hot[p], "row", [(s, partner(s // q, p, groups) * q + s % q) for s in range(nrow)]))
    *terms, d_pair = lax.optimization_barrier((*terms, d_pair))
    short = 3 * part + width // ncol * tall // lanes
    hot = pl.pallas_call(
        functools.partial(chip_sum_kernel, q, groups, ncol, (part, lanes, deep, tall, few)),
        out_shape=[shaped((short, lanes), bf16)] * ncol,
        in_specs=[VMEM] * groups,
        out_specs=[VMEM] * ncol,
        scratch_shapes=[pltpu.VMEM((ncol, short, lanes), bf16)],
        compiler_params=PARAMS,
        name="chip_sum",
    )(*terms)
    terms = [hot[0]]
    for p in range(ncol - 1, 0, -1):
        terms.append(lax.ppermute(hot[p], "col", [(s, partner(s, p, ncol)) for s in range(ncol)]))
    gate, up, out, head = pl.pallas_call(
        functools.partial(col_sum_kernel, (part, lanes, tall, few), factor),
        out_shape=[
            shaped((part, lanes), f32),
            shaped((part, lanes), f32),
            shaped((width // ncol, tall), f32),
            shaped((part, few), f32),
        ],
        in_specs=[VMEM] * ncol,
        out_specs=[VMEM] * 4,
        compiler_params=PARAMS,
        name="col_sum",
    )(*terms)
    return d_pair.reshape(rows, cols, width), gate, up, out.T, head


def solution(mesh):
    placed = (P("row", "col", None), P("row", "col"), P(), P(), P(), P())
    return jax.shard_map(
        body,
        mesh=mesh,
        in_specs=placed,
        out_specs=(P("row", "col", None), P("row", "col"), P("row", "col"), P("row", "col"), P("row", "col")),
        check_vma=False,
    )
```

```python
import functools

import jax
import jax.numpy as jnp
from jax import lax
from jax.experimental import pallas as pl
from jax.experimental.pallas import tpu as pltpu
from jax.sharding import PartitionSpec as P

eps = 1e-05
f32 = jnp.float32
bf16 = jnp.bfloat16
HBM = pl.BlockSpec(memory_space=pltpu.HBM)
VMEM = pl.BlockSpec(memory_space=pltpu.VMEM)
PARAMS = pltpu.CompilerParams(vmem_limit_bytes=24 * 1024 * 1024)


def nn(a, b):
    return lax.dot_general(a, b, (((1,), (0,)), ((), ())), preferred_element_type=f32)


def nt(a, b):
    return lax.dot_general(a, b, (((1,), (1,)), ((), ())), preferred_element_type=f32)


def tn(a, b):
    return lax.dot_general(a, b, (((0,), (0,)), ((), ())), preferred_element_type=f32)


def normalize(flat):
    values = flat.astype(f32)
    centre = values - jnp.mean(values, axis=-1, keepdims=True)
    scale_inv = lax.rsqrt(jnp.mean(centre * centre, axis=-1, keepdims=True) + eps)
    return centre * scale_inv, scale_inv


def sigmoid(v):
    return 0.5 * jnp.tanh(0.5 * v) + 0.5


def chunks_of(size, most):
    step = most if size % most == 0 else size
    return [(at, step) for at in range(0, size, step)]


def partner(s, p, n):
    if n & (n - 1) == 0:
        return s ^ p
    return (s + p) % n if isinstance(s, int) else lax.rem(s + p, n)


def lane_packs(bins, side):
    packs = max(1, 128 // bins)
    return packs if (side // packs) % 16 == 0 else 1


def forward_kernel(q, *refs):
    sources, kept, (updated, logits, sends, halves, sems) = refs[:6], refs[6:12], refs[12:]
    pair, w_gate, w_up, w_out, w_head, _ = kept
    _, side, width = pair.shape
    edge = sources[0].shape[0]
    bins = w_head.shape[0]
    copies = [
        pltpu.make_async_copy(source, target, sems.at[i]) for i, (source, target) in enumerate(zip(sources[1:], kept[1:]))
    ]
    pieces = [
        pltpu.make_async_copy(
            sources[0].at[:, h * edge : (h + 1) * edge, :], pair.reshape(q, edge, edge, width).at[h], sems.at[5 + h]
        )
        for h in range(q)
    ]
    for copy in pieces + copies:
        copy.start()
    shift = edge.bit_length() - 1
    out_row = lax.broadcasted_iota(jnp.int32, (side, side), 0)
    in_row = lax.broadcasted_iota(jnp.int32, (side, side), 1)
    wanted = ((out_row & (edge - 1)) << shift) | (out_row >> shift)
    swap = jnp.where(in_row == wanted, 1.0, 0.0).astype(bf16)
    for copy in pieces:
        copy.wait()
    flat = pair[...].reshape(q * side, width)
    inputs = normalize(flat)[0].astype(bf16)
    total = flat.astype(f32)
    for copy in copies[:4]:
        copy.wait()
    for at, step in chunks_of(w_gate.shape[1], 256):
        gate = nn(inputs, w_gate[:, at : at + step])
        upper = nn(inputs, w_up[:, at : at + step])
        hidden = (gate * sigmoid(gate) * upper).astype(bf16)
        total = total + nn(hidden, w_out[at : at + step, :])
    upd = total.astype(bf16)
    updated[...] = upd.reshape(updated.shape)
    logit = nt(upd, w_head[...]).astype(bf16)
    logits[...] = logit.reshape(logits.shape)
    packs = lane_packs(bins, side)
    deep = side // packs
    for h in range(q):
        piece = nn(swap, logit[h * side : (h + 1) * side])
        if packs > 1:
            piece = jnp.concatenate([piece[u * deep : (u + 1) * deep] for u in range(packs)], axis=1)
        halves[h] = piece.astype(bf16)
    own = lax.rem(lax.axis_index("row"), q)
    for p in range(q):
        sends[p] = halves[partner(own, p, q)]
    copies[4].wait()


def prepare_kernel(pair, updated, w_gate, w_up, inputs_t, updated_t, hidden, slope, swish, normed, scale):
    q, side, width = pair.shape
    units = w_gate.shape[1]
    normal, scale_inv = normalize(pair[...].reshape(q * side, width))
    normed[...] = normal.reshape(normed.shape)
    scale[...] = jnp.broadcast_to(scale_inv, normal.shape).reshape(scale.shape)
    inputs = normal.astype(bf16)
    for h in range(q):
        inputs_t[h] = inputs[h * side : (h + 1) * side].T
        updated_t[h] = updated[h].T
    for at, step in chunks_of(units, 256):
        span = slice(at, at + step)
        gate = nn(inputs, w_gate[:, span])
        upper = nn(inputs, w_up[:, span])
        sigma = sigmoid(gate)
        swished = gate * sigma
        swish[:, :, span] = swished.reshape(q, side, step)
        hidden[:, :, span] = (swished * upper).astype(bf16).reshape(q, side, step)
        slope[:, :, span] = (upper * sigma * (1.0 + gate * (1.0 - sigma))).reshape(q, side, step)


def backward_kernel(q, p, packed, inputs_t, updated_t, hidden, slope, swish, logits, onehot, w_out, w_head, *rest):
    piece, before, rest = rest[0], rest[1:5] if p else (), rest[5 if p else 1 :]
    d_updated, d_gate, d_up, *hot = rest
    _, side, bins = logits.shape
    width, units = inputs_t.shape[1], hidden.shape[2]
    packs = lane_packs(bins, side)
    own = lax.rem(lax.axis_index("row"), q)
    h = partner(own, p, q)
    mirrored = piece[...] if p else piece[0]
    if packs > 1:
        mirrored = jnp.concatenate([mirrored[:, u * bins : (u + 1) * bins] for u in range(packs)], axis=0)
    summed = logits[h].astype(f32) + mirrored.astype(f32)
    powers = jnp.exp(summed - jnp.max(summed, axis=-1, keepdims=True))
    probs = powers / jnp.sum(powers, axis=-1, keepdims=True)
    grad_sym = (probs - onehot[h].astype(f32)).astype(bf16)
    cotangent = (grad_sym.astype(f32) * 2.0).astype(bf16)
    d_upd = nn(cotangent, w_head[...])
    d_updated[...] = d_upd
    d_upd_b = d_upd.astype(bf16)
    d_upd_t = d_upd_b.T
    terms = [[], [], []]
    for at, step in chunks_of(units, 256):
        span = slice(at, at + step)
        d_hidden = nt(d_upd_b, w_out[span, :])
        d_gate_part = (d_hidden * slope[h, :, span]).astype(bf16)
        d_up_part = (d_hidden * swish[h, :, span]).astype(bf16)
        d_gate[:, span] = d_gate_part
        d_up[:, span] = d_up_part
        terms[0].append(nn(inputs_t[h], d_gate_part))
        terms[1].append(nn(inputs_t[h], d_up_part))
        terms[2].append(nn(d_upd_t, hidden[h, :, span]))
    terms = [jnp.concatenate(term, axis=1) for term in terms] + [nn(updated_t[h], cotangent)]
    if p:
        terms = [term + ref[...] for term, ref in zip(terms, before)]
    if p < q - 1 or not packed:
        for ref, term in zip(hot, terms):
            ref[...] = term.astype(ref.dtype)
        return
    gate_term, up_term, out_term, head_term = terms
    hot, slots = hot[:-1], hot[-1]
    nrow, ncol = packed
    groups = nrow // q
    lanes, part, tall = units // ncol, width // nrow, units // nrow
    deep = width // q
    for k in range(q):
        for a in range(groups):
            r = a * q + k
            at = 0
            for term in (gate_term, up_term):
                for c in range(ncol):
                    block = term[r * part : (r + 1) * part, c * lanes : (c + 1) * lanes]
                    slots[k, a, at : at + part] = block.astype(bf16)
                    at += part
            blocks = [out_term[u * deep : (u + 1) * deep, r * tall : (r + 1) * tall] for u in range(q)]
            slots[k, a, at : at + deep] = jnp.concatenate(blocks, axis=1).astype(bf16)
            at += deep
            block = head_term[r * part : (r + 1) * part, :]
            block = jnp.concatenate([block, jnp.zeros((part, lanes - bins), f32)], axis=1)
            slots[k, a, at : at + part] = block.astype(bf16)
    for n in range(q):
        hot[n][...] = slots[partner(own, n, q)]


def input_kernel(q, *refs):
    terms, (normed, scale, w_gate, w_up, d_pair) = refs[: 3 * q], refs[3 * q :]
    own = lax.rem(lax.axis_index("row"), q)
    for p in range(q):
        d_updated, d_gate, d_up = terms[3 * p : 3 * p + 3]
        h = partner(own, p, q)
        d_inputs = nt(d_gate[...], w_gate[...]) + nt(d_up[...], w_up[...])
        normal = normed[h]
        d_norm = (
            d_inputs
            - jnp.mean(d_inputs, axis=-1, keepdims=True)
            - normal * jnp.mean(d_inputs * normal, axis=-1, keepdims=True)
        ) * scale[h]
        result = (d_updated[...] + d_norm).astype(bf16)
        d_pair[:, h] = result.reshape(d_pair.shape[0], d_pair.shape[2], d_pair.shape[3])


def core_sum_kernel(q, groups, *rest):
    terms, hot = rest[:q], rest[q:]
    mine = lax.axis_index("row") // q
    for n, p in enumerate([0] + [p for p, _ in stages(groups)]):
        a = partner(mine, p, groups)
        total = terms[0][a].astype(f32)
        for term in terms[1:]:
            total = total + term[a].astype(f32)
        hot[n][...] = total.astype(bf16)


def chip_sum_kernel(q, ncol, shapes, *rest):
    steps = [0] + [p for p, _ in stages(ncol)]
    terms, hot, slots = rest[: -1 - len(steps)], rest[-1 - len(steps) : -1], rest[-1]
    part, lanes, deep, tall, few = shapes
    total = terms[0][...].astype(f32)
    for term in terms[1:]:
        total = total + term[...].astype(f32)
    at = 2 * ncol * part
    out = total[at : at + deep]
    head = total[at + deep : at + deep + part]
    narrow = deep * q // ncol
    fold = lanes // tall
    short = narrow // fold
    for c in range(ncol):
        slots[c, 0:part] = total[c * part : (c + 1) * part].astype(bf16)
        slots[c, part : 2 * part] = total[(ncol + c) * part : (ncol + c + 1) * part].astype(bf16)
        u, top = (c * narrow) // deep, (c * narrow) % deep
        block = out[top : top + narrow, u * tall : (u + 1) * tall]
        block = jnp.concatenate([block[v * short : (v + 1) * short] for v in range(fold)], axis=1)
        slots[c, 2 * part : 2 * part + short] = block.astype(bf16)
        piece = jnp.concatenate([head[:, c * few : (c + 1) * few], jnp.zeros((part, lanes - few), f32)], axis=1)
        slots[c, 2 * part + short : 3 * part + short] = piece.astype(bf16)
    for n, p in enumerate(steps):
        hot[n][...] = slots[partner(lax.axis_index("col"), p, ncol)]


def col_sum_kernel(shapes, factor, *rest):
    terms, (gate, up, out, head) = rest[:-4], rest[-4:]
    part, lanes, tall, few = shapes
    total = terms[0][...].astype(f32)
    for term in terms[1:]:
        total = total + term[...].astype(f32)
    total = total * factor
    fold = lanes // tall
    short = out.shape[0] // fold
    gate[...] = total[0:part]
    up[...] = total[part : 2 * part]
    for v in range(fold):
        out[v * short : (v + 1) * short, :] = total[2 * part : 2 * part + short, v * tall : (v + 1) * tall]
    head[...] = total[2 * part + short : 3 * part + short, 0:few]


def core_pairs(nrow, q, p):
    return [(s, s - s % q + partner(s % q, p, q)) for s in range(nrow)]


def stages(n):
    if n & (n - 1) or n < 4:
        return [(p, range(n)) for p in range(1, n)]
    half = n // 2
    across = range(half, n)
    return [(p, range(n)) for p in range(1, half)] + [(p, across) for p in across] + [(p, range(half)) for p in across]


def staged_permutes(values, axis, n, pairs):
    moved = [
        lax.ppermute(value, axis, [pair for s in members for pair in pairs(s, p)])
        for value, (p, members) in zip(values[1:], stages(n))
    ]
    return [values[0]] + moved


def shaped(shape, kind):
    return jax.ShapeDtypeStruct(shape, kind)


def cost(flops, moved):
    return pl.CostEstimate(flops=flops, bytes_accessed=moved, transcendentals=0)


def body(pair, targets, w_gate, w_up, w_out, w_head):
    rows, cols, width = pair.shape
    units = w_gate.shape[1]
    bins = w_head.shape[1]
    nrow, ncol = lax.axis_size("row"), lax.axis_size("col")
    q = nrow // ncol
    groups = nrow // q
    side = rows * cols // q
    packs = lane_packs(bins, side)
    head_t = w_head.T
    piece = (side // packs, bins * packs)

    sources = (pair, w_gate, w_up, w_out, head_t, targets)
    kept = [shaped(x.shape, x.dtype) for x in sources]
    kept[0] = shaped((q, side, width), bf16)
    pair, w_gate, w_up, w_out, head_t, targets, updated, logits, sends = pl.pallas_call(
        functools.partial(forward_kernel, q),
        out_shape=kept + [shaped((q, side, width), bf16), shaped((q, side, bins), bf16), shaped((q, *piece), bf16)],
        in_specs=[HBM] * 6,
        out_specs=[VMEM] * 9,
        scratch_shapes=[pltpu.VMEM((q, *piece), bf16), pltpu.SemaphoreType.DMA((5 + q,))],
        compiler_params=PARAMS,
        name="forward",
    )(*(pltpu.with_memory_space_constraint(x, pltpu.HBM) for x in sources))

    pairs = [(r * ncol + c, (q * c + r % q) * ncol + r // q) for r in range(nrow) for c in range(ncol)]
    got = lax.ppermute(sends, ("row", "col"), pairs)
    targets = jnp.swapaxes(targets.reshape(rows, q, rows), 0, 1).reshape(q, side)
    onehot = (targets[:, :, None] == jnp.arange(bins, dtype=jnp.int32)[None, None, :]).astype(bf16)
    inputs_t, updated_t, hidden, slope, swish, normed, scale = pl.pallas_call(
        prepare_kernel,
        out_shape=[
            shaped((q, width, side), bf16),
            shaped((q, width, side), bf16),
            shaped((q, side, units), bf16),
            shaped((q, side, units), f32),
            shaped((q, side, units), f32),
            shaped((q, side, width), f32),
            shaped((q, side, width), f32),
        ],
        in_specs=[VMEM] * 4,
        out_specs=[VMEM] * 7,
        compiler_params=PARAMS,
        cost_estimate=cost(4 * q * side * width * units, 4 * q * side * units),
        name="prepare",
    )(pair, updated, w_gate, w_up)
    got, onehot, inputs_t = lax.optimization_barrier((got, onehot, inputs_t))
    got = [got] + [lax.ppermute(got[p], "row", core_pairs(nrow, q, p)) for p in range(1, q)]

    part, tall, few = width // nrow, units // nrow, bins // ncol
    lanes, deep = units // ncol, width // q
    fits = (
        part % 16 == 0 and lanes == 128 and tall * q == lanes and bins <= lanes and deep % (width // ncol) == 0
        and (width // ncol * tall // lanes) % 16 == 0
    )
    height = 2 * ncol * part + deep + part
    grads = [(width, n) for n in (units, units, units, bins)]
    hot, d_terms = [], []
    for p in range(q):
        scratch = []
        if p < q - 1 or not fits:
            hot_shapes = [shaped(shape, f32 if p < q - 1 else bf16) for shape in grads]
        else:
            hot_shapes = [shaped((groups, height, lanes), bf16)] * q
            scratch = [pltpu.VMEM((q, groups, height, lanes), bf16)]
        results = pl.pallas_call(
            functools.partial(backward_kernel, q, p, (nrow, ncol) if fits else None),
            out_shape=[shaped((side, width), f32)] + [shaped((side, units), bf16)] * 2 + hot_shapes,
            in_specs=[VMEM] * (10 + len(hot)),
            out_specs=[VMEM] * (3 + len(hot_shapes)),
            scratch_shapes=scratch,
            compiler_params=PARAMS,
            cost_estimate=cost(8 * side * width * units, 4 * side * units),
            name="backward",
        )(inputs_t, updated_t, hidden, slope, swish, logits, onehot, w_out, head_t, got[p], *hot)
        d_terms += results[:3]
        hot = list(results[3:])

    d_pair = pl.pallas_call(
        functools.partial(input_kernel, q),
        out_shape=shaped((rows, q, cols // q, width), bf16),
        in_specs=[VMEM] * (3 * q + 4),
        out_specs=VMEM,
        compiler_params=PARAMS,
        cost_estimate=cost(4 * q * side * width * units, 4 * q * side * units),
        name="d_inputs",
    )(*d_terms, normed, scale, w_gate, w_up)
    factor = 1.0 / (rows * nrow)
    if not fits:
        owned = []
        hot[2] = hot[2].T
        for term in hot:
            mine = lax.psum_scatter(term, "row", scatter_dimension=0, tiled=True).astype(f32)
            owned.append(lax.psum_scatter(mine, "col", scatter_dimension=1, tiled=True) * factor)
        return (d_pair.reshape(rows, cols, width), *owned)

    terms = [hot[0]]
    for p in range(1, q):
        terms.append(lax.ppermute(hot[p], "row", core_pairs(nrow, q, p)))
    hot = pl.pallas_call(
        functools.partial(core_sum_kernel, q, groups),
        out_shape=[shaped((height, lanes), bf16)] * (1 + len(stages(groups))),
        in_specs=[VMEM] * q,
        out_specs=[VMEM] * (1 + len(stages(groups))),
        compiler_params=PARAMS,
        name="core_sum",
    )(*terms)
    terms = staged_permutes(hot, "row", groups, lambda s, p: [(s * q + k, partner(s, p, groups) * q + k) for k in range(q)])
    *terms, d_pair = lax.optimization_barrier((*terms, d_pair))
    short = 3 * part + width // ncol * tall // lanes
    hot = pl.pallas_call(
        functools.partial(chip_sum_kernel, q, ncol, (part, lanes, deep, tall, few)),
        out_shape=[shaped((short, lanes), bf16)] * (1 + len(stages(ncol))),
        in_specs=[VMEM] * len(terms),
        out_specs=[VMEM] * (1 + len(stages(ncol))),
        scratch_shapes=[pltpu.VMEM((ncol, short, lanes), bf16)],
        compiler_params=PARAMS,
        name="chip_sum",
    )(*terms)
    terms = staged_permutes(hot, "col", ncol, lambda s, p: [(s, partner(s, p, ncol))])
    gate, up, out, head = pl.pallas_call(
        functools.partial(col_sum_kernel, (part, lanes, tall, few), factor),
        out_shape=[
            shaped((part, lanes), f32),
            shaped((part, lanes), f32),
            shaped((width // ncol, tall), f32),
            shaped((part, few), f32),
        ],
        in_specs=[VMEM] * len(terms),
        out_specs=[VMEM] * 4,
        compiler_params=PARAMS,
        name="col_sum",
    )(*terms)
    return d_pair.reshape(rows, cols, width), gate, up, out.T, head


def solution(mesh):
    placed = (P("row", "col", None), P("row", "col"), P(), P(), P(), P())
    return jax.shard_map(
        body,
        mesh=mesh,
        in_specs=placed,
        out_specs=(P("row", "col", None), P("row", "col"), P("row", "col"), P("row", "col"), P("row", "col")),
        check_vma=False,
    )
```

```python
import functools

import jax
import jax.numpy as jnp
from jax import lax
from jax.experimental import pallas as pl
from jax.experimental.pallas import tpu as pltpu
from jax.sharding import PartitionSpec as P

eps = 1e-05
f32 = jnp.float32
bf16 = jnp.bfloat16
HBM = pl.BlockSpec(memory_space=pltpu.HBM)
VMEM = pl.BlockSpec(memory_space=pltpu.VMEM)
PARAMS = pltpu.CompilerParams(vmem_limit_bytes=24 * 1024 * 1024)


def nn(a, b):
    return lax.dot_general(a, b, (((1,), (0,)), ((), ())), preferred_element_type=f32)


def nt(a, b):
    return lax.dot_general(a, b, (((1,), (1,)), ((), ())), preferred_element_type=f32)


def tn(a, b):
    return lax.dot_general(a, b, (((0,), (0,)), ((), ())), preferred_element_type=f32)


def normalize(flat):
    values = flat.astype(f32)
    centre = values - jnp.mean(values, axis=-1, keepdims=True)
    scale_inv = lax.rsqrt(jnp.mean(centre * centre, axis=-1, keepdims=True) + eps)
    return centre * scale_inv, scale_inv


def sigmoid(v):
    return 0.5 * jnp.tanh(0.5 * v) + 0.5


def chunks_of(size, most):
    step = most if size % most == 0 else size
    return [(at, step) for at in range(0, size, step)]


def partner(s, p, n):
    if n & (n - 1) == 0:
        return s ^ p
    return (s + p) % n if isinstance(s, int) else lax.rem(s + p, n)


def lane_packs(bins, side):
    packs = max(1, 128 // bins)
    return packs if (side // packs) % 16 == 0 else 1


def forward_kernel(q, *refs):
    sources, kept, (updated, logits, sends, halves, sems) = refs[:6], refs[6:12], refs[12:]
    pair, w_gate, w_up, w_out, w_head, _ = kept
    _, side, width = pair.shape
    edge = sources[0].shape[0]
    bins = w_head.shape[0]
    copies = [
        pltpu.make_async_copy(source, target, sems.at[i]) for i, (source, target) in enumerate(zip(sources[1:], kept[1:]))
    ]
    pieces = [
        pltpu.make_async_copy(
            sources[0].at[:, h * edge : (h + 1) * edge, :], pair.reshape(q, edge, edge, width).at[h], sems.at[5 + h]
        )
        for h in range(q)
    ]
    for copy in pieces + copies:
        copy.start()
    shift = edge.bit_length() - 1
    out_row = lax.broadcasted_iota(jnp.int32, (side, side), 0)
    in_row = lax.broadcasted_iota(jnp.int32, (side, side), 1)
    wanted = ((out_row & (edge - 1)) << shift) | (out_row >> shift)
    swap = jnp.where(in_row == wanted, 1.0, 0.0).astype(bf16)
    for copy in pieces:
        copy.wait()
    flat = pair[...].reshape(q * side, width)
    inputs = normalize(flat)[0].astype(bf16)
    total = flat.astype(f32)
    for copy in copies[:4]:
        copy.wait()
    for at, step in chunks_of(w_gate.shape[1], 256):
        gate = nn(inputs, w_gate[:, at : at + step])
        upper = nn(inputs, w_up[:, at : at + step])
        hidden = (gate * sigmoid(gate) * upper).astype(bf16)
        total = total + nn(hidden, w_out[at : at + step, :])
    upd = total.astype(bf16)
    updated[...] = upd.reshape(updated.shape)
    logit = nt(upd, w_head[...]).astype(bf16)
    logits[...] = logit.reshape(logits.shape)
    packs = lane_packs(bins, side)
    deep = side // packs
    for h in range(q):
        piece = nn(swap, logit[h * side : (h + 1) * side])
        if packs > 1:
            piece = jnp.concatenate([piece[u * deep : (u + 1) * deep] for u in range(packs)], axis=1)
        halves[h] = piece.astype(bf16)
    own = lax.rem(lax.axis_index("row"), q)
    for p in range(q):
        sends[p] = halves[partner(own, p, q)]
    copies[4].wait()


def prepare_kernel(pair, updated, w_gate, w_up, inputs_t, updated_t, hidden, slope, swish, normed, scale):
    q, side, width = pair.shape
    units = w_gate.shape[1]
    normal, scale_inv = normalize(pair[...].reshape(q * side, width))
    normed[...] = normal.reshape(normed.shape)
    scale[...] = jnp.broadcast_to(scale_inv, normal.shape).reshape(scale.shape)
    inputs = normal.astype(bf16)
    for h in range(q):
        inputs_t[h] = inputs[h * side : (h + 1) * side].T
        updated_t[h] = updated[h].T
    for at, step in chunks_of(units, 256):
        span = slice(at, at + step)
        gate = nn(inputs, w_gate[:, span])
        upper = nn(inputs, w_up[:, span])
        sigma = sigmoid(gate)
        swished = gate * sigma
        swish[:, :, span] = swished.reshape(q, side, step)
        hidden[:, :, span] = (swished * upper).astype(bf16).reshape(q, side, step)
        slope[:, :, span] = (upper * sigma * (1.0 + gate * (1.0 - sigma))).reshape(q, side, step)


def backward_kernel(q, p, packed, inputs_t, updated_t, hidden, slope, swish, logits, onehot, w_out, w_head, *rest):
    (piece, near), before, rest = rest[:2], rest[2:6] if p else (), rest[6 if p else 2 :]
    d_updated, d_gate, d_up, *hot, mirrored = rest
    _, side, bins = logits.shape
    width, units = inputs_t.shape[1], hidden.shape[2]
    packs = lane_packs(bins, side)
    own = lax.rem(lax.axis_index("row"), q)
    h = partner(own, p, q)
    inside = lax.axis_index("row") // q == lax.axis_index("col")

    @pl.when(inside)
    def _():
        mirrored[...] = near[p]

    @pl.when(jnp.logical_not(inside))
    def _():
        mirrored[...] = piece[...] if p else piece[0]

    mirrored = mirrored[...]
    if packs > 1:
        mirrored = jnp.concatenate([mirrored[:, u * bins : (u + 1) * bins] for u in range(packs)], axis=0)
    summed = logits[h].astype(f32) + mirrored.astype(f32)
    powers = jnp.exp(summed - jnp.max(summed, axis=-1, keepdims=True))
    probs = powers / jnp.sum(powers, axis=-1, keepdims=True)
    grad_sym = (probs - onehot[h].astype(f32)).astype(bf16)
    cotangent = (grad_sym.astype(f32) * 2.0).astype(bf16)
    d_upd = nn(cotangent, w_head[...])
    d_updated[...] = d_upd
    d_upd_b = d_upd.astype(bf16)
    d_upd_t = d_upd_b.T
    terms = [[], [], []]
    for at, step in chunks_of(units, 256):
        span = slice(at, at + step)
        d_hidden = nt(d_upd_b, w_out[span, :])
        d_gate_part = (d_hidden * slope[h, :, span]).astype(bf16)
        d_up_part = (d_hidden * swish[h, :, span]).astype(bf16)
        d_gate[:, span] = d_gate_part
        d_up[:, span] = d_up_part
        terms[0].append(nn(inputs_t[h], d_gate_part))
        terms[1].append(nn(inputs_t[h], d_up_part))
        terms[2].append(nn(d_upd_t, hidden[h, :, span]))
    terms = [jnp.concatenate(term, axis=1) for term in terms] + [nn(updated_t[h], cotangent)]
    if p:
        terms = [term + ref[...] for term, ref in zip(terms, before)]
    if p < q - 1 or not packed:
        for ref, term in zip(hot, terms):
            ref[...] = term.astype(ref.dtype)
        return
    gate_term, up_term, out_term, head_term = terms
    hot, slots = hot[:-1], hot[-1]
    nrow, ncol = packed
    groups = nrow // q
    lanes, part, tall = units // ncol, width // nrow, units // nrow
    deep = width // q
    for k in range(q):
        for a in range(groups):
            r = a * q + k
            at = 0
            for term in (gate_term, up_term):
                for c in range(ncol):
                    block = term[r * part : (r + 1) * part, c * lanes : (c + 1) * lanes]
                    slots[k, a, at : at + part] = block.astype(bf16)
                    at += part
            blocks = [out_term[u * deep : (u + 1) * deep, r * tall : (r + 1) * tall] for u in range(q)]
            slots[k, a, at : at + deep] = jnp.concatenate(blocks, axis=1).astype(bf16)
            at += deep
            block = head_term[r * part : (r + 1) * part, :]
            block = jnp.concatenate([block, jnp.zeros((part, lanes - bins), f32)], axis=1)
            slots[k, a, at : at + part] = block.astype(bf16)
    for n in range(q):
        hot[n][...] = slots[partner(own, n, q)]


def input_kernel(q, *refs):
    terms, (normed, scale, w_gate, w_up, d_pair) = refs[: 3 * q], refs[3 * q :]
    own = lax.rem(lax.axis_index("row"), q)
    for p in range(q):
        d_updated, d_gate, d_up = terms[3 * p : 3 * p + 3]
        h = partner(own, p, q)
        d_inputs = nt(d_gate[...], w_gate[...]) + nt(d_up[...], w_up[...])
        normal = normed[h]
        d_norm = (
            d_inputs
            - jnp.mean(d_inputs, axis=-1, keepdims=True)
            - normal * jnp.mean(d_inputs * normal, axis=-1, keepdims=True)
        ) * scale[h]
        result = (d_updated[...] + d_norm).astype(bf16)
        d_pair[:, h] = result.reshape(d_pair.shape[0], d_pair.shape[2], d_pair.shape[3])


def core_sum_kernel(q, groups, *rest):
    terms, hot = rest[:q], rest[q:]
    mine = lax.axis_index("row") // q
    for p in range(groups):
        a = partner(mine, p, groups)
        total = terms[0][a].astype(f32)
        for term in terms[1:]:
            total = total + term[a].astype(f32)
        hot[p][...] = total.astype(bf16)


def chip_sum_kernel(q, groups, ncol, shapes, *rest):
    terms, hot, slots = rest[:groups], rest[groups:-1], rest[-1]
    part, lanes, deep, tall, few = shapes
    total = terms[0][...].astype(f32)
    for term in terms[1:]:
        total = total + term[...].astype(f32)
    at = 2 * ncol * part
    out = total[at : at + deep]
    head = total[at + deep : at + deep + part]
    narrow = deep * q // ncol
    fold = lanes // tall
    short = narrow // fold
    for c in range(ncol):
        slots[c, 0:part] = total[c * part : (c + 1) * part].astype(bf16)
        slots[c, part : 2 * part] = total[(ncol + c) * part : (ncol + c + 1) * part].astype(bf16)
        u, top = (c * narrow) // deep, (c * narrow) % deep
        block = out[top : top + narrow, u * tall : (u + 1) * tall]
        block = jnp.concatenate([block[v * short : (v + 1) * short] for v in range(fold)], axis=1)
        slots[c, 2 * part : 2 * part + short] = block.astype(bf16)
        piece = jnp.concatenate([head[:, c * few : (c + 1) * few], jnp.zeros((part, lanes - few), f32)], axis=1)
        slots[c, 2 * part + short : 3 * part + short] = piece.astype(bf16)
    for p in range(ncol):
        hot[p][...] = slots[partner(lax.axis_index("col"), p, ncol)]


def col_sum_kernel(shapes, factor, *rest):
    terms, (gate, up, out, head) = rest[:-4], rest[-4:]
    part, lanes, tall, few = shapes
    total = terms[0][...].astype(f32)
    for term in terms[1:]:
        total = total + term[...].astype(f32)
    total = total * factor
    fold = lanes // tall
    short = out.shape[0] // fold
    gate[...] = total[0:part]
    up[...] = total[part : 2 * part]
    for v in range(fold):
        out[v * short : (v + 1) * short, :] = total[2 * part : 2 * part + short, v * tall : (v + 1) * tall]
    head[...] = total[2 * part + short : 3 * part + short, 0:few]


def core_pairs(nrow, q, p):
    return [(s, s - s % q + partner(s % q, p, q)) for s in range(nrow)]


def shaped(shape, kind):
    return jax.ShapeDtypeStruct(shape, kind)


def cost(flops, moved):
    return pl.CostEstimate(flops=flops, bytes_accessed=moved, transcendentals=0)


def body(pair, targets, w_gate, w_up, w_out, w_head):
    rows, cols, width = pair.shape
    units = w_gate.shape[1]
    bins = w_head.shape[1]
    nrow, ncol = lax.axis_size("row"), lax.axis_size("col")
    q = nrow // ncol
    groups = nrow // q
    side = rows * cols // q
    packs = lane_packs(bins, side)
    head_t = w_head.T
    piece = (side // packs, bins * packs)

    sources = (pair, w_gate, w_up, w_out, head_t, targets)
    kept = [shaped(x.shape, x.dtype) for x in sources]
    kept[0] = shaped((q, side, width), bf16)
    pair, w_gate, w_up, w_out, head_t, targets, updated, logits, sends = pl.pallas_call(
        functools.partial(forward_kernel, q),
        out_shape=kept + [shaped((q, side, width), bf16), shaped((q, side, bins), bf16), shaped((q, *piece), bf16)],
        in_specs=[HBM] * 6,
        out_specs=[VMEM] * 9,
        scratch_shapes=[pltpu.VMEM((q, *piece), bf16), pltpu.SemaphoreType.DMA((5 + q,))],
        compiler_params=PARAMS,
        name="forward",
    )(*(pltpu.with_memory_space_constraint(x, pltpu.HBM) for x in sources))

    pairs = [
        (r * ncol + c, (q * c + (partner(r % q, 1, q) if q == 2 and r // q == c else r % q)) * ncol + r // q)
        for r in range(nrow)
        for c in range(ncol)
    ]
    got = lax.ppermute(sends, ("row", "col"), pairs)
    targets = jnp.swapaxes(targets.reshape(rows, q, rows), 0, 1).reshape(q, side)
    onehot = (targets[:, :, None] == jnp.arange(bins, dtype=jnp.int32)[None, None, :]).astype(bf16)
    inputs_t, updated_t, hidden, slope, swish, normed, scale = pl.pallas_call(
        prepare_kernel,
        out_shape=[
            shaped((q, width, side), bf16),
            shaped((q, width, side), bf16),
            shaped((q, side, units), bf16),
            shaped((q, side, units), f32),
            shaped((q, side, units), f32),
            shaped((q, side, width), f32),
            shaped((q, side, width), f32),
        ],
        in_specs=[VMEM] * 4,
        out_specs=[VMEM] * 7,
        compiler_params=PARAMS,
        cost_estimate=cost(4 * q * side * width * units, 4 * q * side * units),
        name="prepare",
    )(pair, updated, w_gate, w_up)
    got, onehot, inputs_t = lax.optimization_barrier((got, onehot, inputs_t))
    near = [sends, got] if q == 2 else [got] * q
    got = [got] + [lax.ppermute(got[p], "row", core_pairs(nrow, q, p)) for p in range(1, q)]

    part, tall, few = width // nrow, units // nrow, bins // ncol
    lanes, deep = units // ncol, width // q
    fits = (
        part % 16 == 0 and lanes == 128 and tall * q == lanes and bins <= lanes and deep % (width // ncol) == 0
        and (width // ncol * tall // lanes) % 16 == 0
    )
    height = 2 * ncol * part + deep + part
    grads = [(width, n) for n in (units, units, units, bins)]
    hot, d_terms = [], []
    for p in range(q):
        scratch = [pltpu.VMEM(piece, bf16)]
        if p < q - 1 or not fits:
            hot_shapes = [shaped(shape, f32 if p < q - 1 else bf16) for shape in grads]
        else:
            hot_shapes = [shaped((groups, height, lanes), bf16)] * q
            scratch.insert(0, pltpu.VMEM((q, groups, height, lanes), bf16))
        results = pl.pallas_call(
            functools.partial(backward_kernel, q, p, (nrow, ncol) if fits else None),
            out_shape=[shaped((side, width), f32)] + [shaped((side, units), bf16)] * 2 + hot_shapes,
            in_specs=[VMEM] * (11 + len(hot)),
            out_specs=[VMEM] * (3 + len(hot_shapes)),
            scratch_shapes=scratch,
            compiler_params=PARAMS,
            cost_estimate=cost(8 * side * width * units, 4 * side * units),
            name="backward",
        )(inputs_t, updated_t, hidden, slope, swish, logits, onehot, w_out, head_t, got[p], near[p], *hot)
        d_terms += results[:3]
        hot = list(results[3:])

    d_pair = pl.pallas_call(
        functools.partial(input_kernel, q),
        out_shape=shaped((rows, q, cols // q, width), bf16),
        in_specs=[VMEM] * (3 * q + 4),
        out_specs=VMEM,
        compiler_params=PARAMS,
        cost_estimate=cost(4 * q * side * width * units, 4 * q * side * units),
        name="d_inputs",
    )(*d_terms, normed, scale, w_gate, w_up)
    factor = 1.0 / (rows * nrow)
    if not fits:
        owned = []
        hot[2] = hot[2].T
        for term in hot:
            mine = lax.psum_scatter(term, "row", scatter_dimension=0, tiled=True).astype(f32)
            owned.append(lax.psum_scatter(mine, "col", scatter_dimension=1, tiled=True) * factor)
        return (d_pair.reshape(rows, cols, width), *owned)

    terms = [hot[0]]
    for p in range(1, q):
        terms.append(lax.ppermute(hot[p], "row", core_pairs(nrow, q, p)))
    hot = pl.pallas_call(
        functools.partial(core_sum_kernel, q, groups),
        out_shape=[shaped((height, lanes), bf16)] * groups,
        in_specs=[VMEM] * q,
        out_specs=[VMEM] * groups,
        compiler_params=PARAMS,
        name="core_sum",
    )(*terms)
    terms = [hot[0]]
    for p in range(groups - 1, 0, -1):
        terms.append(lax.ppermute(hot[p], "row", [(s, partner(s // q, p, groups) * q + s % q) for s in range(nrow)]))
    *terms, d_pair = lax.optimization_barrier((*terms, d_pair))
    short = 3 * part + width // ncol * tall // lanes
    hot = pl.pallas_call(
        functools.partial(chip_sum_kernel, q, groups, ncol, (part, lanes, deep, tall, few)),
        out_shape=[shaped((short, lanes), bf16)] * ncol,
        in_specs=[VMEM] * groups,
        out_specs=[VMEM] * ncol,
        scratch_shapes=[pltpu.VMEM((ncol, short, lanes), bf16)],
        compiler_params=PARAMS,
        name="chip_sum",
    )(*terms)
    terms = [hot[0]]
    for p in range(ncol - 1, 0, -1):
        terms.append(lax.ppermute(hot[p], "col", [(s, partner(s, p, ncol)) for s in range(ncol)]))
    gate, up, out, head = pl.pallas_call(
        functools.partial(col_sum_kernel, (part, lanes, tall, few), factor),
        out_shape=[
            shaped((part, lanes), f32),
            shaped((part, lanes), f32),
            shaped((width // ncol, tall), f32),
            shaped((part, few), f32),
        ],
        in_specs=[VMEM] * ncol,
        out_specs=[VMEM] * 4,
        compiler_params=PARAMS,
        name="col_sum",
    )(*terms)
    return d_pair.reshape(rows, cols, width), gate, up, out.T, head


def solution(mesh):
    placed = (P("row", "col", None), P("row", "col"), P(), P(), P(), P())
    return jax.shard_map(
        body,
        mesh=mesh,
        in_specs=placed,
        out_specs=(P("row", "col", None), P("row", "col"), P("row", "col"), P("row", "col"), P("row", "col")),
        check_vma=False,
    )
```

```python
import functools

import jax
import jax.numpy as jnp
from jax import lax
from jax.experimental import pallas as pl
from jax.experimental.pallas import tpu as pltpu
from jax.sharding import PartitionSpec as P

eps = 1e-05
f32 = jnp.float32
bf16 = jnp.bfloat16
HBM = pl.BlockSpec(memory_space=pltpu.HBM)
VMEM = pl.BlockSpec(memory_space=pltpu.VMEM)
PARAMS = pltpu.CompilerParams(vmem_limit_bytes=24 * 1024 * 1024)


def nn(a, b):
    return lax.dot_general(a, b, (((1,), (0,)), ((), ())), preferred_element_type=f32)


def nt(a, b):
    return lax.dot_general(a, b, (((1,), (1,)), ((), ())), preferred_element_type=f32)


def tn(a, b):
    return lax.dot_general(a, b, (((0,), (0,)), ((), ())), preferred_element_type=f32)


def normalize(flat):
    values = flat.astype(f32)
    centre = values - jnp.mean(values, axis=-1, keepdims=True)
    scale_inv = lax.rsqrt(jnp.mean(centre * centre, axis=-1, keepdims=True) + eps)
    return centre * scale_inv, scale_inv


def sigmoid(v):
    return 0.5 * jnp.tanh(0.5 * v) + 0.5


def chunks_of(size, most):
    step = most if size % most == 0 else size
    return [(at, step) for at in range(0, size, step)]


def partner(s, p, n):
    if n & (n - 1) == 0:
        return s ^ p
    return (s + p) % n if isinstance(s, int) else lax.rem(s + p, n)


def lane_packs(bins, side):
    packs = max(1, 128 // bins)
    return packs if (side // packs) % 16 == 0 else 1


def forward_kernel(q, *refs):
    sources, (pair, w_gate, w_up, w_out, w_head, marks, sends), (targets, halves, sems) = refs[:6], refs[6:13], refs[13:]
    _, side, width = pair.shape
    edge = sources[0].shape[0]
    bins = w_head.shape[0]
    copies = [
        pltpu.make_async_copy(source, target, sems.at[i])
        for i, (source, target) in enumerate(zip(sources[1:], (w_gate, w_up, w_out, w_head, targets)))
    ]
    pieces = [
        pltpu.make_async_copy(
            sources[0].at[:, h * edge : (h + 1) * edge, :], pair.reshape(q, edge, edge, width).at[h], sems.at[5 + h]
        )
        for h in range(q)
    ]
    for copy in pieces + copies:
        copy.start()
    shift = edge.bit_length() - 1
    out_row = lax.broadcasted_iota(jnp.int32, (side, side), 0)
    in_row = lax.broadcasted_iota(jnp.int32, (side, side), 1)
    wanted = ((out_row & (edge - 1)) << shift) | (out_row >> shift)
    swap = jnp.where(in_row == wanted, 1.0, 0.0).astype(bf16)
    own = lax.rem(lax.axis_index("row"), q)
    for copy in pieces:
        copy.wait()
    flat = pair[...].reshape(q * side, width)
    inputs = normalize(flat)[0].astype(bf16)
    total = flat.astype(f32)
    for copy in copies:
        copy.wait()
    for at, step in chunks_of(w_gate.shape[1], 256):
        gate = nn(inputs, w_gate[:, at : at + step])
        upper = nn(inputs, w_up[:, at : at + step])
        hidden = (gate * sigmoid(gate) * upper).astype(bf16)
        total = total + nn(hidden, w_out[at : at + step, :])
    logit = nt(total.astype(bf16), w_head[...]).astype(bf16)
    packs = lane_packs(bins, side)
    deep = side // packs
    for h in range(q):
        piece = nn(swap, logit[h * side : (h + 1) * side])
        if packs > 1:
            piece = jnp.concatenate([piece[u * deep : (u + 1) * deep] for u in range(packs)], axis=1)
        halves[h] = piece.astype(bf16)
        mark = targets[:, h * edge : (h + 1) * edge].astype(f32)
        marks[h] = jnp.concatenate([mark, jnp.zeros((edge, width - edge), f32)], axis=1).astype(bf16)
    for p in range(q):
        sends[p] = halves[partner(own, p, q)]


def lend_kernel(q, pair, marks, *lent):
    own = lax.rem(lax.axis_index("row"), q)
    side = pair.shape[1]
    for p in range(1, q):
        first, second = lent[2 * p - 2 : 2 * p]
        block = pair[partner(own, p, q)]
        first[...] = block[: side // 2]
        second[: side // 2] = block[side // 2 :]
        second[side // 2 :] = marks[partner(own, p, q)]


def prepare_kernel(q, p, *refs):
    if p:
        first, second, refs = refs[0], refs[1], refs[2:]
        side = 2 * first.shape[0]
        edge = second.shape[0] - first.shape[0]
        flat = jnp.concatenate([first[...], second[: side // 2]], axis=0)
        mark = second[side // 2 :]
    else:
        own = lax.rem(lax.axis_index("row"), q)
        side, edge = refs[0].shape[1], refs[1].shape[1]
        flat, mark, refs = refs[0][own], refs[1][own], refs[2:]
    w_gate, w_up, w_out, w_head, inputs_t, updated_t, hidden, slope, swish, logits, onehot, normed, scale = refs
    width, bins = flat.shape[1], w_head.shape[0]
    normal, scale_inv = normalize(flat)
    normed[...] = normal
    scale[...] = jnp.broadcast_to(scale_inv, normal.shape)
    inputs = normal.astype(bf16)
    inputs_t[...] = inputs.T
    total = flat.astype(f32)
    for at, step in chunks_of(w_gate.shape[1], 256):
        span = slice(at, at + step)
        gate = nn(inputs, w_gate[:, span])
        upper = nn(inputs, w_up[:, span])
        sigma = sigmoid(gate)
        swished = gate * sigma
        hidden_part = (swished * upper).astype(bf16)
        swish[:, span] = swished
        hidden[:, span] = hidden_part
        slope[:, span] = upper * sigma * (1.0 + gate * (1.0 - sigma))
        total = total + nn(hidden_part, w_out[span, :])
    upd = total.astype(bf16)
    updated_t[...] = upd.T
    logits[...] = nt(upd, w_head[...]).astype(bf16)
    shift = edge.bit_length() - 1
    rows = lax.broadcasted_iota(jnp.int32, (side, edge), 0) >> shift
    pick = jnp.where(rows == lax.broadcasted_iota(jnp.int32, (side, edge), 1), 1.0, 0.0).astype(bf16)
    columns = lax.broadcasted_iota(jnp.int32, (side, width), 0) & (edge - 1)
    mask = columns == lax.broadcasted_iota(jnp.int32, (side, width), 1)
    lanes = lax.broadcasted_iota(jnp.int32, (side, bins), 1).astype(f32)
    picked = jnp.where(mask, nn(pick, mark), 0.0).astype(bf16)
    wanted = nn(picked, jnp.ones((width, bins), bf16))
    onehot[...] = jnp.where(wanted == lanes, 1.0, 0.0)


def backward_kernel(q, packed, *refs):
    blocks, (w_out, w_head, far, near), rest = [refs[7 * p : 7 * p + 7] for p in range(q)], refs[7 * q : 7 * q + 4], refs[7 * q + 4 :]
    results, hot, mirrored = [rest[3 * p : 3 * p + 3] for p in range(q)], rest[3 * q : -1], rest[-1]
    (width, side), units, bins = blocks[0][0].shape, w_out.shape[0], w_head.shape[0]
    packs = lane_packs(bins, side)
    own = lax.rem(lax.axis_index("row"), q)
    inside = lax.axis_index("row") // q == lax.axis_index("col")

    @pl.when(inside)
    def _():
        mirrored[...] = near[...]

    @pl.when(jnp.logical_not(inside))
    def _():
        mirrored[...] = far[...]

    totals = None
    for p in range(q):
        inputs_t, updated_t, hidden, slope, swish, logits, onehot = blocks[p]
        d_updated, d_gate, d_up = results[p]
        pieces = [mirrored[p, :, u * bins : (u + 1) * bins] for u in range(packs)]
        summed = logits[...].astype(f32) + jnp.concatenate(pieces, axis=0).astype(f32)
        powers = jnp.exp(summed - jnp.max(summed, axis=-1, keepdims=True))
        probs = powers / jnp.sum(powers, axis=-1, keepdims=True)
        grad_sym = (probs - onehot[...]).astype(bf16)
        cotangent = (grad_sym.astype(f32) * 2.0).astype(bf16)
        d_upd = nn(cotangent, w_head[...])
        d_updated[...] = d_upd
        d_upd_b = d_upd.astype(bf16)
        d_upd_t = d_upd_b.T
        terms = [[], [], []]
        for at, step in chunks_of(units, 256):
            span = slice(at, at + step)
            d_hidden = nt(d_upd_b, w_out[span, :])
            d_gate_part = (d_hidden * slope[:, span]).astype(bf16)
            d_up_part = (d_hidden * swish[:, span]).astype(bf16)
            d_gate[:, span] = d_gate_part
            d_up[:, span] = d_up_part
            terms[0].append(nn(inputs_t[...], d_gate_part))
            terms[1].append(nn(inputs_t[...], d_up_part))
            terms[2].append(nn(d_upd_t, hidden[:, span]))
        terms = [jnp.concatenate(term, axis=1) for term in terms] + [nn(updated_t[...], cotangent)]
        totals = [a + b for a, b in zip(totals, terms)] if p else terms
    if not packed:
        for ref, term in zip(hot, totals):
            ref[...] = term.astype(ref.dtype)
        return
    gate_term, up_term, out_term, head_term = totals
    hot, slots = hot[:-1], hot[-1]
    nrow, ncol = packed
    groups = nrow // q
    lanes, part, tall = units // ncol, width // nrow, units // nrow
    deep = width // q
    for k in range(q):
        for a in range(groups):
            r = a * q + k
            at = 0
            for term in (gate_term, up_term):
                for c in range(ncol):
                    block = term[r * part : (r + 1) * part, c * lanes : (c + 1) * lanes]
                    slots[k, a, at : at + part] = block.astype(bf16)
                    at += part
            pieces = [out_term[u * deep : (u + 1) * deep, r * tall : (r + 1) * tall] for u in range(q)]
            slots[k, a, at : at + deep] = jnp.concatenate(pieces, axis=1).astype(bf16)
            at += deep
            block = head_term[r * part : (r + 1) * part, :]
            block = jnp.concatenate([block, jnp.zeros((part, lanes - bins), f32)], axis=1)
            slots[k, a, at : at + part] = block.astype(bf16)
    for n in range(q):
        hot[n][...] = slots[partner(own, n, q)]


def input_kernel(d_updated, d_gate, d_up, normed, scale, w_gate, w_up, result):
    d_inputs = nt(d_gate[...], w_gate[...]) + nt(d_up[...], w_up[...])
    normal = normed[...]
    d_norm = (
        d_inputs
        - jnp.mean(d_inputs, axis=-1, keepdims=True)
        - normal * jnp.mean(d_inputs * normal, axis=-1, keepdims=True)
    ) * scale[...]
    result[...] = (d_updated[...] + d_norm).astype(bf16)


def place_kernel(q, *refs):
    blocks, d_pair = refs[:-1], refs[-1]
    edge, _, _, width = d_pair.shape
    own = lax.rem(lax.axis_index("row"), q)
    d_pair[:, own] = blocks[0][...].reshape(edge, edge, width)
    for p in range(1, q):
        for n, half in enumerate((slice(0, edge // 2), slice(edge // 2, edge))):
            d_pair[half, partner(own, p, q)] = blocks[2 * p - 1 + n][...].reshape(edge // 2, edge, width)


def core_sum_kernel(q, groups, *rest):
    terms, blocks, hot, handed = rest[:q], rest[q : 2 * q - 1], rest[2 * q - 1 : 2 - 2 * q], rest[2 - 2 * q :]
    mine = lax.axis_index("row") // q
    for p in range(groups):
        a = partner(mine, p, groups)
        total = terms[0][a].astype(f32)
        for term in terms[1:]:
            total = total + term[a].astype(f32)
        hot[p][...] = total.astype(bf16)
    for p, block in enumerate(blocks):
        half = block.shape[0] // 2
        handed[2 * p][...] = block[:half]
        handed[2 * p + 1][...] = block[half:]


def chip_sum_kernel(q, groups, ncol, shapes, *rest):
    terms, hot, slots = rest[:groups], rest[groups:-1], rest[-1]
    part, lanes, deep, tall, few = shapes
    total = terms[0][...].astype(f32)
    for term in terms[1:]:
        total = total + term[...].astype(f32)
    at = 2 * ncol * part
    out = total[at : at + deep]
    head = total[at + deep : at + deep + part]
    narrow = deep * q // ncol
    fold = lanes // tall
    short = narrow // fold
    for c in range(ncol):
        slots[c, 0:part] = total[c * part : (c + 1) * part].astype(bf16)
        slots[c, part : 2 * part] = total[(ncol + c) * part : (ncol + c + 1) * part].astype(bf16)
        u, top = (c * narrow) // deep, (c * narrow) % deep
        block = out[top : top + narrow, u * tall : (u + 1) * tall]
        block = jnp.concatenate([block[v * short : (v + 1) * short] for v in range(fold)], axis=1)
        slots[c, 2 * part : 2 * part + short] = block.astype(bf16)
        piece = jnp.concatenate([head[:, c * few : (c + 1) * few], jnp.zeros((part, lanes - few), f32)], axis=1)
        slots[c, 2 * part + short : 3 * part + short] = piece.astype(bf16)
    for p in range(ncol):
        hot[p][...] = slots[partner(lax.axis_index("col"), p, ncol)]


def col_sum_kernel(shapes, factor, *rest):
    terms, (gate, up, out, head) = rest[:-4], rest[-4:]
    part, lanes, tall, few = shapes
    total = terms[0][...].astype(f32)
    for term in terms[1:]:
        total = total + term[...].astype(f32)
    total = total * factor
    fold = lanes // tall
    short = out.shape[0] // fold
    gate[...] = total[0:part]
    up[...] = total[part : 2 * part]
    for v in range(fold):
        out[v * short : (v + 1) * short, :] = total[2 * part : 2 * part + short, v * tall : (v + 1) * tall]
    head[...] = total[2 * part + short : 3 * part + short, 0:few]


def core_pairs(nrow, q, p):
    return [(s, s - s % q + partner(s % q, p, q)) for s in range(nrow)]


def shaped(shape, kind):
    return jax.ShapeDtypeStruct(shape, kind)


def cost(flops, moved):
    return pl.CostEstimate(flops=flops, bytes_accessed=moved, transcendentals=0)


def body(pair, targets, w_gate, w_up, w_out, w_head):
    rows, cols, width = pair.shape
    units = w_gate.shape[1]
    bins = w_head.shape[1]
    nrow, ncol = lax.axis_size("row"), lax.axis_size("col")
    q = nrow // ncol
    groups = nrow // q
    side = rows * cols // q
    packs = lane_packs(bins, side)
    head_t = w_head.T
    piece = (side // packs, bins * packs)

    sources = (pair, w_gate, w_up, w_out, head_t, targets)
    pair, w_gate, w_up, w_out, head_t, marks, sends = pl.pallas_call(
        functools.partial(forward_kernel, q),
        out_shape=[shaped((q, side, width), bf16)]
        + [shaped(x.shape, bf16) for x in sources[1:5]]
        + [shaped((q, rows, width), bf16), shaped((q, *piece), bf16)],
        in_specs=[HBM] * 6,
        out_specs=[VMEM] * 7,
        scratch_shapes=[
            pltpu.VMEM((rows, cols), jnp.int32),
            pltpu.VMEM((q, *piece), bf16),
            pltpu.SemaphoreType.DMA((5 + q,)),
        ],
        compiler_params=PARAMS,
        name="forward",
    )(*(pltpu.with_memory_space_constraint(x, pltpu.HBM) for x in sources))

    pairs = [
        (r * ncol + c, (q * c + (partner(r % q, 1, q) if q == 2 and r // q == c else r % q)) * ncol + r // q)
        for r in range(nrow)
        for c in range(ncol)
    ]
    far = lax.ppermute(sends, ("row", "col"), pairs)
    lent = pl.pallas_call(
        functools.partial(lend_kernel, q),
        out_shape=[shaped((side // 2, width), bf16), shaped((side // 2 + rows, width), bf16)] * (q - 1),
        in_specs=[VMEM] * 2,
        out_specs=[VMEM] * (2 * q - 2),
        compiler_params=PARAMS,
        name="lend",
    )(pair, marks)
    borrowed = [lax.ppermute(x, "row", core_pairs(nrow, q, n // 2 + 1)) for n, x in enumerate(lent)]
    prepared = []
    for p in range(q):
        source = borrowed[2 * p - 2 : 2 * p] if p else (pair, marks)
        prepared.append(
            pl.pallas_call(
                functools.partial(prepare_kernel, q, p),
                out_shape=[
                    shaped((width, side), bf16),
                    shaped((width, side), bf16),
                    shaped((side, units), bf16),
                    shaped((side, units), f32),
                    shaped((side, units), f32),
                    shaped((side, bins), bf16),
                    shaped((side, bins), f32),
                    shaped((side, width), f32),
                    shaped((side, width), f32),
                ],
                in_specs=[VMEM] * (len(source) + 4),
                out_specs=[VMEM] * 9,
                compiler_params=PARAMS,
                cost_estimate=cost(0, 0) if p else cost(6 * side * width * units, 8 * side * units),
                name="prepare",
            )(*source, w_gate, w_up, w_out, head_t)
        )

    part, tall, few = width // nrow, units // nrow, bins // ncol
    lanes, deep = units // ncol, width // q
    fits = (
        part % 16 == 0 and lanes == 128 and tall * q == lanes and bins <= lanes and deep % (width // ncol) == 0
        and (width // ncol * tall // lanes) % 16 == 0
    )
    height = 2 * ncol * part + deep + part
    if fits:
        hot_shapes = [shaped((groups, height, lanes), bf16)] * q
        scratch = [pltpu.VMEM((q, groups, height, lanes), bf16)]
    else:
        hot_shapes = [shaped((width, n), bf16) for n in (units, units, units, bins)]
        scratch = []
    results = pl.pallas_call(
        functools.partial(backward_kernel, q, (nrow, ncol) if fits else None),
        out_shape=([shaped((side, width), f32)] + [shaped((side, units), bf16)] * 2) * q + hot_shapes,
        in_specs=[VMEM] * (7 * q + 4),
        out_specs=[VMEM] * (3 * q + len(hot_shapes)),
        scratch_shapes=scratch + [pltpu.VMEM((q, *piece), bf16)],
        compiler_params=PARAMS,
        cost_estimate=cost(8 * q * side * width * units, 4 * q * side * units),
        name="backward",
    )(*(x for block in prepared for x in block[:7]), w_out, head_t, far, sends)
    hot = list(results[3 * q :])

    def d_inputs(p):
        return pl.pallas_call(
            input_kernel,
            out_shape=shaped((side, width), bf16),
            in_specs=[VMEM] * 7,
            out_specs=VMEM,
            compiler_params=PARAMS,
            cost_estimate=cost(4 * side * width * units, 4 * side * units),
            name="d_inputs",
        )(*results[3 * p : 3 * p + 3], *prepared[p][7:], w_gate, w_up)

    d_blocks = [d_inputs(p) for p in range(q)]

    def returned(blocks):
        moved = [lax.ppermute(x, "row", core_pairs(nrow, q, n // 2 + 1)) for n, x in enumerate(blocks[1:])]
        return blocks[:1] + moved

    def placed(blocks):
        return pl.pallas_call(
            functools.partial(place_kernel, q),
            out_shape=shaped((rows, q, cols // q, width), bf16),
            in_specs=[VMEM] * (2 * q - 1),
            out_specs=VMEM,
            compiler_params=PARAMS,
            name="place",
        )(*blocks).reshape(rows, cols, width)

    factor = 1.0 / (rows * nrow)
    if not fits:
        owned = []
        hot[2] = hot[2].T
        for term in hot:
            mine = lax.psum_scatter(term, "row", scatter_dimension=0, tiled=True).astype(f32)
            owned.append(lax.psum_scatter(mine, "col", scatter_dimension=1, tiled=True) * factor)
        d_blocks = d_blocks[:1] + [half for block in d_blocks[1:] for half in (block[: side // 2], block[side // 2 :])]
        return (placed(returned(d_blocks)), *owned)

    terms = [hot[0]]
    for p in range(1, q):
        terms.append(lax.ppermute(hot[p], "row", core_pairs(nrow, q, p)))
    terms, d_blocks = lax.optimization_barrier((terms, d_blocks))
    hot = pl.pallas_call(
        functools.partial(core_sum_kernel, q, groups),
        out_shape=[shaped((height, lanes), bf16)] * groups + [shaped((side // 2, width), bf16)] * (2 * q - 2),
        in_specs=[VMEM] * (2 * q - 1),
        out_specs=[VMEM] * (groups + 2 * q - 2),
        compiler_params=PARAMS,
        name="core_sum",
    )(*terms, *d_blocks[1:])
    hot, d_blocks = hot[:groups], d_blocks[:1] + list(hot[groups:])
    terms = [hot[0]]
    for p in range(groups - 1, 0, -1):
        terms.append(lax.ppermute(hot[p], "row", [(s, partner(s // q, p, groups) * q + s % q) for s in range(nrow)]))
    terms, d_blocks = lax.optimization_barrier((terms, returned(d_blocks)))
    short = 3 * part + width // ncol * tall // lanes
    hot = pl.pallas_call(
        functools.partial(chip_sum_kernel, q, groups, ncol, (part, lanes, deep, tall, few)),
        out_shape=[shaped((short, lanes), bf16)] * ncol,
        in_specs=[VMEM] * groups,
        out_specs=[VMEM] * ncol,
        scratch_shapes=[pltpu.VMEM((ncol, short, lanes), bf16)],
        compiler_params=PARAMS,
        name="chip_sum",
    )(*terms)
    terms = [hot[0]]
    for p in sorted(range(1, ncol), key=lambda p: (p != ncol // 2, -p)):
        terms.append(lax.ppermute(hot[p], "col", [(s, partner(s, p, ncol)) for s in range(ncol)]))
    *terms, d_pair = lax.optimization_barrier((*terms, placed(d_blocks)))
    gate, up, out, head = pl.pallas_call(
        functools.partial(col_sum_kernel, (part, lanes, tall, few), factor),
        out_shape=[
            shaped((part, lanes), f32),
            shaped((part, lanes), f32),
            shaped((width // ncol, tall), f32),
            shaped((part, few), f32),
        ],
        in_specs=[VMEM] * ncol,
        out_specs=[VMEM] * 4,
        compiler_params=PARAMS,
        name="col_sum",
    )(*terms)
    return d_pair, gate, up, out.T, head


def solution(mesh):
    placed = (P("row", "col", None), P("row", "col"), P(), P(), P(), P())
    return jax.shard_map(
        body,
        mesh=mesh,
        in_specs=placed,
        out_specs=(P("row", "col", None), P("row", "col"), P("row", "col"), P("row", "col"), P("row", "col")),
        check_vma=False,
    )
```

```python
import functools

import jax
import jax.numpy as jnp
from jax import lax
from jax.experimental import pallas as pl
from jax.experimental.pallas import tpu as pltpu
from jax.sharding import PartitionSpec as P

eps = 1e-05
f32 = jnp.float32
bf16 = jnp.bfloat16
HBM = pl.BlockSpec(memory_space=pltpu.HBM)
VMEM = pl.BlockSpec(memory_space=pltpu.VMEM)
PARAMS = pltpu.CompilerParams(vmem_limit_bytes=24 * 1024 * 1024)


def nn(a, b):
    return lax.dot_general(a, b, (((1,), (0,)), ((), ())), preferred_element_type=f32)


def nt(a, b):
    return lax.dot_general(a, b, (((1,), (1,)), ((), ())), preferred_element_type=f32)


def tn(a, b):
    return lax.dot_general(a, b, (((0,), (0,)), ((), ())), preferred_element_type=f32)


def normalize(flat):
    values = flat.astype(f32)
    centre = values - jnp.mean(values, axis=-1, keepdims=True)
    scale_inv = lax.rsqrt(jnp.mean(centre * centre, axis=-1, keepdims=True) + eps)
    return centre * scale_inv, scale_inv


def sigmoid(v):
    return 0.5 * jnp.tanh(0.5 * v) + 0.5


def chunks_of(size, most):
    step = most if size % most == 0 else size
    return [(at, step) for at in range(0, size, step)]


def partner(s, p, n):
    if n & (n - 1) == 0:
        return s ^ p
    return (s + p) % n if isinstance(s, int) else lax.rem(s + p, n)


def following(s, p, n):
    return (s + p) % n if isinstance(s, int) else lax.rem(s + p, n)


def lane_packs(bins, side):
    packs = max(1, 128 // bins)
    return packs if (side // packs) % 16 == 0 else 1


def forward_kernel(q, *refs):
    sources, (pair, w_gate, w_up, w_out, w_head, marks, sends), (targets, halves, sems) = refs[:6], refs[6:13], refs[13:]
    _, side, width = pair.shape
    edge = sources[0].shape[0]
    bins = w_head.shape[0]
    copies = [
        pltpu.make_async_copy(source, target, sems.at[i])
        for i, (source, target) in enumerate(zip(sources[1:], (w_gate, w_up, w_out, w_head, targets)))
    ]
    pieces = [
        pltpu.make_async_copy(
            sources[0].at[:, h * edge : (h + 1) * edge, :], pair.reshape(q, edge, edge, width).at[h], sems.at[5 + h]
        )
        for h in range(q)
    ]
    for copy in pieces + copies:
        copy.start()
    shift = edge.bit_length() - 1
    out_row = lax.broadcasted_iota(jnp.int32, (side, side), 0)
    in_row = lax.broadcasted_iota(jnp.int32, (side, side), 1)
    wanted = ((out_row & (edge - 1)) << shift) | (out_row >> shift)
    swap = jnp.where(in_row == wanted, 1.0, 0.0).astype(bf16)
    own = lax.rem(lax.axis_index("row"), q)
    for copy in pieces:
        copy.wait()
    flat = pair[...].reshape(q * side, width)
    inputs = normalize(flat)[0].astype(bf16)
    total = flat.astype(f32)
    for copy in copies:
        copy.wait()
    for at, step in chunks_of(w_gate.shape[1], 256):
        gate = nn(inputs, w_gate[:, at : at + step])
        upper = nn(inputs, w_up[:, at : at + step])
        hidden = (gate * sigmoid(gate) * upper).astype(bf16)
        total = total + nn(hidden, w_out[at : at + step, :])
    logit = nt(total.astype(bf16), w_head[...]).astype(bf16)
    packs = lane_packs(bins, side)
    deep = side // packs
    for h in range(q):
        piece = nn(swap, logit[h * side : (h + 1) * side])
        if packs > 1:
            piece = jnp.concatenate([piece[u * deep : (u + 1) * deep] for u in range(packs)], axis=1)
        halves[h] = piece.astype(bf16)
        mark = targets[:, h * edge : (h + 1) * edge].astype(f32)
        marks[h] = jnp.concatenate([mark, jnp.zeros((edge, width - edge), f32)], axis=1).astype(bf16)
    for p in range(q):
        sends[p] = halves[partner(own, p, q)]


def lend_kernel(q, pair, marks, *lent):
    own = lax.rem(lax.axis_index("row"), q)
    side = pair.shape[1]
    for p in range(1, q):
        first, second = lent[2 * p - 2 : 2 * p]
        block = pair[partner(own, p, q)]
        first[...] = block[: side // 2]
        second[: side // 2] = block[side // 2 :]
        second[side // 2 :] = marks[partner(own, p, q)]


def prepare_kernel(q, p, *refs):
    if p:
        first, second, refs = refs[0], refs[1], refs[2:]
        side = 2 * first.shape[0]
        edge = second.shape[0] - first.shape[0]
        flat = jnp.concatenate([first[...], second[: side // 2]], axis=0)
        mark = second[side // 2 :]
    else:
        own = lax.rem(lax.axis_index("row"), q)
        side, edge = refs[0].shape[1], refs[1].shape[1]
        flat, mark, refs = refs[0][own], refs[1][own], refs[2:]
    w_gate, w_up, w_out, w_head, inputs_t, updated_t, hidden, slope, swish, logits, onehot, normed, scale = refs
    width, bins = flat.shape[1], w_head.shape[0]
    normal, scale_inv = normalize(flat)
    normed[...] = normal
    scale[...] = jnp.broadcast_to(scale_inv, normal.shape)
    inputs = normal.astype(bf16)
    inputs_t[...] = inputs.T
    total = flat.astype(f32)
    for at, step in chunks_of(w_gate.shape[1], 256):
        span = slice(at, at + step)
        gate = nn(inputs, w_gate[:, span])
        upper = nn(inputs, w_up[:, span])
        sigma = sigmoid(gate)
        swished = gate * sigma
        hidden_part = (swished * upper).astype(bf16)
        swish[:, span] = swished
        hidden[:, span] = hidden_part
        slope[:, span] = upper * sigma * (1.0 + gate * (1.0 - sigma))
        total = total + nn(hidden_part, w_out[span, :])
    upd = total.astype(bf16)
    updated_t[...] = upd.T
    logits[...] = nt(upd, w_head[...]).astype(bf16)
    shift = edge.bit_length() - 1
    rows = lax.broadcasted_iota(jnp.int32, (side, edge), 0) >> shift
    pick = jnp.where(rows == lax.broadcasted_iota(jnp.int32, (side, edge), 1), 1.0, 0.0).astype(bf16)
    columns = lax.broadcasted_iota(jnp.int32, (side, width), 0) & (edge - 1)
    mask = columns == lax.broadcasted_iota(jnp.int32, (side, width), 1)
    lanes = lax.broadcasted_iota(jnp.int32, (side, bins), 1).astype(f32)
    picked = jnp.where(mask, nn(pick, mark), 0.0).astype(bf16)
    wanted = nn(picked, jnp.ones((width, bins), bf16))
    onehot[...] = jnp.where(wanted == lanes, 1.0, 0.0)


def backward_kernel(q, packed, *refs):
    blocks, (w_out, w_head, far, near), rest = [refs[7 * p : 7 * p + 7] for p in range(q)], refs[7 * q : 7 * q + 4], refs[7 * q + 4 :]
    results, hot, mirrored = [rest[3 * p : 3 * p + 3] for p in range(q)], rest[3 * q : -1], rest[-1]
    (width, side), units, bins = blocks[0][0].shape, w_out.shape[0], w_head.shape[0]
    packs = lane_packs(bins, side)
    own = lax.rem(lax.axis_index("row"), q)
    inside = lax.axis_index("row") // q == lax.axis_index("col")

    @pl.when(inside)
    def _():
        mirrored[...] = near[...]

    @pl.when(jnp.logical_not(inside))
    def _():
        mirrored[...] = far[...]

    totals = None
    for p in range(q):
        inputs_t, updated_t, hidden, slope, swish, logits, onehot = blocks[p]
        d_updated, d_gate, d_up = results[p]
        pieces = [mirrored[p, :, u * bins : (u + 1) * bins] for u in range(packs)]
        summed = logits[...].astype(f32) + jnp.concatenate(pieces, axis=0).astype(f32)
        powers = jnp.exp(summed - jnp.max(summed, axis=-1, keepdims=True))
        probs = powers / jnp.sum(powers, axis=-1, keepdims=True)
        grad_sym = (probs - onehot[...]).astype(bf16)
        cotangent = (grad_sym.astype(f32) * 2.0).astype(bf16)
        d_upd = nn(cotangent, w_head[...])
        d_updated[...] = d_upd
        d_upd_b = d_upd.astype(bf16)
        d_upd_t = d_upd_b.T
        terms = [[], [], []]
        for at, step in chunks_of(units, 256):
            span = slice(at, at + step)
            d_hidden = nt(d_upd_b, w_out[span, :])
            d_gate_part = (d_hidden * slope[:, span]).astype(bf16)
            d_up_part = (d_hidden * swish[:, span]).astype(bf16)
            d_gate[:, span] = d_gate_part
            d_up[:, span] = d_up_part
            terms[0].append(nn(inputs_t[...], d_gate_part))
            terms[1].append(nn(inputs_t[...], d_up_part))
            terms[2].append(nn(d_upd_t, hidden[:, span]))
        terms = [jnp.concatenate(term, axis=1) for term in terms] + [nn(updated_t[...], cotangent)]
        totals = [a + b for a, b in zip(totals, terms)] if p else terms
    if not packed:
        for ref, term in zip(hot, totals):
            ref[...] = term.astype(ref.dtype)
        return
    gate_term, up_term, out_term, head_term = totals
    hot, slots = hot[:-1], hot[-1]
    nrow, ncol = packed
    groups = nrow // q
    lanes, part, tall = units // ncol, width // nrow, units // nrow
    deep = width // q
    for k in range(q):
        for a in range(groups):
            r = a * q + k
            at = 0
            for term in (gate_term, up_term):
                for c in range(ncol):
                    block = term[r * part : (r + 1) * part, c * lanes : (c + 1) * lanes]
                    slots[k, a, at : at + part] = block.astype(bf16)
                    at += part
            pieces = [out_term[u * deep : (u + 1) * deep, r * tall : (r + 1) * tall] for u in range(q)]
            slots[k, a, at : at + deep] = jnp.concatenate(pieces, axis=1).astype(bf16)
            at += deep
            block = head_term[r * part : (r + 1) * part, :]
            block = jnp.concatenate([block, jnp.zeros((part, lanes - bins), f32)], axis=1)
            slots[k, a, at : at + part] = block.astype(bf16)
    for n in range(q):
        hot[n][...] = slots[partner(own, n, q)]


def input_kernel(d_updated, d_gate, d_up, normed, scale, w_gate, w_up, result):
    d_inputs = nt(d_gate[...], w_gate[...]) + nt(d_up[...], w_up[...])
    normal = normed[...]
    d_norm = (
        d_inputs
        - jnp.mean(d_inputs, axis=-1, keepdims=True)
        - normal * jnp.mean(d_inputs * normal, axis=-1, keepdims=True)
    ) * scale[...]
    result[...] = (d_updated[...] + d_norm).astype(bf16)


def place_kernel(q, *refs):
    blocks, d_pair = refs[:-1], refs[-1]
    edge, _, _, width = d_pair.shape
    own = lax.rem(lax.axis_index("row"), q)
    d_pair[:, own] = blocks[0][...].reshape(edge, edge, width)
    for p in range(1, q):
        for n, half in enumerate((slice(0, edge // 2), slice(edge // 2, edge))):
            d_pair[half, partner(own, p, q)] = blocks[2 * p - 1 + n][...].reshape(edge // 2, edge, width)


def core_sum_kernel(q, groups, *rest):
    terms, blocks, hot, handed = rest[:q], rest[q : 2 * q - 1], rest[2 * q - 1 : 2 - 2 * q], rest[2 - 2 * q :]
    mine = lax.axis_index("row") // q
    for p in range(groups):
        a = following(mine, p, groups)
        total = terms[0][a].astype(f32)
        for term in terms[1:]:
            total = total + term[a].astype(f32)
        hot[p][...] = total.astype(bf16)
    for p, block in enumerate(blocks):
        half = block.shape[0] // 2
        handed[2 * p][...] = block[:half]
        handed[2 * p + 1][...] = block[half:]


def chip_sum_kernel(q, groups, ncol, shapes, *rest):
    terms, hot, slots = rest[:groups], rest[groups:-1], rest[-1]
    part, lanes, deep, tall, few = shapes
    total = terms[0][...].astype(f32)
    for term in terms[1:]:
        total = total + term[...].astype(f32)
    at = 2 * ncol * part
    out = total[at : at + deep]
    head = total[at + deep : at + deep + part]
    narrow = deep * q // ncol
    fold = lanes // tall
    short = narrow // fold
    for c in range(ncol):
        slots[c, 0:part] = total[c * part : (c + 1) * part].astype(bf16)
        slots[c, part : 2 * part] = total[(ncol + c) * part : (ncol + c + 1) * part].astype(bf16)
        u, top = (c * narrow) // deep, (c * narrow) % deep
        block = out[top : top + narrow, u * tall : (u + 1) * tall]
        block = jnp.concatenate([block[v * short : (v + 1) * short] for v in range(fold)], axis=1)
        slots[c, 2 * part : 2 * part + short] = block.astype(bf16)
        piece = jnp.concatenate([head[:, c * few : (c + 1) * few], jnp.zeros((part, lanes - few), f32)], axis=1)
        slots[c, 2 * part + short : 3 * part + short] = piece.astype(bf16)
    for p in range(ncol):
        hot[p][...] = slots[partner(lax.axis_index("col"), p, ncol)]


def col_sum_kernel(shapes, factor, *rest):
    terms, (gate, up, out, head) = rest[:-4], rest[-4:]
    part, lanes, tall, few = shapes
    total = terms[0][...].astype(f32)
    for term in terms[1:]:
        total = total + term[...].astype(f32)
    total = total * factor
    fold = lanes // tall
    short = out.shape[0] // fold
    gate[...] = total[0:part]
    up[...] = total[part : 2 * part]
    for v in range(fold):
        out[v * short : (v + 1) * short, :] = total[2 * part : 2 * part + short, v * tall : (v + 1) * tall]
    head[...] = total[2 * part + short : 3 * part + short, 0:few]


def core_pairs(nrow, q, p):
    return [(s, s - s % q + partner(s % q, p, q)) for s in range(nrow)]


def shaped(shape, kind):
    return jax.ShapeDtypeStruct(shape, kind)


def cost(flops, moved):
    return pl.CostEstimate(flops=flops, bytes_accessed=moved, transcendentals=0)


def body(pair, targets, w_gate, w_up, w_out, w_head):
    rows, cols, width = pair.shape
    units = w_gate.shape[1]
    bins = w_head.shape[1]
    nrow, ncol = lax.axis_size("row"), lax.axis_size("col")
    q = nrow // ncol
    groups = nrow // q
    side = rows * cols // q
    packs = lane_packs(bins, side)
    head_t = w_head.T
    piece = (side // packs, bins * packs)

    sources = (pair, w_gate, w_up, w_out, head_t, targets)
    pair, w_gate, w_up, w_out, head_t, marks, sends = pl.pallas_call(
        functools.partial(forward_kernel, q),
        out_shape=[shaped((q, side, width), bf16)]
        + [shaped(x.shape, bf16) for x in sources[1:5]]
        + [shaped((q, rows, width), bf16), shaped((q, *piece), bf16)],
        in_specs=[HBM] * 6,
        out_specs=[VMEM] * 7,
        scratch_shapes=[
            pltpu.VMEM((rows, cols), jnp.int32),
            pltpu.VMEM((q, *piece), bf16),
            pltpu.SemaphoreType.DMA((5 + q,)),
        ],
        compiler_params=PARAMS,
        name="forward",
    )(*(pltpu.with_memory_space_constraint(x, pltpu.HBM) for x in sources))

    pairs = [
        (r * ncol + c, (q * c + (partner(r % q, 1, q) if q == 2 and r // q == c else r % q)) * ncol + r // q)
        for r in range(nrow)
        for c in range(ncol)
    ]
    far = lax.ppermute(sends, ("row", "col"), pairs)
    lent = pl.pallas_call(
        functools.partial(lend_kernel, q),
        out_shape=[shaped((side // 2, width), bf16), shaped((side // 2 + rows, width), bf16)] * (q - 1),
        in_specs=[VMEM] * 2,
        out_specs=[VMEM] * (2 * q - 2),
        compiler_params=PARAMS,
        name="lend",
    )(pair, marks)
    borrowed = [lax.ppermute(x, "row", core_pairs(nrow, q, n // 2 + 1)) for n, x in enumerate(lent)]
    prepared = []
    for p in range(q):
        source = borrowed[2 * p - 2 : 2 * p] if p else (pair, marks)
        prepared.append(
            pl.pallas_call(
                functools.partial(prepare_kernel, q, p),
                out_shape=[
                    shaped((width, side), bf16),
                    shaped((width, side), bf16),
                    shaped((side, units), bf16),
                    shaped((side, units), f32),
                    shaped((side, units), f32),
                    shaped((side, bins), bf16),
                    shaped((side, bins), f32),
                    shaped((side, width), f32),
                    shaped((side, width), f32),
                ],
                in_specs=[VMEM] * (len(source) + 4),
                out_specs=[VMEM] * 9,
                compiler_params=PARAMS,
                cost_estimate=cost(0, 0) if p else cost(6 * side * width * units, 8 * side * units),
                name="prepare",
            )(*source, w_gate, w_up, w_out, head_t)
        )

    part, tall, few = width // nrow, units // nrow, bins // ncol
    lanes, deep = units // ncol, width // q
    fits = (
        part % 16 == 0 and lanes == 128 and tall * q == lanes and bins <= lanes and deep % (width // ncol) == 0
        and (width // ncol * tall // lanes) % 16 == 0
    )
    height = 2 * ncol * part + deep + part
    if fits:
        hot_shapes = [shaped((groups, height, lanes), bf16)] * q
        scratch = [pltpu.VMEM((q, groups, height, lanes), bf16)]
    else:
        hot_shapes = [shaped((width, n), bf16) for n in (units, units, units, bins)]
        scratch = []
    results = pl.pallas_call(
        functools.partial(backward_kernel, q, (nrow, ncol) if fits else None),
        out_shape=([shaped((side, width), f32)] + [shaped((side, units), bf16)] * 2) * q + hot_shapes,
        in_specs=[VMEM] * (7 * q + 4),
        out_specs=[VMEM] * (3 * q + len(hot_shapes)),
        scratch_shapes=scratch + [pltpu.VMEM((q, *piece), bf16)],
        compiler_params=PARAMS,
        cost_estimate=cost(8 * q * side * width * units, 4 * q * side * units),
        name="backward",
    )(*(x for block in prepared for x in block[:7]), w_out, head_t, far, sends)
    hot = list(results[3 * q :])

    def d_inputs(p):
        return pl.pallas_call(
            input_kernel,
            out_shape=shaped((side, width), bf16),
            in_specs=[VMEM] * 7,
            out_specs=VMEM,
            compiler_params=PARAMS,
            cost_estimate=cost(4 * side * width * units, 4 * side * units),
            name="d_inputs",
        )(*results[3 * p : 3 * p + 3], *prepared[p][7:], w_gate, w_up)

    d_blocks = [d_inputs(p) for p in range(q)]

    def returned(blocks):
        moved = [lax.ppermute(x, "row", core_pairs(nrow, q, n // 2 + 1)) for n, x in enumerate(blocks[1:])]
        return blocks[:1] + moved

    def placed(blocks):
        return pl.pallas_call(
            functools.partial(place_kernel, q),
            out_shape=shaped((rows, q, cols // q, width), bf16),
            in_specs=[VMEM] * (2 * q - 1),
            out_specs=VMEM,
            compiler_params=PARAMS,
            name="place",
        )(*blocks).reshape(rows, cols, width)

    factor = 1.0 / (rows * nrow)
    if not fits:
        owned = []
        hot[2] = hot[2].T
        for term in hot:
            mine = lax.psum_scatter(term, "row", scatter_dimension=0, tiled=True).astype(f32)
            owned.append(lax.psum_scatter(mine, "col", scatter_dimension=1, tiled=True) * factor)
        d_blocks = d_blocks[:1] + [half for block in d_blocks[1:] for half in (block[: side // 2], block[side // 2 :])]
        return (placed(returned(d_blocks)), *owned)

    terms = [hot[0]]
    for p in range(1, q):
        terms.append(lax.ppermute(hot[p], "row", core_pairs(nrow, q, p)))
    terms, d_blocks = lax.optimization_barrier((terms, d_blocks))
    hot = pl.pallas_call(
        functools.partial(core_sum_kernel, q, groups),
        out_shape=[shaped((height, lanes), bf16)] * groups + [shaped((side // 2, width), bf16)] * (2 * q - 2),
        in_specs=[VMEM] * (2 * q - 1),
        out_specs=[VMEM] * (groups + 2 * q - 2),
        compiler_params=PARAMS,
        name="core_sum",
    )(*terms, *d_blocks[1:])
    hot, d_blocks = hot[:groups], d_blocks[:1] + list(hot[groups:])
    terms = [hot[0]]
    for p in range(1, groups):
        terms.append(lax.ppermute(hot[p], "row", [(s, following(s // q, p, groups) * q + s % q) for s in range(nrow)]))
    terms, d_blocks = lax.optimization_barrier((terms, returned(d_blocks)))
    short = 3 * part + width // ncol * tall // lanes
    hot = pl.pallas_call(
        functools.partial(chip_sum_kernel, q, groups, ncol, (part, lanes, deep, tall, few)),
        out_shape=[shaped((short, lanes), bf16)] * ncol,
        in_specs=[VMEM] * groups,
        out_specs=[VMEM] * ncol,
        scratch_shapes=[pltpu.VMEM((ncol, short, lanes), bf16)],
        compiler_params=PARAMS,
        name="chip_sum",
    )(*terms)
    terms = [hot[0]]
    for p in sorted(range(1, ncol), key=lambda p: (p != ncol // 2, -p)):
        terms.append(lax.ppermute(hot[p], "col", [(s, partner(s, p, ncol)) for s in range(ncol)]))
    *terms, d_pair = lax.optimization_barrier((*terms, placed(d_blocks)))
    gate, up, out, head = pl.pallas_call(
        functools.partial(col_sum_kernel, (part, lanes, tall, few), factor),
        out_shape=[
            shaped((part, lanes), f32),
            shaped((part, lanes), f32),
            shaped((width // ncol, tall), f32),
            shaped((part, few), f32),
        ],
        in_specs=[VMEM] * ncol,
        out_specs=[VMEM] * 4,
        compiler_params=PARAMS,
        name="col_sum",
    )(*terms)
    return d_pair, gate, up, out.T, head


def solution(mesh):
    placed = (P("row", "col", None), P("row", "col"), P(), P(), P(), P())
    return jax.shard_map(
        body,
        mesh=mesh,
        in_specs=placed,
        out_specs=(P("row", "col", None), P("row", "col"), P("row", "col"), P("row", "col"), P("row", "col")),
        check_vma=False,
    )
```

```python
import functools

import jax
import jax.numpy as jnp
from jax import lax
from jax.experimental import pallas as pl
from jax.experimental.pallas import tpu as pltpu
from jax.sharding import PartitionSpec as P

eps = 1e-05
f32 = jnp.float32
bf16 = jnp.bfloat16
HBM = pl.BlockSpec(memory_space=pltpu.HBM)
VMEM = pl.BlockSpec(memory_space=pltpu.VMEM)
PARAMS = pltpu.CompilerParams(vmem_limit_bytes=24 * 1024 * 1024)


def nn(a, b):
    return lax.dot_general(a, b, (((1,), (0,)), ((), ())), preferred_element_type=f32)


def nt(a, b):
    return lax.dot_general(a, b, (((1,), (1,)), ((), ())), preferred_element_type=f32)


def tn(a, b):
    return lax.dot_general(a, b, (((0,), (0,)), ((), ())), preferred_element_type=f32)


def normalize(flat):
    values = flat.astype(f32)
    centre = values - jnp.mean(values, axis=-1, keepdims=True)
    scale_inv = lax.rsqrt(jnp.mean(centre * centre, axis=-1, keepdims=True) + eps)
    return centre * scale_inv, scale_inv


def sigmoid(v):
    return 0.5 * jnp.tanh(0.5 * v) + 0.5


def chunks_of(size, most):
    step = most if size % most == 0 else size
    return [(at, step) for at in range(0, size, step)]


def partner(s, p, n):
    if n & (n - 1) == 0:
        return s ^ p
    return (s + p) % n if isinstance(s, int) else lax.rem(s + p, n)


def following(s, p, n):
    return (s + p) % n if isinstance(s, int) else lax.rem(s + p, n)


def joined(refs, axis):
    return jnp.concatenate([ref[...] for ref in refs], axis=axis)


def lane_packs(bins, side):
    packs = max(1, 128 // bins)
    return packs if (side // packs) % 16 == 0 else 1


def forward_kernel(q, *refs):
    sources, (pair, w_gate, w_up, w_out, w_head, marks, sends), scratch = refs[:6], refs[6:13], refs[13:]
    targets, halves, hidden, sems = scratch
    _, side, width = pair.shape
    edge = sources[0].shape[0]
    bins = w_head.shape[0]
    copies = [
        pltpu.make_async_copy(source, target, sems.at[i])
        for i, (source, target) in enumerate(zip(sources[1:], (w_gate, w_up, w_out, w_head, targets)))
    ]
    pieces = [
        pltpu.make_async_copy(
            sources[0].at[:, h * edge : (h + 1) * edge, :], pair.reshape(q, edge, edge, width).at[h], sems.at[5 + h]
        )
        for h in range(q)
    ]
    for copy in pieces + copies:
        copy.start()
    shift = edge.bit_length() - 1
    out_row = lax.broadcasted_iota(jnp.int32, (side, side), 0)
    in_row = lax.broadcasted_iota(jnp.int32, (side, side), 1)
    wanted = ((out_row & (edge - 1)) << shift) | (out_row >> shift)
    swap = jnp.where(in_row == wanted, 1.0, 0.0).astype(bf16)
    own = lax.rem(lax.axis_index("row"), q)
    for copy in pieces:
        copy.wait()
    flat = pair[...].reshape(q * side, width)
    inputs = normalize(flat)[0].astype(bf16)
    for copy in copies[:2]:
        copy.wait()
    for top, tall in chunks_of(q * side, 128):
        for at, step in chunks_of(w_gate.shape[1], 256):
            gate = nn(inputs[top : top + tall], w_gate[:, at : at + step])
            upper = nn(inputs[top : top + tall], w_up[:, at : at + step])
            hidden[top : top + tall, at : at + step] = (gate * sigmoid(gate) * upper).astype(bf16)
    for copy in copies[2:]:
        copy.wait()
    total = flat.astype(f32) + nn(hidden[...], w_out[...])
    logit = nt(total.astype(bf16), w_head[...]).astype(bf16)
    packs = lane_packs(bins, side)
    deep = side // packs
    for h in range(q):
        piece = nn(swap, logit[h * side : (h + 1) * side])
        if packs > 1:
            piece = jnp.concatenate([piece[u * deep : (u + 1) * deep] for u in range(packs)], axis=1)
        halves[h] = piece.astype(bf16)
        mark = targets[:, h * edge : (h + 1) * edge].astype(f32)
        marks[h] = jnp.concatenate([mark, jnp.zeros((edge, width - edge), f32)], axis=1).astype(bf16)
    for p in range(q):
        sends[p] = halves[partner(own, p, q)]


def lend_kernel(q, pair, marks, *lent):
    own = lax.rem(lax.axis_index("row"), q)
    side = pair.shape[1]
    for p in range(1, q):
        first, second = lent[2 * p - 2 : 2 * p]
        block = pair[partner(own, p, q)]
        first[...] = block[: side // 2]
        second[: side // 2] = block[side // 2 :]
        second[side // 2 :] = marks[partner(own, p, q)]


def prepare_kernel(q, p, *refs):
    if p:
        first, second, refs = refs[0], refs[1], refs[2:]
        side = 2 * first.shape[0]
        edge = second.shape[0] - first.shape[0]
        flat = jnp.concatenate([first[...], second[: side // 2]], axis=0)
        mark = second[side // 2 :]
    else:
        own = lax.rem(lax.axis_index("row"), q)
        side, edge = refs[0].shape[1], refs[1].shape[1]
        flat, mark, refs = refs[0][own], refs[1][own], refs[2:]
    w_gate, w_up, w_out, w_head, inputs_t, updated_t, hidden, slope, swish, logits, onehot, normed, scale = refs
    width, bins = flat.shape[1], w_head.shape[0]
    normal, scale_inv = normalize(flat)
    normed[...] = normal
    scale[...] = jnp.broadcast_to(scale_inv, normal.shape)
    inputs = normal.astype(bf16)
    inputs_t[...] = inputs.T
    total = flat.astype(f32)
    for at, step in chunks_of(w_gate.shape[1], 256):
        span = slice(at, at + step)
        gate = nn(inputs, w_gate[:, span])
        upper = nn(inputs, w_up[:, span])
        sigma = sigmoid(gate)
        swished = gate * sigma
        hidden_part = (swished * upper).astype(bf16)
        swish[:, span] = swished
        hidden[:, span] = hidden_part
        slope[:, span] = upper * sigma * (1.0 + gate * (1.0 - sigma))
        total = total + nn(hidden_part, w_out[span, :])
    upd = total.astype(bf16)
    updated_t[...] = upd.T
    logits[...] = nt(upd, w_head[...]).astype(bf16)
    shift = edge.bit_length() - 1
    rows = lax.broadcasted_iota(jnp.int32, (side, edge), 0) >> shift
    pick = jnp.where(rows == lax.broadcasted_iota(jnp.int32, (side, edge), 1), 1.0, 0.0).astype(bf16)
    columns = lax.broadcasted_iota(jnp.int32, (side, width), 0) & (edge - 1)
    mask = columns == lax.broadcasted_iota(jnp.int32, (side, width), 1)
    lanes = lax.broadcasted_iota(jnp.int32, (side, bins), 1).astype(f32)
    picked = jnp.where(mask, nn(pick, mark), 0.0).astype(bf16)
    wanted = nn(picked, jnp.ones((width, bins), bf16))
    onehot[...] = jnp.where(wanted == lanes, 1.0, 0.0)


def backward_kernel(q, packed, *refs):
    blocks, (w_out, w_head, far, near), rest = [refs[7 * p : 7 * p + 7] for p in range(q)], refs[7 * q : 7 * q + 4], refs[7 * q + 4 :]
    (d_updated, d_gate, d_up), hot, mirrored = rest[:3], rest[3:-1], rest[-1]
    (width, side), units, bins = blocks[0][0].shape, w_out.shape[0], w_head.shape[0]
    packs = lane_packs(bins, side)
    own = lax.rem(lax.axis_index("row"), q)
    inside = lax.axis_index("row") // q == lax.axis_index("col")

    @pl.when(inside)
    def _():
        mirrored[...] = near[...]

    @pl.when(jnp.logical_not(inside))
    def _():
        mirrored[...] = far[...]

    inputs_t, updated_t, hidden, slope, swish, logits, onehot = zip(*blocks)
    mirror = jnp.concatenate([mirrored[p, :, u * bins : (u + 1) * bins] for p in range(q) for u in range(packs)], axis=0)
    summed = joined(logits, 0).astype(f32) + mirror.astype(f32)
    powers = jnp.exp(summed - jnp.max(summed, axis=-1, keepdims=True))
    probs = powers / jnp.sum(powers, axis=-1, keepdims=True)
    grad_sym = (probs - joined(onehot, 0)).astype(bf16)
    cotangent = (grad_sym.astype(f32) * 2.0).astype(bf16)
    d_upd = nn(cotangent, w_head[...])
    d_updated[...] = d_upd
    d_upd_b = d_upd.astype(bf16)
    for p in range(q):
        for top, tall in chunks_of(side, 128):
            row = slice(p * side + top, p * side + top + tall)
            for at, step in chunks_of(units, 256):
                span = slice(at, at + step)
                d_hidden = nt(d_upd_b[row], w_out[span, :])
                d_gate[row, span] = (d_hidden * slope[p][top : top + tall, span]).astype(bf16)
                d_up[row, span] = (d_hidden * swish[p][top : top + tall, span]).astype(bf16)
    depth = joined(inputs_t, 1)
    totals = (
        nn(depth, d_gate[...]),
        nn(depth, d_up[...]),
        nn(d_upd_b.T, joined(hidden, 0)),
        nn(joined(updated_t, 1), cotangent),
    )
    if not packed:
        for ref, term in zip(hot, totals):
            ref[...] = term.astype(ref.dtype)
        return
    gate_term, up_term, out_term, head_term = totals
    hot, slots = hot[:-1], hot[-1]
    nrow, ncol = packed
    groups = nrow // q
    lanes, part, tall = units // ncol, width // nrow, units // nrow
    deep = width // q
    for k in range(q):
        for a in range(groups):
            r = a * q + k
            at = 0
            for term in (gate_term, up_term):
                for c in range(ncol):
                    block = term[r * part : (r + 1) * part, c * lanes : (c + 1) * lanes]
                    slots[k, a, at : at + part] = block.astype(bf16)
                    at += part
            pieces = [out_term[u * deep : (u + 1) * deep, r * tall : (r + 1) * tall] for u in range(q)]
            slots[k, a, at : at + deep] = jnp.concatenate(pieces, axis=1).astype(bf16)
            at += deep
            block = head_term[r * part : (r + 1) * part, :]
            block = jnp.concatenate([block, jnp.zeros((part, lanes - bins), f32)], axis=1)
            slots[k, a, at : at + part] = block.astype(bf16)
    for n in range(q):
        hot[n][...] = slots[partner(own, n, q)]


def input_kernel(p, d_updated, d_gate, d_up, normed, scale, w_gate, w_up, result):
    side = result.shape[0]
    row = slice(p * side, (p + 1) * side)
    d_inputs = nt(d_gate[row], w_gate[...]) + nt(d_up[row], w_up[...])
    normal = normed[...]
    d_norm = (
        d_inputs
        - jnp.mean(d_inputs, axis=-1, keepdims=True)
        - normal * jnp.mean(d_inputs * normal, axis=-1, keepdims=True)
    ) * scale[...]
    result[...] = (d_updated[row] + d_norm).astype(bf16)


def place_kernel(q, *refs):
    blocks, d_pair = refs[:-1], refs[-1]
    edge, _, _, width = d_pair.shape
    own = lax.rem(lax.axis_index("row"), q)
    d_pair[:, own] = blocks[0][...].reshape(edge, edge, width)
    for p in range(1, q):
        for n, half in enumerate((slice(0, edge // 2), slice(edge // 2, edge))):
            d_pair[half, partner(own, p, q)] = blocks[2 * p - 1 + n][...].reshape(edge // 2, edge, width)


def core_sum_kernel(q, groups, *rest):
    terms, blocks, hot, handed = rest[:q], rest[q : 2 * q - 1], rest[2 * q - 1 : 2 - 2 * q], rest[2 - 2 * q :]
    mine = lax.axis_index("row") // q
    for p in range(groups):
        a = following(mine, p, groups)
        total = terms[0][a].astype(f32)
        for term in terms[1:]:
            total = total + term[a].astype(f32)
        hot[p][...] = total.astype(bf16)
    for p, block in enumerate(blocks):
        half = block.shape[0] // 2
        handed[2 * p][...] = block[:half]
        handed[2 * p + 1][...] = block[half:]


def chip_sum_kernel(q, groups, ncol, shapes, *rest):
    terms, hot, slots = rest[:groups], rest[groups:-1], rest[-1]
    part, lanes, deep, tall, few = shapes
    total = terms[0][...].astype(f32)
    for term in terms[1:]:
        total = total + term[...].astype(f32)
    at = 2 * ncol * part
    out = total[at : at + deep]
    head = total[at + deep : at + deep + part]
    narrow = deep * q // ncol
    fold = lanes // tall
    short = narrow // fold
    for c in range(ncol):
        slots[c, 0:part] = total[c * part : (c + 1) * part].astype(bf16)
        slots[c, part : 2 * part] = total[(ncol + c) * part : (ncol + c + 1) * part].astype(bf16)
        u, top = (c * narrow) // deep, (c * narrow) % deep
        block = out[top : top + narrow, u * tall : (u + 1) * tall]
        block = jnp.concatenate([block[v * short : (v + 1) * short] for v in range(fold)], axis=1)
        slots[c, 2 * part : 2 * part + short] = block.astype(bf16)
        piece = jnp.concatenate([head[:, c * few : (c + 1) * few], jnp.zeros((part, lanes - few), f32)], axis=1)
        slots[c, 2 * part + short : 3 * part + short] = piece.astype(bf16)
    for p in range(ncol):
        hot[p][...] = slots[partner(lax.axis_index("col"), p, ncol)]


def col_sum_kernel(shapes, factor, *rest):
    terms, (gate, up, out, head) = rest[:-4], rest[-4:]
    part, lanes, tall, few = shapes
    total = terms[0][...].astype(f32)
    for term in terms[1:]:
        total = total + term[...].astype(f32)
    total = total * factor
    fold = lanes // tall
    short = out.shape[0] // fold
    gate[...] = total[0:part]
    up[...] = total[part : 2 * part]
    for v in range(fold):
        out[v * short : (v + 1) * short, :] = total[2 * part : 2 * part + short, v * tall : (v + 1) * tall]
    head[...] = total[2 * part + short : 3 * part + short, 0:few]


def core_pairs(nrow, q, p):
    return [(s, s - s % q + partner(s % q, p, q)) for s in range(nrow)]


def shaped(shape, kind):
    return jax.ShapeDtypeStruct(shape, kind)


def cost(flops, moved):
    return pl.CostEstimate(flops=flops, bytes_accessed=moved, transcendentals=0)


def body(pair, targets, w_gate, w_up, w_out, w_head):
    rows, cols, width = pair.shape
    units = w_gate.shape[1]
    bins = w_head.shape[1]
    nrow, ncol = lax.axis_size("row"), lax.axis_size("col")
    q = nrow // ncol
    groups = nrow // q
    side = rows * cols // q
    packs = lane_packs(bins, side)
    head_t = w_head.T
    piece = (side // packs, bins * packs)

    sources = (pair, w_gate, w_up, w_out, head_t, targets)
    pair, w_gate, w_up, w_out, head_t, marks, sends = pl.pallas_call(
        functools.partial(forward_kernel, q),
        out_shape=[shaped((q, side, width), bf16)]
        + [shaped(x.shape, bf16) for x in sources[1:5]]
        + [shaped((q, rows, width), bf16), shaped((q, *piece), bf16)],
        in_specs=[HBM] * 6,
        out_specs=[VMEM] * 7,
        scratch_shapes=[
            pltpu.VMEM((rows, cols), jnp.int32),
            pltpu.VMEM((q, *piece), bf16),
            pltpu.VMEM((q * side, units), bf16),
            pltpu.SemaphoreType.DMA((5 + q,)),
        ],
        compiler_params=PARAMS,
        name="forward",
    )(*(pltpu.with_memory_space_constraint(x, pltpu.HBM) for x in sources))

    pairs = [
        (r * ncol + c, (q * c + (partner(r % q, 1, q) if q == 2 and r // q == c else r % q)) * ncol + r // q)
        for r in range(nrow)
        for c in range(ncol)
    ]
    far = lax.ppermute(sends, ("row", "col"), pairs)
    lent = pl.pallas_call(
        functools.partial(lend_kernel, q),
        out_shape=[shaped((side // 2, width), bf16), shaped((side // 2 + rows, width), bf16)] * (q - 1),
        in_specs=[VMEM] * 2,
        out_specs=[VMEM] * (2 * q - 2),
        compiler_params=PARAMS,
        name="lend",
    )(pair, marks)
    borrowed = [lax.ppermute(x, "row", core_pairs(nrow, q, n // 2 + 1)) for n, x in enumerate(lent)]
    prepared = []
    for p in range(q):
        source = borrowed[2 * p - 2 : 2 * p] if p else (pair, marks)
        prepared.append(
            pl.pallas_call(
                functools.partial(prepare_kernel, q, p),
                out_shape=[
                    shaped((width, side), bf16),
                    shaped((width, side), bf16),
                    shaped((side, units), bf16),
                    shaped((side, units), f32),
                    shaped((side, units), f32),
                    shaped((side, bins), bf16),
                    shaped((side, bins), f32),
                    shaped((side, width), f32),
                    shaped((side, width), f32),
                ],
                in_specs=[VMEM] * (len(source) + 4),
                out_specs=[VMEM] * 9,
                compiler_params=PARAMS,
                cost_estimate=cost(0, 0) if p else cost(6 * side * width * units, 8 * side * units),
                name="prepare",
            )(*source, w_gate, w_up, w_out, head_t)
        )

    part, tall, few = width // nrow, units // nrow, bins // ncol
    lanes, deep = units // ncol, width // q
    fits = (
        part % 16 == 0 and lanes == 128 and tall * q == lanes and bins <= lanes and deep % (width // ncol) == 0
        and (width // ncol * tall // lanes) % 16 == 0
    )
    height = 2 * ncol * part + deep + part
    if fits:
        hot_shapes = [shaped((groups, height, lanes), bf16)] * q
        scratch = [pltpu.VMEM((q, groups, height, lanes), bf16)]
    else:
        hot_shapes = [shaped((width, n), bf16) for n in (units, units, units, bins)]
        scratch = []
    results = pl.pallas_call(
        functools.partial(backward_kernel, q, (nrow, ncol) if fits else None),
        out_shape=[shaped((q * side, width), f32)] + [shaped((q * side, units), bf16)] * 2 + hot_shapes,
        in_specs=[VMEM] * (7 * q + 4),
        out_specs=[VMEM] * (3 + len(hot_shapes)),
        scratch_shapes=scratch + [pltpu.VMEM((q, *piece), bf16)],
        compiler_params=PARAMS,
        cost_estimate=cost(8 * q * side * width * units, 4 * q * side * units),
        name="backward",
    )(*(x for block in prepared for x in block[:7]), w_out, head_t, far, sends)
    hot = list(results[3:])

    def d_inputs(p):
        return pl.pallas_call(
            functools.partial(input_kernel, p),
            out_shape=shaped((side, width), bf16),
            in_specs=[VMEM] * 7,
            out_specs=VMEM,
            compiler_params=PARAMS,
            cost_estimate=cost(4 * side * width * units, 4 * side * units),
            name="d_inputs",
        )(*results[:3], *prepared[p][7:], w_gate, w_up)

    d_blocks = [d_inputs(p) for p in range(q)]

    def returned(blocks):
        moved = [lax.ppermute(x, "row", core_pairs(nrow, q, n // 2 + 1)) for n, x in enumerate(blocks[1:])]
        return blocks[:1] + moved

    def placed(blocks):
        return pl.pallas_call(
            functools.partial(place_kernel, q),
            out_shape=shaped((rows, q, cols // q, width), bf16),
            in_specs=[VMEM] * (2 * q - 1),
            out_specs=VMEM,
            compiler_params=PARAMS,
            name="place",
        )(*blocks).reshape(rows, cols, width)

    factor = 1.0 / (rows * nrow)
    if not fits:
        owned = []
        hot[2] = hot[2].T
        for term in hot:
            mine = lax.psum_scatter(term, "row", scatter_dimension=0, tiled=True).astype(f32)
            owned.append(lax.psum_scatter(mine, "col", scatter_dimension=1, tiled=True) * factor)
        d_blocks = d_blocks[:1] + [half for block in d_blocks[1:] for half in (block[: side // 2], block[side // 2 :])]
        return (placed(returned(d_blocks)), *owned)

    terms = [hot[0]]
    for p in range(1, q):
        terms.append(lax.ppermute(hot[p], "row", core_pairs(nrow, q, p)))
    terms, d_blocks = lax.optimization_barrier((terms, d_blocks))
    hot = pl.pallas_call(
        functools.partial(core_sum_kernel, q, groups),
        out_shape=[shaped((height, lanes), bf16)] * groups + [shaped((side // 2, width), bf16)] * (2 * q - 2),
        in_specs=[VMEM] * (2 * q - 1),
        out_specs=[VMEM] * (groups + 2 * q - 2),
        compiler_params=PARAMS,
        name="core_sum",
    )(*terms, *d_blocks[1:])
    hot, d_blocks = hot[:groups], d_blocks[:1] + list(hot[groups:])
    terms = [hot[0]]
    for p in range(1, groups):
        terms.append(lax.ppermute(hot[p], "row", [(s, following(s // q, p, groups) * q + s % q) for s in range(nrow)]))
    terms, d_blocks = lax.optimization_barrier((terms, returned(d_blocks)))
    short = 3 * part + width // ncol * tall // lanes
    hot = pl.pallas_call(
        functools.partial(chip_sum_kernel, q, groups, ncol, (part, lanes, deep, tall, few)),
        out_shape=[shaped((short, lanes), bf16)] * ncol,
        in_specs=[VMEM] * groups,
        out_specs=[VMEM] * ncol,
        scratch_shapes=[pltpu.VMEM((ncol, short, lanes), bf16)],
        compiler_params=PARAMS,
        name="chip_sum",
    )(*terms)
    terms = [hot[0]]
    for p in sorted(range(1, ncol), key=lambda p: (p != ncol // 2, -p)):
        terms.append(lax.ppermute(hot[p], "col", [(s, partner(s, p, ncol)) for s in range(ncol)]))
    *terms, d_pair = lax.optimization_barrier((*terms, placed(d_blocks)))
    gate, up, out, head = pl.pallas_call(
        functools.partial(col_sum_kernel, (part, lanes, tall, few), factor),
        out_shape=[
            shaped((part, lanes), f32),
            shaped((part, lanes), f32),
            shaped((width // ncol, tall), f32),
            shaped((part, few), f32),
        ],
        in_specs=[VMEM] * ncol,
        out_specs=[VMEM] * 4,
        compiler_params=PARAMS,
        name="col_sum",
    )(*terms)
    return d_pair, gate, up, out.T, head


def solution(mesh):
    placed = (P("row", "col", None), P("row", "col"), P(), P(), P(), P())
    return jax.shard_map(
        body,
        mesh=mesh,
        in_specs=placed,
        out_specs=(P("row", "col", None), P("row", "col"), P("row", "col"), P("row", "col"), P("row", "col")),
        check_vma=False,
    )
```

```python
import functools

import jax
import jax.numpy as jnp
from jax import lax
from jax.experimental import pallas as pl
from jax.experimental.pallas import tpu as pltpu
from jax.sharding import PartitionSpec as P

eps = 1e-05
f32 = jnp.float32
bf16 = jnp.bfloat16
HBM = pl.BlockSpec(memory_space=pltpu.HBM)
VMEM = pl.BlockSpec(memory_space=pltpu.VMEM)
PARAMS = pltpu.CompilerParams(vmem_limit_bytes=24 * 1024 * 1024)


def nn(a, b):
    return lax.dot_general(a, b, (((1,), (0,)), ((), ())), preferred_element_type=f32)


def nt(a, b):
    return lax.dot_general(a, b, (((1,), (1,)), ((), ())), preferred_element_type=f32)


def tn(a, b):
    return lax.dot_general(a, b, (((0,), (0,)), ((), ())), preferred_element_type=f32)


def normalize(flat):
    values = flat.astype(f32)
    centre = values - jnp.mean(values, axis=-1, keepdims=True)
    scale_inv = lax.rsqrt(jnp.mean(centre * centre, axis=-1, keepdims=True) + eps)
    return centre * scale_inv, scale_inv


def sigmoid(v):
    return 0.5 * jnp.tanh(0.5 * v) + 0.5


def chunks_of(size, most):
    step = most if size % most == 0 else size
    return [(at, step) for at in range(0, size, step)]


def partner(s, p, n):
    if n & (n - 1) == 0:
        return s ^ p
    return (s + p) % n if isinstance(s, int) else lax.rem(s + p, n)


def crossed(k, q):
    return partner(k, 1, q) if q > 1 else k


def following(s, p, n):
    return (s + p) % n if isinstance(s, int) else lax.rem(s + p, n)


def joined(refs, axis):
    return jnp.concatenate([ref[...] for ref in refs], axis=axis)


def lane_packs(bins, side):
    packs = max(1, 128 // bins)
    return packs if (side // packs) % 16 == 0 else 1


def forward_kernel(q, *refs):
    sources, (pair, w_gate, w_up, w_out, w_head, marks, sends), scratch = refs[:6], refs[6:13], refs[13:]
    targets, halves, hidden, sems = scratch
    _, side, width = pair.shape
    edge = sources[0].shape[0]
    bins = w_head.shape[0]
    copies = [
        pltpu.make_async_copy(source, target, sems.at[i])
        for i, (source, target) in enumerate(zip(sources[1:], (w_gate, w_up, w_out, w_head, targets)))
    ]
    pieces = [
        pltpu.make_async_copy(
            sources[0].at[:, h * edge : (h + 1) * edge, :], pair.reshape(q, edge, edge, width).at[h], sems.at[5 + h]
        )
        for h in range(q)
    ]
    for copy in pieces + copies:
        copy.start()
    shift = edge.bit_length() - 1
    out_row = lax.broadcasted_iota(jnp.int32, (side, side), 0)
    in_row = lax.broadcasted_iota(jnp.int32, (side, side), 1)
    wanted = ((out_row & (edge - 1)) << shift) | (out_row >> shift)
    swap = jnp.where(in_row == wanted, 1.0, 0.0).astype(bf16)
    own = lax.rem(lax.axis_index("row"), q)
    for copy in pieces:
        copy.wait()
    flat = pair[...].reshape(q * side, width)
    inputs = normalize(flat)[0].astype(bf16)
    for copy in copies[:2]:
        copy.wait()
    for top, tall in chunks_of(q * side, 128):
        for at, step in chunks_of(w_gate.shape[1], 256):
            gate = nn(inputs[top : top + tall], w_gate[:, at : at + step])
            upper = nn(inputs[top : top + tall], w_up[:, at : at + step])
            hidden[top : top + tall, at : at + step] = (gate * sigmoid(gate) * upper).astype(bf16)
    for copy in copies[2:]:
        copy.wait()
    total = flat.astype(f32) + nn(hidden[...], w_out[...])
    logit = nt(total.astype(bf16), w_head[...]).astype(bf16)
    packs = lane_packs(bins, side)
    deep = side // packs
    for h in range(q):
        piece = nn(swap, logit[h * side : (h + 1) * side])
        if packs > 1:
            piece = jnp.concatenate([piece[u * deep : (u + 1) * deep] for u in range(packs)], axis=1)
        halves[h] = piece.astype(bf16)
        mark = targets[:, h * edge : (h + 1) * edge].astype(f32)
        marks[h] = jnp.concatenate([mark, jnp.zeros((edge, width - edge), f32)], axis=1).astype(bf16)
    for p in range(q):
        sends[p] = halves[partner(crossed(own, q), p, q)]


def lend_kernel(q, pair, marks, *lent):
    own = lax.rem(lax.axis_index("row"), q)
    side = pair.shape[1]
    for p in range(1, q):
        first, second = lent[2 * p - 2 : 2 * p]
        lent_half = crossed(partner(own, p, q), q)
        block = pair[lent_half]
        first[...] = block[: side // 2]
        second[: side // 2] = block[side // 2 :]
        second[side // 2 :] = marks[lent_half]


def prepare_kernel(q, p, *refs):
    if p:
        first, second, refs = refs[0], refs[1], refs[2:]
        side = 2 * first.shape[0]
        edge = second.shape[0] - first.shape[0]
        flat = jnp.concatenate([first[...], second[: side // 2]], axis=0)
        mark = second[side // 2 :]
    else:
        own = lax.rem(lax.axis_index("row"), q)
        side, edge = refs[0].shape[1], refs[1].shape[1]
        own = crossed(own, q)
        flat, mark, refs = refs[0][own], refs[1][own], refs[2:]
    w_gate, w_up, w_out, w_head, inputs_t, updated_t, hidden, slope, swish, logits, onehot, normed, scale = refs
    width, bins = flat.shape[1], w_head.shape[0]
    normal, scale_inv = normalize(flat)
    normed[...] = normal
    scale[...] = jnp.broadcast_to(scale_inv, normal.shape)
    inputs = normal.astype(bf16)
    inputs_t[...] = inputs.T
    total = flat.astype(f32)
    for at, step in chunks_of(w_gate.shape[1], 256):
        span = slice(at, at + step)
        gate = nn(inputs, w_gate[:, span])
        upper = nn(inputs, w_up[:, span])
        sigma = sigmoid(gate)
        swished = gate * sigma
        hidden_part = (swished * upper).astype(bf16)
        swish[:, span] = swished
        hidden[:, span] = hidden_part
        slope[:, span] = upper * sigma * (1.0 + gate * (1.0 - sigma))
        total = total + nn(hidden_part, w_out[span, :])
    upd = total.astype(bf16)
    updated_t[...] = upd.T
    logits[...] = nt(upd, w_head[...]).astype(bf16)
    shift = edge.bit_length() - 1
    rows = lax.broadcasted_iota(jnp.int32, (side, edge), 0) >> shift
    pick = jnp.where(rows == lax.broadcasted_iota(jnp.int32, (side, edge), 1), 1.0, 0.0).astype(bf16)
    columns = lax.broadcasted_iota(jnp.int32, (side, width), 0) & (edge - 1)
    mask = columns == lax.broadcasted_iota(jnp.int32, (side, width), 1)
    lanes = lax.broadcasted_iota(jnp.int32, (side, bins), 1).astype(f32)
    picked = jnp.where(mask, nn(pick, mark), 0.0).astype(bf16)
    wanted = nn(picked, jnp.ones((width, bins), bf16))
    onehot[...] = jnp.where(wanted == lanes, 1.0, 0.0)


def backward_kernel(q, packed, *refs):
    blocks, (w_out, w_head, far), rest = [refs[7 * p : 7 * p + 7] for p in range(q)], refs[7 * q : 7 * q + 3], refs[7 * q + 3 :]
    (d_updated, d_gate, d_up), hot = rest[:3], rest[3:]
    (width, side), units, bins = blocks[0][0].shape, w_out.shape[0], w_head.shape[0]
    packs = lane_packs(bins, side)
    own = lax.rem(lax.axis_index("row"), q)
    inputs_t, updated_t, hidden, slope, swish, logits, onehot = zip(*blocks)
    mirror = jnp.concatenate([far[p, :, u * bins : (u + 1) * bins] for p in range(q) for u in range(packs)], axis=0)
    summed = joined(logits, 0).astype(f32) + mirror.astype(f32)
    powers = jnp.exp(summed - jnp.max(summed, axis=-1, keepdims=True))
    probs = powers / jnp.sum(powers, axis=-1, keepdims=True)
    grad_sym = (probs - joined(onehot, 0)).astype(bf16)
    cotangent = (grad_sym.astype(f32) * 2.0).astype(bf16)
    d_upd = nn(cotangent, w_head[...])
    d_updated[...] = d_upd
    d_upd_b = d_upd.astype(bf16)
    for p in range(q):
        for top, tall in chunks_of(side, 128):
            row = slice(p * side + top, p * side + top + tall)
            for at, step in chunks_of(units, 256):
                span = slice(at, at + step)
                d_hidden = nt(d_upd_b[row], w_out[span, :])
                d_gate[row, span] = (d_hidden * slope[p][top : top + tall, span]).astype(bf16)
                d_up[row, span] = (d_hidden * swish[p][top : top + tall, span]).astype(bf16)
    depth = joined(inputs_t, 1)
    totals = (
        nn(depth, d_gate[...]),
        nn(depth, d_up[...]),
        nn(d_upd_b.T, joined(hidden, 0)),
        nn(joined(updated_t, 1), cotangent),
    )
    if not packed:
        for ref, term in zip(hot, totals):
            ref[...] = term.astype(ref.dtype)
        return
    gate_term, up_term, out_term, head_term = totals
    hot, slots = hot[:-1], hot[-1]
    nrow, ncol = packed
    groups = nrow // q
    lanes, part, tall = units // ncol, width // nrow, units // nrow
    deep = width // q
    for k in range(q):
        for a in range(groups):
            r = a * q + k
            at = 0
            for term in (gate_term, up_term):
                for c in range(ncol):
                    block = term[r * part : (r + 1) * part, c * lanes : (c + 1) * lanes]
                    slots[k, a, at : at + part] = block.astype(bf16)
                    at += part
            pieces = [out_term[u * deep : (u + 1) * deep, r * tall : (r + 1) * tall] for u in range(q)]
            slots[k, a, at : at + deep] = jnp.concatenate(pieces, axis=1).astype(bf16)
            at += deep
            block = head_term[r * part : (r + 1) * part, :]
            block = jnp.concatenate([block, jnp.zeros((part, lanes - bins), f32)], axis=1)
            slots[k, a, at : at + part] = block.astype(bf16)
    mine = lax.axis_index("row") // q
    for n in range(q):
        core = partner(own, n, q)
        for a in range(groups):
            hot[n][a] = slots[jnp.where(mine == a, core, crossed(core, q)), a]


def input_kernel(p, d_updated, d_gate, d_up, normed, scale, w_gate, w_up, result):
    side = result.shape[0]
    row = slice(p * side, (p + 1) * side)
    d_inputs = nt(d_gate[row], w_gate[...]) + nt(d_up[row], w_up[...])
    normal = normed[...]
    d_norm = (
        d_inputs
        - jnp.mean(d_inputs, axis=-1, keepdims=True)
        - normal * jnp.mean(d_inputs * normal, axis=-1, keepdims=True)
    ) * scale[...]
    result[...] = (d_updated[row] + d_norm).astype(bf16)


def place_kernel(q, *refs):
    blocks, d_pair = refs[:-1], refs[-1]
    edge, _, _, width = d_pair.shape
    own = lax.rem(lax.axis_index("row"), q)
    d_pair[:, crossed(own, q)] = blocks[0][...].reshape(edge, edge, width)
    for p in range(1, q):
        for n, half in enumerate((slice(0, edge // 2), slice(edge // 2, edge))):
            d_pair[half, crossed(partner(own, p, q), q)] = blocks[2 * p - 1 + n][...].reshape(edge // 2, edge, width)


def core_sum_kernel(q, groups, *rest):
    terms, blocks, hot, handed = rest[:q], rest[q : 2 * q - 1], rest[2 * q - 1 : 2 - 2 * q], rest[2 - 2 * q :]
    mine = lax.axis_index("row") // q
    for p in range(groups):
        a = following(mine, p, groups)
        total = terms[0][a].astype(f32)
        for term in terms[1:]:
            total = total + term[a].astype(f32)
        hot[p][...] = total.astype(bf16)
    for p, block in enumerate(blocks):
        half = block.shape[0] // 2
        handed[2 * p][...] = block[:half]
        handed[2 * p + 1][...] = block[half:]


def chip_sum_kernel(q, groups, ncol, shapes, *rest):
    terms, hot, slots = rest[:groups], rest[groups:-1], rest[-1]
    part, lanes, deep, tall, few = shapes
    total = terms[0][...].astype(f32)
    for term in terms[1:]:
        total = total + term[...].astype(f32)
    at = 2 * ncol * part
    out = total[at : at + deep]
    head = total[at + deep : at + deep + part]
    narrow = deep * q // ncol
    fold = lanes // tall
    short = narrow // fold
    for c in range(ncol):
        slots[c, 0:part] = total[c * part : (c + 1) * part].astype(bf16)
        slots[c, part : 2 * part] = total[(ncol + c) * part : (ncol + c + 1) * part].astype(bf16)
        u, top = (c * narrow) // deep, (c * narrow) % deep
        block = out[top : top + narrow, u * tall : (u + 1) * tall]
        block = jnp.concatenate([block[v * short : (v + 1) * short] for v in range(fold)], axis=1)
        slots[c, 2 * part : 2 * part + short] = block.astype(bf16)
        piece = jnp.concatenate([head[:, c * few : (c + 1) * few], jnp.zeros((part, lanes - few), f32)], axis=1)
        slots[c, 2 * part + short : 3 * part + short] = piece.astype(bf16)
    for p in range(ncol):
        hot[p][...] = slots[partner(lax.axis_index("col"), p, ncol)]


def col_sum_kernel(shapes, factor, *rest):
    terms, (gate, up, out, head) = rest[:-4], rest[-4:]
    part, lanes, tall, few = shapes
    total = terms[0][...].astype(f32)
    for term in terms[1:]:
        total = total + term[...].astype(f32)
    total = total * factor
    fold = lanes // tall
    short = out.shape[0] // fold
    gate[...] = total[0:part]
    up[...] = total[part : 2 * part]
    for v in range(fold):
        out[v * short : (v + 1) * short, :] = total[2 * part : 2 * part + short, v * tall : (v + 1) * tall]
    head[...] = total[2 * part + short : 3 * part + short, 0:few]


def core_pairs(nrow, q, p):
    return [(s, s - s % q + partner(s % q, p, q)) for s in range(nrow)]


def shaped(shape, kind):
    return jax.ShapeDtypeStruct(shape, kind)


def cost(flops, moved):
    return pl.CostEstimate(flops=flops, bytes_accessed=moved, transcendentals=0)


def body(pair, targets, w_gate, w_up, w_out, w_head):
    rows, cols, width = pair.shape
    units = w_gate.shape[1]
    bins = w_head.shape[1]
    nrow, ncol = lax.axis_size("row"), lax.axis_size("col")
    q = nrow // ncol
    groups = nrow // q
    side = rows * cols // q
    packs = lane_packs(bins, side)
    head_t = w_head.T
    piece = (side // packs, bins * packs)

    sources = (pair, w_gate, w_up, w_out, head_t, targets)
    pair, w_gate, w_up, w_out, head_t, marks, sends = pl.pallas_call(
        functools.partial(forward_kernel, q),
        out_shape=[shaped((q, side, width), bf16)]
        + [shaped(x.shape, bf16) for x in sources[1:5]]
        + [shaped((q, rows, width), bf16), shaped((q, *piece), bf16)],
        in_specs=[HBM] * 6,
        out_specs=[VMEM] * 7,
        scratch_shapes=[
            pltpu.VMEM((rows, cols), jnp.int32),
            pltpu.VMEM((q, *piece), bf16),
            pltpu.VMEM((q * side, units), bf16),
            pltpu.SemaphoreType.DMA((5 + q,)),
        ],
        compiler_params=PARAMS,
        name="forward",
    )(*(pltpu.with_memory_space_constraint(x, pltpu.HBM) for x in sources))

    pairs = [
        (r * ncol + c, (q * c + crossed(r % q, q)) * ncol + r // q) for r in range(nrow) for c in range(ncol)
    ]
    far = lax.ppermute(sends, ("row", "col"), pairs)
    lent = pl.pallas_call(
        functools.partial(lend_kernel, q),
        out_shape=[shaped((side // 2, width), bf16), shaped((side // 2 + rows, width), bf16)] * (q - 1),
        in_specs=[VMEM] * 2,
        out_specs=[VMEM] * (2 * q - 2),
        compiler_params=PARAMS,
        name="lend",
    )(pair, marks)
    borrowed = [lax.ppermute(x, "row", core_pairs(nrow, q, n // 2 + 1)) for n, x in enumerate(lent)]
    prepared = []
    for p in range(q):
        source = borrowed[2 * p - 2 : 2 * p] if p else (pair, marks)
        prepared.append(
            pl.pallas_call(
                functools.partial(prepare_kernel, q, p),
                out_shape=[
                    shaped((width, side), bf16),
                    shaped((width, side), bf16),
                    shaped((side, units), bf16),
                    shaped((side, units), f32),
                    shaped((side, units), f32),
                    shaped((side, bins), bf16),
                    shaped((side, bins), f32),
                    shaped((side, width), f32),
                    shaped((side, width), f32),
                ],
                in_specs=[VMEM] * (len(source) + 4),
                out_specs=[VMEM] * 9,
                compiler_params=PARAMS,
                cost_estimate=cost(0, 0) if p else cost(6 * side * width * units, 8 * side * units),
                name="prepare",
            )(*source, w_gate, w_up, w_out, head_t)
        )

    part, tall, few = width // nrow, units // nrow, bins // ncol
    lanes, deep = units // ncol, width // q
    fits = (
        part % 16 == 0 and lanes == 128 and tall * q == lanes and bins <= lanes and deep % (width // ncol) == 0
        and (width // ncol * tall // lanes) % 16 == 0
    )
    height = 2 * ncol * part + deep + part
    if fits:
        hot_shapes = [shaped((groups, height, lanes), bf16)] * q
        scratch = [pltpu.VMEM((q, groups, height, lanes), bf16)]
    else:
        hot_shapes = [shaped((width, n), bf16) for n in (units, units, units, bins)]
        scratch = []
    results = pl.pallas_call(
        functools.partial(backward_kernel, q, (nrow, ncol) if fits else None),
        out_shape=[shaped((q * side, width), f32)] + [shaped((q * side, units), bf16)] * 2 + hot_shapes,
        in_specs=[VMEM] * (7 * q + 3),
        out_specs=[VMEM] * (3 + len(hot_shapes)),
        scratch_shapes=scratch,
        compiler_params=PARAMS,
        cost_estimate=cost(8 * q * side * width * units, 4 * q * side * units),
        name="backward",
    )(*(x for block in prepared for x in block[:7]), w_out, head_t, far)
    hot = list(results[3:])

    def d_inputs(p):
        return pl.pallas_call(
            functools.partial(input_kernel, p),
            out_shape=shaped((side, width), bf16),
            in_specs=[VMEM] * 7,
            out_specs=VMEM,
            compiler_params=PARAMS,
            cost_estimate=cost(4 * side * width * units, 4 * side * units),
            name="d_inputs",
        )(*results[:3], *prepared[p][7:], w_gate, w_up)

    d_blocks = [d_inputs(p) for p in range(q)]

    def returned(blocks):
        moved = [lax.ppermute(x, "row", core_pairs(nrow, q, n // 2 + 1)) for n, x in enumerate(blocks[1:])]
        return blocks[:1] + moved

    def placed(blocks):
        return pl.pallas_call(
            functools.partial(place_kernel, q),
            out_shape=shaped((rows, q, cols // q, width), bf16),
            in_specs=[VMEM] * (2 * q - 1),
            out_specs=VMEM,
            compiler_params=PARAMS,
            name="place",
        )(*blocks).reshape(rows, cols, width)

    factor = 1.0 / (rows * nrow)
    if not fits:
        owned = []
        hot[2] = hot[2].T
        for term in hot:
            mine = lax.psum_scatter(term, "row", scatter_dimension=0, tiled=True).astype(f32)
            owned.append(lax.psum_scatter(mine, "col", scatter_dimension=1, tiled=True) * factor)
        d_blocks = d_blocks[:1] + [half for block in d_blocks[1:] for half in (block[: side // 2], block[side // 2 :])]
        return (placed(returned(d_blocks)), *owned)

    terms = [hot[0]]
    for p in range(1, q):
        terms.append(lax.ppermute(hot[p], "row", core_pairs(nrow, q, p)))
    terms, d_blocks = lax.optimization_barrier((terms, d_blocks))
    hot = pl.pallas_call(
        functools.partial(core_sum_kernel, q, groups),
        out_shape=[shaped((height, lanes), bf16)] * groups + [shaped((side // 2, width), bf16)] * (2 * q - 2),
        in_specs=[VMEM] * (2 * q - 1),
        out_specs=[VMEM] * (groups + 2 * q - 2),
        compiler_params=PARAMS,
        name="core_sum",
    )(*terms, *d_blocks[1:])
    hot, d_blocks = hot[:groups], d_blocks[:1] + list(hot[groups:])
    terms = [hot[0]]
    for p in range(1, groups):
        terms.append(lax.ppermute(hot[p], "row", [(s, following(s // q, p, groups) * q + crossed(s % q, q)) for s in range(nrow)]))
    terms, d_blocks = lax.optimization_barrier((terms, returned(d_blocks)))
    short = 3 * part + width // ncol * tall // lanes
    hot = pl.pallas_call(
        functools.partial(chip_sum_kernel, q, groups, ncol, (part, lanes, deep, tall, few)),
        out_shape=[shaped((short, lanes), bf16)] * ncol,
        in_specs=[VMEM] * groups,
        out_specs=[VMEM] * ncol,
        scratch_shapes=[pltpu.VMEM((ncol, short, lanes), bf16)],
        compiler_params=PARAMS,
        name="chip_sum",
    )(*terms)
    terms = [hot[0]]
    for p in sorted(range(1, ncol), key=lambda p: (p != ncol // 2, -p)):
        terms.append(lax.ppermute(hot[p], "col", [(s, partner(s, p, ncol)) for s in range(ncol)]))
    *terms, d_pair = lax.optimization_barrier((*terms, placed(d_blocks)))
    gate, up, out, head = pl.pallas_call(
        functools.partial(col_sum_kernel, (part, lanes, tall, few), factor),
        out_shape=[
            shaped((part, lanes), f32),
            shaped((part, lanes), f32),
            shaped((width // ncol, tall), f32),
            shaped((part, few), f32),
        ],
        in_specs=[VMEM] * ncol,
        out_specs=[VMEM] * 4,
        compiler_params=PARAMS,
        name="col_sum",
    )(*terms)
    return d_pair, gate, up, out.T, head


def solution(mesh):
    placed = (P("row", "col", None), P("row", "col"), P(), P(), P(), P())
    return jax.shard_map(
        body,
        mesh=mesh,
        in_specs=placed,
        out_specs=(P("row", "col", None), P("row", "col"), P("row", "col"), P("row", "col"), P("row", "col")),
        check_vma=False,
    )
```

```python
import functools

import jax
import jax.numpy as jnp
from jax import lax
from jax.experimental import pallas as pl
from jax.experimental.pallas import tpu as pltpu
from jax.sharding import PartitionSpec as P

eps = 1e-05
f32 = jnp.float32
bf16 = jnp.bfloat16
HBM = pl.BlockSpec(memory_space=pltpu.HBM)
VMEM = pl.BlockSpec(memory_space=pltpu.VMEM)
PARAMS = pltpu.CompilerParams(vmem_limit_bytes=24 * 1024 * 1024)


def nn(a, b):
    return lax.dot_general(a, b, (((1,), (0,)), ((), ())), preferred_element_type=f32)


def nt(a, b):
    return lax.dot_general(a, b, (((1,), (1,)), ((), ())), preferred_element_type=f32)


def tn(a, b):
    return lax.dot_general(a, b, (((0,), (0,)), ((), ())), preferred_element_type=f32)


def normalize(flat):
    values = flat.astype(f32)
    centre = values - jnp.mean(values, axis=-1, keepdims=True)
    scale_inv = lax.rsqrt(jnp.mean(centre * centre, axis=-1, keepdims=True) + eps)
    return centre * scale_inv, scale_inv


def sigmoid(v):
    return 0.5 * jnp.tanh(0.5 * v) + 0.5


def chunks_of(size, most):
    step = most if size % most == 0 else size
    return [(at, step) for at in range(0, size, step)]


def partner(s, p, n):
    if n & (n - 1) == 0:
        return s ^ p
    return (s + p) % n if isinstance(s, int) else lax.rem(s + p, n)


def crossed(k, q):
    return partner(k, 1, q) if q > 1 else k


def following(s, p, n):
    return (s + p) % n if isinstance(s, int) else lax.rem(s + p, n)


def joined(refs, axis):
    return jnp.concatenate([ref[...] for ref in refs], axis=axis)


def lane_packs(bins, side):
    packs = max(1, 128 // bins)
    return packs if (side // packs) % 16 == 0 else 1


def forward_kernel(q, *refs):
    sources, (pair, w_gate, w_up, w_out, w_head, marks, sends), scratch = refs[:6], refs[6:13], refs[13:]
    targets, halves, hidden, sems = scratch
    _, side, width = pair.shape
    edge = sources[0].shape[0]
    bins = w_head.shape[0]
    copies = [
        pltpu.make_async_copy(source, target, sems.at[i])
        for i, (source, target) in enumerate(zip(sources[1:], (w_gate, w_up, w_out, w_head, targets)))
    ]
    pieces = [
        pltpu.make_async_copy(
            sources[0].at[:, h * edge : (h + 1) * edge, :], pair.reshape(q, edge, edge, width).at[h], sems.at[5 + h]
        )
        for h in range(q)
    ]
    for copy in pieces + copies:
        copy.start()
    shift = edge.bit_length() - 1
    out_row = lax.broadcasted_iota(jnp.int32, (side, side), 0)
    in_row = lax.broadcasted_iota(jnp.int32, (side, side), 1)
    wanted = ((out_row & (edge - 1)) << shift) | (out_row >> shift)
    swap = jnp.where(in_row == wanted, 1.0, 0.0).astype(bf16)
    own = lax.rem(lax.axis_index("row"), q)
    for copy in pieces:
        copy.wait()
    flat = pair[...].reshape(q * side, width)
    inputs = normalize(flat)[0].astype(bf16)
    for copy in copies[:2]:
        copy.wait()
    for top, tall in chunks_of(q * side, 128):
        for at, step in chunks_of(w_gate.shape[1], 256):
            gate = nn(inputs[top : top + tall], w_gate[:, at : at + step])
            upper = nn(inputs[top : top + tall], w_up[:, at : at + step])
            hidden[top : top + tall, at : at + step] = (gate * sigmoid(gate) * upper).astype(bf16)
    for copy in copies[2:]:
        copy.wait()
    total = flat.astype(f32) + nn(hidden[...], w_out[...])
    logit = nt(total.astype(bf16), w_head[...]).astype(bf16)
    packs = lane_packs(bins, side)
    deep = side // packs
    for h in range(q):
        piece = nn(swap, logit[h * side : (h + 1) * side])
        if packs > 1:
            piece = jnp.concatenate([piece[u * deep : (u + 1) * deep] for u in range(packs)], axis=1)
        halves[h] = piece.astype(bf16)
        mark = targets[:, h * edge : (h + 1) * edge].astype(f32)
        marks[h] = jnp.concatenate([mark, jnp.zeros((edge, width - edge), f32)], axis=1).astype(bf16)
    for p in range(q):
        sends[p] = halves[partner(own, p, q)]


def lend_kernel(q, pair, marks, *lent):
    own = lax.rem(lax.axis_index("row"), q)
    side = pair.shape[1]
    for p in range(1, q):
        first, second = lent[2 * p - 2 : 2 * p]
        block = pair[partner(own, p, q)]
        first[...] = block[: side // 2]
        second[: side // 2] = block[side // 2 :]
        second[side // 2 :] = marks[partner(own, p, q)]


def prepare_kernel(q, p, *refs):
    if p:
        first, second, refs = refs[0], refs[1], refs[2:]
        side = 2 * first.shape[0]
        edge = second.shape[0] - first.shape[0]
        flat = jnp.concatenate([first[...], second[: side // 2]], axis=0)
        mark = second[side // 2 :]
    else:
        own = lax.rem(lax.axis_index("row"), q)
        side, edge = refs[0].shape[1], refs[1].shape[1]
        flat, mark, refs = refs[0][own], refs[1][own], refs[2:]
    w_gate, w_up, w_out, w_head, inputs_t, updated_t, hidden, slope, swish, logits, onehot, normed, scale = refs
    width, bins = flat.shape[1], w_head.shape[0]
    normal, scale_inv = normalize(flat)
    normed[...] = normal
    scale[...] = jnp.broadcast_to(scale_inv, normal.shape)
    inputs = normal.astype(bf16)
    inputs_t[...] = inputs.T
    total = flat.astype(f32)
    for at, step in chunks_of(w_gate.shape[1], 256):
        span = slice(at, at + step)
        gate = nn(inputs, w_gate[:, span])
        upper = nn(inputs, w_up[:, span])
        sigma = sigmoid(gate)
        swished = gate * sigma
        hidden_part = (swished * upper).astype(bf16)
        swish[:, span] = swished
        hidden[:, span] = hidden_part
        slope[:, span] = upper * sigma * (1.0 + gate * (1.0 - sigma))
        total = total + nn(hidden_part, w_out[span, :])
    upd = total.astype(bf16)
    updated_t[...] = upd.T
    logits[...] = nt(upd, w_head[...]).astype(bf16)
    shift = edge.bit_length() - 1
    rows = lax.broadcasted_iota(jnp.int32, (side, edge), 0) >> shift
    pick = jnp.where(rows == lax.broadcasted_iota(jnp.int32, (side, edge), 1), 1.0, 0.0).astype(bf16)
    columns = lax.broadcasted_iota(jnp.int32, (side, width), 0) & (edge - 1)
    mask = columns == lax.broadcasted_iota(jnp.int32, (side, width), 1)
    lanes = lax.broadcasted_iota(jnp.int32, (side, bins), 1).astype(f32)
    picked = jnp.where(mask, nn(pick, mark), 0.0).astype(bf16)
    wanted = nn(picked, jnp.ones((width, bins), bf16))
    onehot[...] = jnp.where(wanted == lanes, 1.0, 0.0)


def backward_kernel(q, packed, *refs):
    blocks, (w_out, w_head, far, near), rest = [refs[7 * p : 7 * p + 7] for p in range(q)], refs[7 * q : 7 * q + 4], refs[7 * q + 4 :]
    (d_updated, d_gate, d_up), hot, mirrored = rest[:3], rest[3:-1], rest[-1]
    (width, side), units, bins = blocks[0][0].shape, w_out.shape[0], w_head.shape[0]
    packs = lane_packs(bins, side)
    own = lax.rem(lax.axis_index("row"), q)
    inside = lax.axis_index("row") // q == lax.axis_index("col")

    @pl.when(inside)
    def _():
        mirrored[...] = near[...]

    @pl.when(jnp.logical_not(inside))
    def _():
        mirrored[...] = far[...]

    inputs_t, updated_t, hidden, slope, swish, logits, onehot = zip(*blocks)
    mirror = jnp.concatenate([mirrored[p, :, u * bins : (u + 1) * bins] for p in range(q) for u in range(packs)], axis=0)
    summed = joined(logits, 0).astype(f32) + mirror.astype(f32)
    powers = jnp.exp(summed - jnp.max(summed, axis=-1, keepdims=True))
    probs = powers / jnp.sum(powers, axis=-1, keepdims=True)
    grad_sym = (probs - joined(onehot, 0)).astype(bf16)
    cotangent = (grad_sym.astype(f32) * 2.0).astype(bf16)
    d_upd = nn(cotangent, w_head[...])
    d_updated[...] = d_upd
    d_upd_b = d_upd.astype(bf16)
    for p in range(q):
        for top, tall in chunks_of(side, 128):
            row = slice(p * side + top, p * side + top + tall)
            for at, step in chunks_of(units, 256):
                span = slice(at, at + step)
                d_hidden = nt(d_upd_b[row], w_out[span, :])
                d_gate[row, span] = (d_hidden * slope[p][top : top + tall, span]).astype(bf16)
                d_up[row, span] = (d_hidden * swish[p][top : top + tall, span]).astype(bf16)
    depth = joined(inputs_t, 1)
    totals = (
        nn(depth, d_gate[...]),
        nn(depth, d_up[...]),
        nn(d_upd_b.T, joined(hidden, 0)),
        nn(joined(updated_t, 1), cotangent),
    )
    if not packed:
        for ref, term in zip(hot, totals):
            ref[...] = term.astype(ref.dtype)
        return
    gate_term, up_term, out_term, head_term = totals
    hot, slots = hot[:-1], hot[-1]
    nrow, ncol = packed
    groups = nrow // q
    lanes, part, tall = units // ncol, width // nrow, units // nrow
    narrow = width // ncol
    fold = lanes // tall
    short = narrow // fold
    for k in range(q):
        for a in range(groups):
            r = a * q + k
            for c in range(ncol):
                for n, term in enumerate((gate_term, up_term)):
                    block = term[r * part : (r + 1) * part, c * lanes : (c + 1) * lanes]
                    slots[k, a, (n * ncol + c) * part : (n * ncol + c + 1) * part] = block.astype(bf16)
                at = 2 * ncol * part + c * short
                block = out_term[c * narrow : (c + 1) * narrow, r * tall : (r + 1) * tall]
                block = jnp.concatenate([block[v * short : (v + 1) * short] for v in range(fold)], axis=1)
                slots[k, a, at : at + short] = block.astype(bf16)
            at = 2 * ncol * part + ncol * short
            block = head_term[r * part : (r + 1) * part, :]
            block = jnp.concatenate([block, jnp.zeros((part, lanes - bins), f32)], axis=1)
            slots[k, a, at : at + part] = block.astype(bf16)
    mine, level = lax.axis_index("row") // q, lax.axis_index("col")
    at = 2 * ncol * part + ncol * short
    lane = lax.broadcasted_iota(jnp.int32, (part, lanes), 1)
    here = (lane >= level * (bins // ncol)) & (lane < (level + 1) * (bins // ncol))
    for n in range(q):
        core = partner(own, n, q)
        for a in range(groups):
            same = jnp.where(mine == a, crossed(core, q), core)
            other = jnp.where(mine == a, core, crossed(core, q))
            for c in range(ncol):
                k = jnp.where(level == c, other, same)
                for m in (c, ncol + c):
                    hot[n][a, m * part : (m + 1) * part] = slots[k, a, m * part : (m + 1) * part]
                row = slice(2 * ncol * part + c * short, 2 * ncol * part + (c + 1) * short)
                hot[n][a, row] = slots[k, a, row]
            head = jnp.where(here, slots[other, a, at : at + part].astype(f32), slots[same, a, at : at + part].astype(f32))
            hot[n][a, at : at + part] = head.astype(bf16)


def input_kernel(p, d_updated, d_gate, d_up, normed, scale, w_gate, w_up, result):
    side = result.shape[0]
    row = slice(p * side, (p + 1) * side)
    d_inputs = nt(d_gate[row], w_gate[...]) + nt(d_up[row], w_up[...])
    normal = normed[...]
    d_norm = (
        d_inputs
        - jnp.mean(d_inputs, axis=-1, keepdims=True)
        - normal * jnp.mean(d_inputs * normal, axis=-1, keepdims=True)
    ) * scale[...]
    result[...] = (d_updated[row] + d_norm).astype(bf16)


def place_kernel(q, *refs):
    blocks, d_pair = refs[:-1], refs[-1]
    edge, _, _, width = d_pair.shape
    own = lax.rem(lax.axis_index("row"), q)
    d_pair[:, own] = blocks[0][...].reshape(edge, edge, width)
    for p in range(1, q):
        for n, half in enumerate((slice(0, edge // 2), slice(edge // 2, edge))):
            d_pair[half, partner(own, p, q)] = blocks[2 * p - 1 + n][...].reshape(edge // 2, edge, width)


def core_sum_kernel(q, groups, *rest):
    terms, blocks, hot, handed = rest[:q], rest[q : 2 * q - 1], rest[2 * q - 1 : 2 - 2 * q], rest[2 - 2 * q :]
    mine = lax.axis_index("row") // q
    for p in range(groups):
        a = following(mine, p, groups)
        total = terms[0][a].astype(f32)
        for term in terms[1:]:
            total = total + term[a].astype(f32)
        hot[p][...] = total.astype(bf16)
    for p, block in enumerate(blocks):
        half = block.shape[0] // 2
        handed[2 * p][...] = block[:half]
        handed[2 * p + 1][...] = block[half:]


def chip_sum_kernel(q, groups, ncol, shapes, *rest):
    terms, hot, slots = rest[:groups], rest[groups:-1], rest[-1]
    part, lanes, short, tall, few = shapes
    total = terms[0][...].astype(f32)
    for term in terms[1:]:
        total = total + term[...].astype(f32)
    at = 2 * ncol * part
    head = total[at + ncol * short : at + ncol * short + part]
    for c in range(ncol):
        slots[c, 0:part] = total[c * part : (c + 1) * part].astype(bf16)
        slots[c, part : 2 * part] = total[(ncol + c) * part : (ncol + c + 1) * part].astype(bf16)
        slots[c, 2 * part : 2 * part + short] = total[at + c * short : at + (c + 1) * short].astype(bf16)
        piece = jnp.concatenate([head[:, c * few : (c + 1) * few], jnp.zeros((part, lanes - few), f32)], axis=1)
        slots[c, 2 * part + short : 3 * part + short] = piece.astype(bf16)
    for p in range(ncol):
        hot[p][...] = slots[partner(lax.axis_index("col"), p, ncol)]


def col_sum_kernel(shapes, factor, *rest):
    terms, (gate, up, out, head) = rest[:-4], rest[-4:]
    part, lanes, tall, few = shapes
    total = terms[0][...].astype(f32)
    for term in terms[1:]:
        total = total + term[...].astype(f32)
    total = total * factor
    fold = lanes // tall
    short = out.shape[0] // fold
    gate[...] = total[0:part]
    up[...] = total[part : 2 * part]
    for v in range(fold):
        out[v * short : (v + 1) * short, :] = total[2 * part : 2 * part + short, v * tall : (v + 1) * tall]
    head[...] = total[2 * part + short : 3 * part + short, 0:few]


def core_pairs(nrow, q, p):
    return [(s, s - s % q + partner(s % q, p, q)) for s in range(nrow)]


def shaped(shape, kind):
    return jax.ShapeDtypeStruct(shape, kind)


def cost(flops, moved):
    return pl.CostEstimate(flops=flops, bytes_accessed=moved, transcendentals=0)


def body(pair, targets, w_gate, w_up, w_out, w_head):
    rows, cols, width = pair.shape
    units = w_gate.shape[1]
    bins = w_head.shape[1]
    nrow, ncol = lax.axis_size("row"), lax.axis_size("col")
    q = nrow // ncol
    groups = nrow // q
    side = rows * cols // q
    packs = lane_packs(bins, side)
    head_t = w_head.T
    piece = (side // packs, bins * packs)

    sources = (pair, w_gate, w_up, w_out, head_t, targets)
    pair, w_gate, w_up, w_out, head_t, marks, sends = pl.pallas_call(
        functools.partial(forward_kernel, q),
        out_shape=[shaped((q, side, width), bf16)]
        + [shaped(x.shape, bf16) for x in sources[1:5]]
        + [shaped((q, rows, width), bf16), shaped((q, *piece), bf16)],
        in_specs=[HBM] * 6,
        out_specs=[VMEM] * 7,
        scratch_shapes=[
            pltpu.VMEM((rows, cols), jnp.int32),
            pltpu.VMEM((q, *piece), bf16),
            pltpu.VMEM((q * side, units), bf16),
            pltpu.SemaphoreType.DMA((5 + q,)),
        ],
        compiler_params=PARAMS,
        name="forward",
    )(*(pltpu.with_memory_space_constraint(x, pltpu.HBM) for x in sources))

    pairs = [
        (r * ncol + c, (q * c + (partner(r % q, 1, q) if q == 2 and r // q == c else r % q)) * ncol + r // q)
        for r in range(nrow)
        for c in range(ncol)
    ]
    far = lax.ppermute(sends, ("row", "col"), pairs)
    lent = pl.pallas_call(
        functools.partial(lend_kernel, q),
        out_shape=[shaped((side // 2, width), bf16), shaped((side // 2 + rows, width), bf16)] * (q - 1),
        in_specs=[VMEM] * 2,
        out_specs=[VMEM] * (2 * q - 2),
        compiler_params=PARAMS,
        name="lend",
    )(pair, marks)
    borrowed = [lax.ppermute(x, "row", core_pairs(nrow, q, n // 2 + 1)) for n, x in enumerate(lent)]
    prepared = []
    for p in range(q):
        source = borrowed[2 * p - 2 : 2 * p] if p else (pair, marks)
        prepared.append(
            pl.pallas_call(
                functools.partial(prepare_kernel, q, p),
                out_shape=[
                    shaped((width, side), bf16),
                    shaped((width, side), bf16),
                    shaped((side, units), bf16),
                    shaped((side, units), f32),
                    shaped((side, units), f32),
                    shaped((side, bins), bf16),
                    shaped((side, bins), f32),
                    shaped((side, width), f32),
                    shaped((side, width), f32),
                ],
                in_specs=[VMEM] * (len(source) + 4),
                out_specs=[VMEM] * 9,
                compiler_params=PARAMS,
                cost_estimate=cost(0, 0) if p else cost(6 * side * width * units, 8 * side * units),
                name="prepare",
            )(*source, w_gate, w_up, w_out, head_t)
        )

    part, tall, few = width // nrow, units // nrow, bins // ncol
    lanes = units // ncol
    short = width // ncol * tall // lanes
    fits = part % 16 == 0 and lanes == 128 and lanes % tall == 0 and bins <= lanes and short % 16 == 0
    height = 2 * ncol * part + ncol * short + part
    if fits:
        hot_shapes = [shaped((groups, height, lanes), bf16)] * q
        scratch = [pltpu.VMEM((q, groups, height, lanes), bf16)]
    else:
        hot_shapes = [shaped((width, n), bf16) for n in (units, units, units, bins)]
        scratch = []
    results = pl.pallas_call(
        functools.partial(backward_kernel, q, (nrow, ncol) if fits else None),
        out_shape=[shaped((q * side, width), f32)] + [shaped((q * side, units), bf16)] * 2 + hot_shapes,
        in_specs=[VMEM] * (7 * q + 4),
        out_specs=[VMEM] * (3 + len(hot_shapes)),
        scratch_shapes=scratch + [pltpu.VMEM((q, *piece), bf16)],
        compiler_params=PARAMS,
        cost_estimate=cost(8 * q * side * width * units, 4 * q * side * units),
        name="backward",
    )(*(x for block in prepared for x in block[:7]), w_out, head_t, far, sends)
    hot = list(results[3:])

    def d_inputs(p):
        return pl.pallas_call(
            functools.partial(input_kernel, p),
            out_shape=shaped((side, width), bf16),
            in_specs=[VMEM] * 7,
            out_specs=VMEM,
            compiler_params=PARAMS,
            cost_estimate=cost(4 * side * width * units, 4 * side * units),
            name="d_inputs",
        )(*results[:3], *prepared[p][7:], w_gate, w_up)

    d_blocks = [d_inputs(p) for p in range(q)]

    def returned(blocks):
        moved = [lax.ppermute(x, "row", core_pairs(nrow, q, n // 2 + 1)) for n, x in enumerate(blocks[1:])]
        return blocks[:1] + moved

    def placed(blocks):
        return pl.pallas_call(
            functools.partial(place_kernel, q),
            out_shape=shaped((rows, q, cols // q, width), bf16),
            in_specs=[VMEM] * (2 * q - 1),
            out_specs=VMEM,
            compiler_params=PARAMS,
            name="place",
        )(*blocks).reshape(rows, cols, width)

    factor = 1.0 / (rows * nrow)
    if not fits:
        owned = []
        hot[2] = hot[2].T
        for term in hot:
            mine = lax.psum_scatter(term, "row", scatter_dimension=0, tiled=True).astype(f32)
            owned.append(lax.psum_scatter(mine, "col", scatter_dimension=1, tiled=True) * factor)
        d_blocks = d_blocks[:1] + [half for block in d_blocks[1:] for half in (block[: side // 2], block[side // 2 :])]
        return (placed(returned(d_blocks)), *owned)

    terms = [hot[0]]
    for p in range(1, q):
        terms.append(lax.ppermute(hot[p], "row", core_pairs(nrow, q, p)))
    terms, d_blocks = lax.optimization_barrier((terms, d_blocks))
    hot = pl.pallas_call(
        functools.partial(core_sum_kernel, q, groups),
        out_shape=[shaped((height, lanes), bf16)] * groups + [shaped((side // 2, width), bf16)] * (2 * q - 2),
        in_specs=[VMEM] * (2 * q - 1),
        out_specs=[VMEM] * (groups + 2 * q - 2),
        compiler_params=PARAMS,
        name="core_sum",
    )(*terms, *d_blocks[1:])
    hot, d_blocks = hot[:groups], d_blocks[:1] + list(hot[groups:])
    terms = [hot[0]]
    for p in range(1, groups):
        terms.append(lax.ppermute(hot[p], "row", [(s, following(s // q, p, groups) * q + crossed(s % q, q)) for s in range(nrow)]))
    terms, d_blocks = lax.optimization_barrier((terms, returned(d_blocks)))
    low = 3 * part + short
    hot = pl.pallas_call(
        functools.partial(chip_sum_kernel, q, groups, ncol, (part, lanes, short, tall, few)),
        out_shape=[shaped((low, lanes), bf16)] * ncol,
        in_specs=[VMEM] * groups,
        out_specs=[VMEM] * ncol,
        scratch_shapes=[pltpu.VMEM((ncol, low, lanes), bf16)],
        compiler_params=PARAMS,
        name="chip_sum",
    )(*terms)
    terms = [hot[0]]
    for p in sorted(range(1, ncol), key=lambda p: (p != ncol // 2, -p)):
        pairs = [
            (r * ncol + c, (r - r % q + crossed(r % q, q)) * ncol + partner(c, p, ncol))
            for r in range(nrow)
            for c in range(ncol)
        ]
        terms.append(lax.ppermute(hot[p], ("row", "col"), pairs))
    *terms, d_pair = lax.optimization_barrier((*terms, placed(d_blocks)))
    gate, up, out, head = pl.pallas_call(
        functools.partial(col_sum_kernel, (part, lanes, tall, few), factor),
        out_shape=[
            shaped((part, lanes), f32),
            shaped((part, lanes), f32),
            shaped((width // ncol, tall), f32),
            shaped((part, few), f32),
        ],
        in_specs=[VMEM] * ncol,
        out_specs=[VMEM] * 4,
        compiler_params=PARAMS,
        name="col_sum",
    )(*terms)
    return d_pair, gate, up, out.T, head


def solution(mesh):
    placed = (P("row", "col", None), P("row", "col"), P(), P(), P(), P())
    return jax.shard_map(
        body,
        mesh=mesh,
        in_specs=placed,
        out_specs=(P("row", "col", None), P("row", "col"), P("row", "col"), P("row", "col"), P("row", "col")),
        check_vma=False,
    )
```

```python
import functools

import jax
import jax.numpy as jnp
from jax import lax
from jax.experimental import pallas as pl
from jax.experimental.pallas import tpu as pltpu
from jax.sharding import PartitionSpec as P

eps = 1e-05
f32 = jnp.float32
bf16 = jnp.bfloat16
HBM = pl.BlockSpec(memory_space=pltpu.HBM)
VMEM = pl.BlockSpec(memory_space=pltpu.VMEM)
PARAMS = pltpu.CompilerParams(vmem_limit_bytes=24 * 1024 * 1024)


def nn(a, b):
    return lax.dot_general(a, b, (((1,), (0,)), ((), ())), preferred_element_type=f32)


def nt(a, b):
    return lax.dot_general(a, b, (((1,), (1,)), ((), ())), preferred_element_type=f32)


def tn(a, b):
    return lax.dot_general(a, b, (((0,), (0,)), ((), ())), preferred_element_type=f32)


def normalize(flat):
    values = flat.astype(f32)
    centre = values - jnp.mean(values, axis=-1, keepdims=True)
    scale_inv = lax.rsqrt(jnp.mean(centre * centre, axis=-1, keepdims=True) + eps)
    return centre * scale_inv, scale_inv


def sigmoid(v):
    return 0.5 * jnp.tanh(0.5 * v) + 0.5


def chunks_of(size, most):
    step = most if size % most == 0 else size
    return [(at, step) for at in range(0, size, step)]


def partner(s, p, n):
    if n & (n - 1) == 0:
        return s ^ p
    return (s + p) % n if isinstance(s, int) else lax.rem(s + p, n)


def crossed(k, q):
    return partner(k, 1, q) if q > 1 else k


def following(s, p, n):
    return (s + p) % n if isinstance(s, int) else lax.rem(s + p, n)


def joined(refs, axis):
    return jnp.concatenate([ref[...] for ref in refs], axis=axis)


def lane_packs(bins, side):
    packs = max(1, 128 // bins)
    return packs if (side // packs) % 16 == 0 else 1


def forward_kernel(q, *refs):
    sources, kept, (sends, hidden, sems) = refs[:6], refs[6:12], refs[12:]
    pair, w_gate, w_up, w_out, w_head, _ = kept
    _, side, width = pair.shape
    edge = sources[0].shape[0]
    bins = w_head.shape[0]
    pieces = [
        pltpu.make_async_copy(
            sources[0].at[:, h * edge : (h + 1) * edge, :], pair.reshape(q, edge, edge, width).at[h], sems.at[5 + h]
        )
        for h in range(q)
    ]
    copies = [
        pltpu.make_async_copy(source, target, sems.at[i])
        for i, (source, target) in enumerate(zip(sources[1:], kept[1:]))
    ]
    for copy in pieces + copies:
        copy.start()
    shift = edge.bit_length() - 1
    out_row = lax.broadcasted_iota(jnp.int32, (side, side), 0)
    in_row = lax.broadcasted_iota(jnp.int32, (side, side), 1)
    wanted = ((out_row & (edge - 1)) << shift) | (out_row >> shift)
    swap = jnp.where(in_row == wanted, 1.0, 0.0).astype(bf16)
    own = lax.rem(lax.axis_index("row"), q)
    for copy in pieces:
        copy.wait()
    flats = [nn(swap, pair[partner(own, p, q)]) for p in range(q)]
    inputs = [normalize(flat)[0].astype(bf16) for flat in flats]
    for copy in copies[:2]:
        copy.wait()
    packs = lane_packs(bins, side)
    deep = side // packs
    for p in range(q):
        for top, tall in chunks_of(side, 128):
            for at, step in chunks_of(w_gate.shape[1], 256):
                gate = nn(inputs[p][top : top + tall], w_gate[:, at : at + step])
                upper = nn(inputs[p][top : top + tall], w_up[:, at : at + step])
                hidden[p, top : top + tall, at : at + step] = (gate * sigmoid(gate) * upper).astype(bf16)
        if p == 0:
            for copy in copies[2:]:
                copy.wait()
        total = flats[p] + nn(hidden[p], w_out[...])
        piece = nt(total.astype(bf16), w_head[...])
        if packs > 1:
            piece = jnp.concatenate([piece[u * deep : (u + 1) * deep] for u in range(packs)], axis=1)
        sends[p] = piece.astype(bf16)


def lend_kernel(q, pair, targets, marks, *lent):
    own = lax.rem(lax.axis_index("row"), q)
    _, side, width = pair.shape
    edge = targets.shape[0]
    for h in range(q):
        mark = targets[:, h * edge : (h + 1) * edge].astype(f32)
        marks[h] = jnp.concatenate([mark, jnp.zeros((edge, width - edge), f32)], axis=1).astype(bf16)
    for p in range(1, q):
        first, second = lent[2 * p - 2 : 2 * p]
        block = pair[partner(own, p, q)]
        first[...] = block[: side // 2]
        second[: side // 2] = block[side // 2 :]
        second[side // 2 :] = marks[partner(own, p, q)]


def prepare_kernel(q, p, *refs):
    if p:
        first, second, refs = refs[0], refs[1], refs[2:]
        side = 2 * first.shape[0]
        edge = second.shape[0] - first.shape[0]
        flat = jnp.concatenate([first[...], second[: side // 2]], axis=0)
        mark = second[side // 2 :]
    else:
        own = lax.rem(lax.axis_index("row"), q)
        side, edge = refs[0].shape[1], refs[1].shape[1]
        flat, mark, refs = refs[0][own], refs[1][own], refs[2:]
    w_gate, w_up, w_out, w_head, inputs_t, updated_t, hidden, slope, swish, logits, onehot, normed, scale = refs
    width, bins = flat.shape[1], w_head.shape[0]
    normal, scale_inv = normalize(flat)
    normed[...] = normal
    scale[...] = jnp.broadcast_to(scale_inv, normal.shape)
    inputs = normal.astype(bf16)
    inputs_t[...] = inputs.T
    total = flat.astype(f32)
    for at, step in chunks_of(w_gate.shape[1], 256):
        span = slice(at, at + step)
        gate = nn(inputs, w_gate[:, span])
        upper = nn(inputs, w_up[:, span])
        sigma = sigmoid(gate)
        swished = gate * sigma
        hidden_part = (swished * upper).astype(bf16)
        swish[:, span] = swished
        hidden[:, span] = hidden_part
        slope[:, span] = upper * sigma * (1.0 + gate * (1.0 - sigma))
        total = total + nn(hidden_part, w_out[span, :])
    upd = total.astype(bf16)
    updated_t[...] = upd.T
    logits[...] = nt(upd, w_head[...]).astype(bf16)
    shift = edge.bit_length() - 1
    rows = lax.broadcasted_iota(jnp.int32, (side, edge), 0) >> shift
    pick = jnp.where(rows == lax.broadcasted_iota(jnp.int32, (side, edge), 1), 1.0, 0.0).astype(bf16)
    columns = lax.broadcasted_iota(jnp.int32, (side, width), 0) & (edge - 1)
    mask = columns == lax.broadcasted_iota(jnp.int32, (side, width), 1)
    lanes = lax.broadcasted_iota(jnp.int32, (side, bins), 1).astype(f32)
    picked = jnp.where(mask, nn(pick, mark), 0.0).astype(bf16)
    wanted = nn(picked, jnp.ones((width, bins), bf16))
    onehot[...] = jnp.where(wanted == lanes, 1.0, 0.0)


def backward_kernel(q, packed, *refs):
    blocks, (w_out, w_head, far, near), rest = [refs[7 * p : 7 * p + 7] for p in range(q)], refs[7 * q : 7 * q + 4], refs[7 * q + 4 :]
    (d_updated, d_gate, d_up), hot, mirrored = rest[:3], rest[3:-1], rest[-1]
    (width, side), units, bins = blocks[0][0].shape, w_out.shape[0], w_head.shape[0]
    packs = lane_packs(bins, side)
    own = lax.rem(lax.axis_index("row"), q)
    inside = lax.axis_index("row") // q == lax.axis_index("col")

    @pl.when(inside)
    def _():
        mirrored[...] = near[...]

    @pl.when(jnp.logical_not(inside))
    def _():
        mirrored[...] = far[...]

    inputs_t, updated_t, hidden, slope, swish, logits, onehot = zip(*blocks)
    mirror = jnp.concatenate([mirrored[p, :, u * bins : (u + 1) * bins] for p in range(q) for u in range(packs)], axis=0)
    summed = joined(logits, 0).astype(f32) + mirror.astype(f32)
    powers = jnp.exp(summed - jnp.max(summed, axis=-1, keepdims=True))
    probs = powers / jnp.sum(powers, axis=-1, keepdims=True)
    grad_sym = (probs - joined(onehot, 0)).astype(bf16)
    cotangent = (grad_sym.astype(f32) * 2.0).astype(bf16)
    d_upd = nn(cotangent, w_head[...])
    d_updated[...] = d_upd
    d_upd_b = d_upd.astype(bf16)
    for p in range(q):
        for top, tall in chunks_of(side, 128):
            row = slice(p * side + top, p * side + top + tall)
            for at, step in chunks_of(units, 256):
                span = slice(at, at + step)
                d_hidden = nt(d_upd_b[row], w_out[span, :])
                d_gate[row, span] = (d_hidden * slope[p][top : top + tall, span]).astype(bf16)
                d_up[row, span] = (d_hidden * swish[p][top : top + tall, span]).astype(bf16)
    depth = joined(inputs_t, 1)
    totals = (
        nn(depth, d_gate[...]),
        nn(depth, d_up[...]),
        nn(d_upd_b.T, joined(hidden, 0)),
        nn(joined(updated_t, 1), cotangent),
    )
    if not packed:
        for ref, term in zip(hot, totals):
            ref[...] = term.astype(ref.dtype)
        return
    gate_term, up_term, out_term, head_term = totals
    hot, slots = hot[:-1], hot[-1]
    nrow, ncol = packed
    groups = nrow // q
    lanes, part, tall = units // ncol, width // nrow, units // nrow
    narrow = width // ncol
    fold = lanes // tall
    short = narrow // fold
    for k in range(q):
        for a in range(groups):
            r = a * q + k
            for c in range(ncol):
                for n, term in enumerate((gate_term, up_term)):
                    block = term[r * part : (r + 1) * part, c * lanes : (c + 1) * lanes]
                    slots[k, a, (n * ncol + c) * part : (n * ncol + c + 1) * part] = block.astype(bf16)
                at = 2 * ncol * part + c * short
                block = out_term[c * narrow : (c + 1) * narrow, r * tall : (r + 1) * tall]
                block = jnp.concatenate([block[v * short : (v + 1) * short] for v in range(fold)], axis=1)
                slots[k, a, at : at + short] = block.astype(bf16)
            at = 2 * ncol * part + ncol * short
            block = head_term[r * part : (r + 1) * part, :]
            block = jnp.concatenate([block, jnp.zeros((part, lanes - bins), f32)], axis=1)
            slots[k, a, at : at + part] = block.astype(bf16)
    mine, level = lax.axis_index("row") // q, lax.axis_index("col")
    at = 2 * ncol * part + ncol * short
    lane = lax.broadcasted_iota(jnp.int32, (part, lanes), 1)
    here = (lane >= level * (bins // ncol)) & (lane < (level + 1) * (bins // ncol))
    for n in range(q):
        core = partner(own, n, q)
        for a in range(groups):
            same = jnp.where(mine == a, crossed(core, q), core)
            other = jnp.where(mine == a, core, crossed(core, q))
            for c in range(ncol):
                k = jnp.where(level == c, other, same)
                for m in (c, ncol + c):
                    hot[n][a, m * part : (m + 1) * part] = slots[k, a, m * part : (m + 1) * part]
                row = slice(2 * ncol * part + c * short, 2 * ncol * part + (c + 1) * short)
                hot[n][a, row] = slots[k, a, row]
            head = jnp.where(here, slots[other, a, at : at + part].astype(f32), slots[same, a, at : at + part].astype(f32))
            hot[n][a, at : at + part] = head.astype(bf16)


def input_kernel(p, d_updated, d_gate, d_up, normed, scale, w_gate, w_up, result):
    side = result.shape[0]
    row = slice(p * side, (p + 1) * side)
    d_inputs = nt(d_gate[row], w_gate[...]) + nt(d_up[row], w_up[...])
    normal = normed[...]
    d_norm = (
        d_inputs
        - jnp.mean(d_inputs, axis=-1, keepdims=True)
        - normal * jnp.mean(d_inputs * normal, axis=-1, keepdims=True)
    ) * scale[...]
    result[...] = (d_updated[row] + d_norm).astype(bf16)


def place_kernel(q, *refs):
    blocks, d_pair = refs[:-1], refs[-1]
    edge, _, _, width = d_pair.shape
    own = lax.rem(lax.axis_index("row"), q)
    d_pair[:, own] = blocks[0][...].reshape(edge, edge, width)
    for p in range(1, q):
        for n, half in enumerate((slice(0, edge // 2), slice(edge // 2, edge))):
            d_pair[half, partner(own, p, q)] = blocks[2 * p - 1 + n][...].reshape(edge // 2, edge, width)


def core_sum_kernel(q, groups, *rest):
    terms, blocks, hot, handed = rest[:q], rest[q : 2 * q - 1], rest[2 * q - 1 : 2 - 2 * q], rest[2 - 2 * q :]
    mine = lax.axis_index("row") // q
    for p in range(groups):
        a = following(mine, p, groups)
        total = terms[0][a].astype(f32)
        for term in terms[1:]:
            total = total + term[a].astype(f32)
        hot[p][...] = total.astype(bf16)
    for p, block in enumerate(blocks):
        half = block.shape[0] // 2
        handed[2 * p][...] = block[:half]
        handed[2 * p + 1][...] = block[half:]


def chip_sum_kernel(q, groups, ncol, shapes, *rest):
    terms, hot, slots = rest[:groups], rest[groups:-1], rest[-1]
    part, lanes, short, tall, few = shapes
    total = terms[0][...].astype(f32)
    for term in terms[1:]:
        total = total + term[...].astype(f32)
    at = 2 * ncol * part
    head = total[at + ncol * short : at + ncol * short + part]
    for c in range(ncol):
        slots[c, 0:part] = total[c * part : (c + 1) * part].astype(bf16)
        slots[c, part : 2 * part] = total[(ncol + c) * part : (ncol + c + 1) * part].astype(bf16)
        slots[c, 2 * part : 2 * part + short] = total[at + c * short : at + (c + 1) * short].astype(bf16)
        piece = jnp.concatenate([head[:, c * few : (c + 1) * few], jnp.zeros((part, lanes - few), f32)], axis=1)
        slots[c, 2 * part + short : 3 * part + short] = piece.astype(bf16)
    for p in range(ncol):
        hot[p][...] = slots[partner(lax.axis_index("col"), p, ncol)]


def col_sum_kernel(shapes, factor, *rest):
    terms, (gate, up, out, head) = rest[:-4], rest[-4:]
    part, lanes, tall, few = shapes
    total = terms[0][...].astype(f32)
    for term in terms[1:]:
        total = total + term[...].astype(f32)
    total = total * factor
    fold = lanes // tall
    short = out.shape[0] // fold
    gate[...] = total[0:part]
    up[...] = total[part : 2 * part]
    for v in range(fold):
        out[v * short : (v + 1) * short, :] = total[2 * part : 2 * part + short, v * tall : (v + 1) * tall]
    head[...] = total[2 * part + short : 3 * part + short, 0:few]


def core_pairs(nrow, q, p):
    return [(s, s - s % q + partner(s % q, p, q)) for s in range(nrow)]


def shaped(shape, kind):
    return jax.ShapeDtypeStruct(shape, kind)


def cost(flops, moved):
    return pl.CostEstimate(flops=flops, bytes_accessed=moved, transcendentals=0)


def body(pair, targets, w_gate, w_up, w_out, w_head):
    rows, cols, width = pair.shape
    units = w_gate.shape[1]
    bins = w_head.shape[1]
    nrow, ncol = lax.axis_size("row"), lax.axis_size("col")
    q = nrow // ncol
    groups = nrow // q
    side = rows * cols // q
    packs = lane_packs(bins, side)
    head_t = w_head.T
    piece = (side // packs, bins * packs)

    sources = (pair, w_gate, w_up, w_out, head_t, targets)
    pair, w_gate, w_up, w_out, head_t, targets, sends = pl.pallas_call(
        functools.partial(forward_kernel, q),
        out_shape=[shaped((q, side, width), bf16)]
        + [shaped(x.shape, x.dtype) for x in sources[1:]]
        + [shaped((q, *piece), bf16)],
        in_specs=[HBM] * 6,
        out_specs=[VMEM] * 7,
        scratch_shapes=[pltpu.VMEM((q, side, units), bf16), pltpu.SemaphoreType.DMA((5 + q,))],
        compiler_params=PARAMS,
        name="forward",
    )(*(pltpu.with_memory_space_constraint(x, pltpu.HBM) for x in sources))

    pairs = [
        (r * ncol + c, (q * c + (partner(r % q, 1, q) if q == 2 and r // q == c else r % q)) * ncol + r // q)
        for r in range(nrow)
        for c in range(ncol)
    ]
    far = lax.ppermute(sends, ("row", "col"), pairs)
    marks, *lent = pl.pallas_call(
        functools.partial(lend_kernel, q),
        out_shape=[shaped((q, rows, width), bf16)] + [shaped((side // 2, width), bf16), shaped((side // 2 + rows, width), bf16)] * (q - 1),
        in_specs=[VMEM] * 2,
        out_specs=[VMEM] * (2 * q - 1),
        compiler_params=PARAMS,
        name="lend",
    )(pair, targets)
    borrowed = [lax.ppermute(x, "row", core_pairs(nrow, q, n // 2 + 1)) for n, x in enumerate(lent)]
    prepared = []
    for p in range(q):
        source = borrowed[2 * p - 2 : 2 * p] if p else (pair, marks)
        prepared.append(
            pl.pallas_call(
                functools.partial(prepare_kernel, q, p),
                out_shape=[
                    shaped((width, side), bf16),
                    shaped((width, side), bf16),
                    shaped((side, units), bf16),
                    shaped((side, units), f32),
                    shaped((side, units), f32),
                    shaped((side, bins), bf16),
                    shaped((side, bins), f32),
                    shaped((side, width), f32),
                    shaped((side, width), f32),
                ],
                in_specs=[VMEM] * (len(source) + 4),
                out_specs=[VMEM] * 9,
                compiler_params=PARAMS,
                cost_estimate=cost(0, 0) if p else cost(6 * side * width * units, 8 * side * units),
                name="prepare",
            )(*source, w_gate, w_up, w_out, head_t)
        )

    part, tall, few = width // nrow, units // nrow, bins // ncol
    lanes = units // ncol
    short = width // ncol * tall // lanes
    fits = part % 16 == 0 and lanes == 128 and lanes % tall == 0 and bins <= lanes and short % 16 == 0
    height = 2 * ncol * part + ncol * short + part
    if fits:
        hot_shapes = [shaped((groups, height, lanes), bf16)] * q
        scratch = [pltpu.VMEM((q, groups, height, lanes), bf16)]
    else:
        hot_shapes = [shaped((width, n), bf16) for n in (units, units, units, bins)]
        scratch = []
    results = pl.pallas_call(
        functools.partial(backward_kernel, q, (nrow, ncol) if fits else None),
        out_shape=[shaped((q * side, width), f32)] + [shaped((q * side, units), bf16)] * 2 + hot_shapes,
        in_specs=[VMEM] * (7 * q + 4),
        out_specs=[VMEM] * (3 + len(hot_shapes)),
        scratch_shapes=scratch + [pltpu.VMEM((q, *piece), bf16)],
        compiler_params=PARAMS,
        cost_estimate=cost(8 * q * side * width * units, 4 * q * side * units),
        name="backward",
    )(*(x for block in prepared for x in block[:7]), w_out, head_t, far, sends)
    hot = list(results[3:])

    def d_inputs(p):
        return pl.pallas_call(
            functools.partial(input_kernel, p),
            out_shape=shaped((side, width), bf16),
            in_specs=[VMEM] * 7,
            out_specs=VMEM,
            compiler_params=PARAMS,
            cost_estimate=cost(4 * side * width * units, 4 * side * units),
            name="d_inputs",
        )(*results[:3], *prepared[p][7:], w_gate, w_up)

    d_blocks = [d_inputs(p) for p in range(q)]

    def returned(blocks):
        moved = [lax.ppermute(x, "row", core_pairs(nrow, q, n // 2 + 1)) for n, x in enumerate(blocks[1:])]
        return blocks[:1] + moved

    def placed(blocks):
        return pl.pallas_call(
            functools.partial(place_kernel, q),
            out_shape=shaped((rows, q, cols // q, width), bf16),
            in_specs=[VMEM] * (2 * q - 1),
            out_specs=VMEM,
            compiler_params=PARAMS,
            name="place",
        )(*blocks).reshape(rows, cols, width)

    factor = 1.0 / (rows * nrow)
    if not fits:
        owned = []
        hot[2] = hot[2].T
        for term in hot:
            mine = lax.psum_scatter(term, "row", scatter_dimension=0, tiled=True).astype(f32)
            owned.append(lax.psum_scatter(mine, "col", scatter_dimension=1, tiled=True) * factor)
        d_blocks = d_blocks[:1] + [half for block in d_blocks[1:] for half in (block[: side // 2], block[side // 2 :])]
        return (placed(returned(d_blocks)), *owned)

    terms = [hot[0]]
    for p in range(1, q):
        terms.append(lax.ppermute(hot[p], "row", core_pairs(nrow, q, p)))
    terms, d_blocks = lax.optimization_barrier((terms, d_blocks))
    hot = pl.pallas_call(
        functools.partial(core_sum_kernel, q, groups),
        out_shape=[shaped((height, lanes), bf16)] * groups + [shaped((side // 2, width), bf16)] * (2 * q - 2),
        in_specs=[VMEM] * (2 * q - 1),
        out_specs=[VMEM] * (groups + 2 * q - 2),
        compiler_params=PARAMS,
        name="core_sum",
    )(*terms, *d_blocks[1:])
    hot, d_blocks = hot[:groups], d_blocks[:1] + list(hot[groups:])
    terms = [hot[0]]
    for p in range(1, groups):
        terms.append(lax.ppermute(hot[p], "row", [(s, following(s // q, p, groups) * q + crossed(s % q, q)) for s in range(nrow)]))
    terms, d_blocks = lax.optimization_barrier((terms, returned(d_blocks)))
    low = 3 * part + short
    hot = pl.pallas_call(
        functools.partial(chip_sum_kernel, q, groups, ncol, (part, lanes, short, tall, few)),
        out_shape=[shaped((low, lanes), bf16)] * ncol,
        in_specs=[VMEM] * groups,
        out_specs=[VMEM] * ncol,
        scratch_shapes=[pltpu.VMEM((ncol, low, lanes), bf16)],
        compiler_params=PARAMS,
        name="chip_sum",
    )(*terms)
    terms = [hot[0]]
    for p in sorted(range(1, ncol), key=lambda p: (p != ncol // 2, -p)):
        pairs = [
            (r * ncol + c, (r - r % q + crossed(r % q, q)) * ncol + partner(c, p, ncol))
            for r in range(nrow)
            for c in range(ncol)
        ]
        terms.append(lax.ppermute(hot[p], ("row", "col"), pairs))
    *terms, d_pair = lax.optimization_barrier((*terms, placed(d_blocks)))
    gate, up, out, head = pl.pallas_call(
        functools.partial(col_sum_kernel, (part, lanes, tall, few), factor),
        out_shape=[
            shaped((part, lanes), f32),
            shaped((part, lanes), f32),
            shaped((width // ncol, tall), f32),
            shaped((part, few), f32),
        ],
        in_specs=[VMEM] * ncol,
        out_specs=[VMEM] * 4,
        compiler_params=PARAMS,
        name="col_sum",
    )(*terms)
    return d_pair, gate, up, out.T, head


def solution(mesh):
    placed = (P("row", "col", None), P("row", "col"), P(), P(), P(), P())
    return jax.shard_map(
        body,
        mesh=mesh,
        in_specs=placed,
        out_specs=(P("row", "col", None), P("row", "col"), P("row", "col"), P("row", "col"), P("row", "col")),
        check_vma=False,
    )
```

```python
import functools

import jax
import jax.numpy as jnp
from jax import lax
from jax.experimental import pallas as pl
from jax.experimental.pallas import tpu as pltpu
from jax.sharding import PartitionSpec as P

eps = 1e-05
PARTS = 4
f32 = jnp.float32
bf16 = jnp.bfloat16
HBM = pl.BlockSpec(memory_space=pltpu.HBM)
VMEM = pl.BlockSpec(memory_space=pltpu.VMEM)
PARAMS = pltpu.CompilerParams(vmem_limit_bytes=24 * 1024 * 1024)


def nn(a, b):
    return lax.dot_general(a, b, (((1,), (0,)), ((), ())), preferred_element_type=f32)


def nt(a, b):
    return lax.dot_general(a, b, (((1,), (1,)), ((), ())), preferred_element_type=f32)


def tn(a, b):
    return lax.dot_general(a, b, (((0,), (0,)), ((), ())), preferred_element_type=f32)


def normalize(flat):
    values = flat.astype(f32)
    centre = values - jnp.mean(values, axis=-1, keepdims=True)
    scale_inv = lax.rsqrt(jnp.mean(centre * centre, axis=-1, keepdims=True) + eps)
    return centre * scale_inv, scale_inv


def sigmoid(v):
    return 0.5 * jnp.tanh(0.5 * v) + 0.5


def chunks_of(size, most):
    step = most if size % most == 0 else size
    return [(at, step) for at in range(0, size, step)]


def partner(s, p, n):
    if n & (n - 1) == 0:
        return s ^ p
    return (s + p) % n if isinstance(s, int) else lax.rem(s + p, n)


def crossed(k, q):
    return partner(k, 1, q) if q > 1 else k


def following(s, p, n):
    return (s + p) % n if isinstance(s, int) else lax.rem(s + p, n)


def joined(refs, axis):
    return jnp.concatenate([ref[...] for ref in refs], axis=axis)


def lane_packs(bins, side):
    packs = max(1, 128 // bins)
    return packs if (side // packs) % 16 == 0 else 1


def forward_kernel(q, *refs):
    sources, (pair, w_gate, w_up, w_out, w_head, marks, sends), scratch = refs[:6], refs[6:13], refs[13:]
    targets, halves, hidden, sems = scratch
    _, side, width = pair.shape
    edge = sources[0].shape[0]
    bins = w_head.shape[0]
    copies, n = [], q
    for source, target in zip(sources[1:], (w_gate, w_up, w_out, w_head, targets)):
        parts = PARTS if source.shape[0] % (PARTS * 16) == 0 else 1
        tall = source.shape[0] // parts
        rows = [slice(i * tall, (i + 1) * tall) for i in range(parts)]
        copies.append([pltpu.make_async_copy(source.at[r], target.at[r], sems.at[n + i]) for i, r in enumerate(rows)])
        n += parts
    pieces = [
        pltpu.make_async_copy(
            sources[0].at[:, h * edge : (h + 1) * edge, :], pair.reshape(q, edge, edge, width).at[h], sems.at[h]
        )
        for h in range(q)
    ]
    for copy in pieces + [copy for group in copies for copy in group]:
        copy.start()
    shift = edge.bit_length() - 1
    out_row = lax.broadcasted_iota(jnp.int32, (side, side), 0)
    in_row = lax.broadcasted_iota(jnp.int32, (side, side), 1)
    wanted = ((out_row & (edge - 1)) << shift) | (out_row >> shift)
    swap = jnp.where(in_row == wanted, 1.0, 0.0).astype(bf16)
    own = lax.rem(lax.axis_index("row"), q)
    for copy in pieces:
        copy.wait()
    flat = pair[...].reshape(q * side, width)
    inputs = normalize(flat)[0].astype(bf16)
    for copy in copies[0] + copies[1]:
        copy.wait()
    for top, tall in chunks_of(q * side, 128):
        for at, step in chunks_of(w_gate.shape[1], 256):
            gate = nn(inputs[top : top + tall], w_gate[:, at : at + step])
            upper = nn(inputs[top : top + tall], w_up[:, at : at + step])
            hidden[top : top + tall, at : at + step] = (gate * sigmoid(gate) * upper).astype(bf16)
    for copy in copies[2] + copies[3] + copies[4]:
        copy.wait()
    total = flat.astype(f32) + nn(hidden[...], w_out[...])
    logit = nt(total.astype(bf16), w_head[...]).astype(bf16)
    packs = lane_packs(bins, side)
    deep = side // packs
    for h in range(q):
        piece = nn(swap, logit[h * side : (h + 1) * side])
        if packs > 1:
            piece = jnp.concatenate([piece[u * deep : (u + 1) * deep] for u in range(packs)], axis=1)
        halves[h] = piece.astype(bf16)
        mark = targets[:, h * edge : (h + 1) * edge].astype(f32)
        marks[h] = jnp.concatenate([mark, jnp.zeros((edge, width - edge), f32)], axis=1).astype(bf16)
    for p in range(q):
        sends[p] = halves[partner(own, p, q)]


def lend_kernel(q, pair, marks, *lent):
    own = lax.rem(lax.axis_index("row"), q)
    side = pair.shape[1]
    for p in range(1, q):
        first, second = lent[2 * p - 2 : 2 * p]
        block = pair[partner(own, p, q)]
        first[...] = block[: side // 2]
        second[: side // 2] = block[side // 2 :]
        second[side // 2 :] = marks[partner(own, p, q)]


def prepare_kernel(q, p, *refs):
    if p:
        first, second, refs = refs[0], refs[1], refs[2:]
        side = 2 * first.shape[0]
        edge = second.shape[0] - first.shape[0]
        flat = jnp.concatenate([first[...], second[: side // 2]], axis=0)
        mark = second[side // 2 :]
    else:
        own = lax.rem(lax.axis_index("row"), q)
        side, edge = refs[0].shape[1], refs[1].shape[1]
        flat, mark, refs = refs[0][own], refs[1][own], refs[2:]
    w_gate, w_up, w_out, w_head, inputs_t, updated_t, hidden, slope, swish, logits, onehot, normed, scale = refs
    width, bins = flat.shape[1], w_head.shape[0]
    normal, scale_inv = normalize(flat)
    normed[...] = normal
    scale[...] = jnp.broadcast_to(scale_inv, normal.shape)
    inputs = normal.astype(bf16)
    inputs_t[...] = inputs.T
    total = flat.astype(f32)
    for at, step in chunks_of(w_gate.shape[1], 256):
        span = slice(at, at + step)
        gate = nn(inputs, w_gate[:, span])
        upper = nn(inputs, w_up[:, span])
        sigma = sigmoid(gate)
        swished = gate * sigma
        hidden_part = (swished * upper).astype(bf16)
        swish[:, span] = swished
        hidden[:, span] = hidden_part
        slope[:, span] = upper * sigma * (1.0 + gate * (1.0 - sigma))
        total = total + nn(hidden_part, w_out[span, :])
    upd = total.astype(bf16)
    updated_t[...] = upd.T
    logits[...] = nt(upd, w_head[...]).astype(bf16)
    shift = edge.bit_length() - 1
    rows = lax.broadcasted_iota(jnp.int32, (side, edge), 0) >> shift
    pick = jnp.where(rows == lax.broadcasted_iota(jnp.int32, (side, edge), 1), 1.0, 0.0).astype(bf16)
    columns = lax.broadcasted_iota(jnp.int32, (side, width), 0) & (edge - 1)
    mask = columns == lax.broadcasted_iota(jnp.int32, (side, width), 1)
    lanes = lax.broadcasted_iota(jnp.int32, (side, bins), 1).astype(f32)
    picked = jnp.where(mask, nn(pick, mark), 0.0).astype(bf16)
    wanted = nn(picked, jnp.ones((width, bins), bf16))
    onehot[...] = jnp.where(wanted == lanes, 1.0, 0.0)


def backward_kernel(q, packed, *refs):
    blocks, (w_out, w_head, far, near), rest = [refs[7 * p : 7 * p + 7] for p in range(q)], refs[7 * q : 7 * q + 4], refs[7 * q + 4 :]
    (d_updated, d_gate, d_up), hot, mirrored = rest[:3], rest[3:-1], rest[-1]
    (width, side), units, bins = blocks[0][0].shape, w_out.shape[0], w_head.shape[0]
    packs = lane_packs(bins, side)
    own = lax.rem(lax.axis_index("row"), q)
    inside = lax.axis_index("row") // q == lax.axis_index("col")

    @pl.when(inside)
    def _():
        mirrored[...] = near[...]

    @pl.when(jnp.logical_not(inside))
    def _():
        mirrored[...] = far[...]

    inputs_t, updated_t, hidden, slope, swish, logits, onehot = zip(*blocks)
    mirror = jnp.concatenate([mirrored[p, :, u * bins : (u + 1) * bins] for p in range(q) for u in range(packs)], axis=0)
    summed = joined(logits, 0).astype(f32) + mirror.astype(f32)
    powers = jnp.exp(summed - jnp.max(summed, axis=-1, keepdims=True))
    probs = powers / jnp.sum(powers, axis=-1, keepdims=True)
    grad_sym = (probs - joined(onehot, 0)).astype(bf16)
    cotangent = (grad_sym.astype(f32) * 2.0).astype(bf16)
    d_upd = nn(cotangent, w_head[...])
    d_updated[...] = d_upd
    d_upd_b = d_upd.astype(bf16)
    for p in range(q):
        for top, tall in chunks_of(side, 128):
            row = slice(p * side + top, p * side + top + tall)
            for at, step in chunks_of(units, 256):
                span = slice(at, at + step)
                d_hidden = nt(d_upd_b[row], w_out[span, :])
                d_gate[row, span] = (d_hidden * slope[p][top : top + tall, span]).astype(bf16)
                d_up[row, span] = (d_hidden * swish[p][top : top + tall, span]).astype(bf16)
    depth = joined(inputs_t, 1)
    totals = (
        nn(depth, d_gate[...]),
        nn(depth, d_up[...]),
        nn(d_upd_b.T, joined(hidden, 0)),
        nn(joined(updated_t, 1), cotangent),
    )
    if not packed:
        for ref, term in zip(hot, totals):
            ref[...] = term.astype(ref.dtype)
        return
    gate_term, up_term, out_term, head_term = totals
    hot, slots = hot[:-1], hot[-1]
    nrow, ncol = packed
    groups = nrow // q
    lanes, part, tall = units // ncol, width // nrow, units // nrow
    narrow = width // ncol
    fold = lanes // tall
    short = narrow // fold
    for k in range(q):
        for a in range(groups):
            r = a * q + k
            for c in range(ncol):
                for n, term in enumerate((gate_term, up_term)):
                    block = term[r * part : (r + 1) * part, c * lanes : (c + 1) * lanes]
                    slots[k, a, (n * ncol + c) * part : (n * ncol + c + 1) * part] = block.astype(bf16)
                at = 2 * ncol * part + c * short
                block = out_term[c * narrow : (c + 1) * narrow, r * tall : (r + 1) * tall]
                block = jnp.concatenate([block[v * short : (v + 1) * short] for v in range(fold)], axis=1)
                slots[k, a, at : at + short] = block.astype(bf16)
            at = 2 * ncol * part + ncol * short
            block = head_term[r * part : (r + 1) * part, :]
            block = jnp.concatenate([block, jnp.zeros((part, lanes - bins), f32)], axis=1)
            slots[k, a, at : at + part] = block.astype(bf16)
    mine, level = lax.axis_index("row") // q, lax.axis_index("col")
    at = 2 * ncol * part + ncol * short
    lane = lax.broadcasted_iota(jnp.int32, (part, lanes), 1)
    here = (lane >= level * (bins // ncol)) & (lane < (level + 1) * (bins // ncol))
    for n in range(q):
        core = partner(own, n, q)
        for a in range(groups):
            same = jnp.where(mine == a, crossed(core, q), core)
            other = jnp.where(mine == a, core, crossed(core, q))
            for c in range(ncol):
                k = jnp.where(level == c, other, same)
                for m in (c, ncol + c):
                    hot[n][a, m * part : (m + 1) * part] = slots[k, a, m * part : (m + 1) * part]
                row = slice(2 * ncol * part + c * short, 2 * ncol * part + (c + 1) * short)
                hot[n][a, row] = slots[k, a, row]
            head = jnp.where(here, slots[other, a, at : at + part].astype(f32), slots[same, a, at : at + part].astype(f32))
            hot[n][a, at : at + part] = head.astype(bf16)


def input_kernel(p, d_updated, d_gate, d_up, normed, scale, w_gate, w_up, result):
    side = result.shape[0]
    row = slice(p * side, (p + 1) * side)
    d_inputs = nt(d_gate[row], w_gate[...]) + nt(d_up[row], w_up[...])
    normal = normed[...]
    d_norm = (
        d_inputs
        - jnp.mean(d_inputs, axis=-1, keepdims=True)
        - normal * jnp.mean(d_inputs * normal, axis=-1, keepdims=True)
    ) * scale[...]
    result[...] = (d_updated[row] + d_norm).astype(bf16)


def place_kernel(q, *refs):
    blocks, d_pair = refs[:-1], refs[-1]
    edge, _, _, width = d_pair.shape
    own = lax.rem(lax.axis_index("row"), q)
    d_pair[:, own] = blocks[0][...].reshape(edge, edge, width)
    for p in range(1, q):
        for n, half in enumerate((slice(0, edge // 2), slice(edge // 2, edge))):
            d_pair[half, partner(own, p, q)] = blocks[2 * p - 1 + n][...].reshape(edge // 2, edge, width)


def core_sum_kernel(q, groups, *rest):
    terms, blocks, hot, handed = rest[:q], rest[q : 2 * q - 1], rest[2 * q - 1 : 2 - 2 * q], rest[2 - 2 * q :]
    mine = lax.axis_index("row") // q
    for p in range(groups):
        a = following(mine, p, groups)
        total = terms[0][a].astype(f32)
        for term in terms[1:]:
            total = total + term[a].astype(f32)
        hot[p][...] = total.astype(bf16)
    for p, block in enumerate(blocks):
        half = block.shape[0] // 2
        handed[2 * p][...] = block[:half]
        handed[2 * p + 1][...] = block[half:]


def chip_sum_kernel(q, groups, ncol, shapes, *rest):
    terms, hot, slots = rest[:groups], rest[groups:-1], rest[-1]
    part, lanes, short, tall, few = shapes
    total = terms[0][...].astype(f32)
    for term in terms[1:]:
        total = total + term[...].astype(f32)
    at = 2 * ncol * part
    head = total[at + ncol * short : at + ncol * short + part]
    for c in range(ncol):
        slots[c, 0:part] = total[c * part : (c + 1) * part].astype(bf16)
        slots[c, part : 2 * part] = total[(ncol + c) * part : (ncol + c + 1) * part].astype(bf16)
        slots[c, 2 * part : 2 * part + short] = total[at + c * short : at + (c + 1) * short].astype(bf16)
        piece = jnp.concatenate([head[:, c * few : (c + 1) * few], jnp.zeros((part, lanes - few), f32)], axis=1)
        slots[c, 2 * part + short : 3 * part + short] = piece.astype(bf16)
    for p in range(ncol):
        hot[p][...] = slots[partner(lax.axis_index("col"), p, ncol)]


def col_sum_kernel(shapes, factor, *rest):
    terms, (gate, up, out, head) = rest[:-4], rest[-4:]
    part, lanes, tall, few = shapes
    total = terms[0][...].astype(f32)
    for term in terms[1:]:
        total = total + term[...].astype(f32)
    total = total * factor
    fold = lanes // tall
    short = out.shape[0] // fold
    gate[...] = total[0:part]
    up[...] = total[part : 2 * part]
    for v in range(fold):
        out[v * short : (v + 1) * short, :] = total[2 * part : 2 * part + short, v * tall : (v + 1) * tall]
    head[...] = total[2 * part + short : 3 * part + short, 0:few]


def core_pairs(nrow, q, p):
    return [(s, s - s % q + partner(s % q, p, q)) for s in range(nrow)]


def shaped(shape, kind):
    return jax.ShapeDtypeStruct(shape, kind)


def cost(flops, moved):
    return pl.CostEstimate(flops=flops, bytes_accessed=moved, transcendentals=0)


def body(pair, targets, w_gate, w_up, w_out, w_head):
    rows, cols, width = pair.shape
    units = w_gate.shape[1]
    bins = w_head.shape[1]
    nrow, ncol = lax.axis_size("row"), lax.axis_size("col")
    q = nrow // ncol
    groups = nrow // q
    side = rows * cols // q
    packs = lane_packs(bins, side)
    head_t = w_head.T
    piece = (side // packs, bins * packs)

    sources = (pair, w_gate, w_up, w_out, head_t, targets)
    pair, w_gate, w_up, w_out, head_t, marks, sends = pl.pallas_call(
        functools.partial(forward_kernel, q),
        out_shape=[shaped((q, side, width), bf16)]
        + [shaped(x.shape, bf16) for x in sources[1:5]]
        + [shaped((q, rows, width), bf16), shaped((q, *piece), bf16)],
        in_specs=[HBM] * 6,
        out_specs=[VMEM] * 7,
        scratch_shapes=[
            pltpu.VMEM((rows, cols), jnp.int32),
            pltpu.VMEM((q, *piece), bf16),
            pltpu.VMEM((q * side, units), bf16),
            pltpu.SemaphoreType.DMA((5 * PARTS + q,)),
        ],
        compiler_params=PARAMS,
        name="forward",
    )(*(pltpu.with_memory_space_constraint(x, pltpu.HBM) for x in sources))

    pairs = [
        (r * ncol + c, (q * c + (partner(r % q, 1, q) if q == 2 and r // q == c else r % q)) * ncol + r // q)
        for r in range(nrow)
        for c in range(ncol)
    ]
    far = lax.ppermute(sends, ("row", "col"), pairs)
    lent = pl.pallas_call(
        functools.partial(lend_kernel, q),
        out_shape=[shaped((side // 2, width), bf16), shaped((side // 2 + rows, width), bf16)] * (q - 1),
        in_specs=[VMEM] * 2,
        out_specs=[VMEM] * (2 * q - 2),
        compiler_params=PARAMS,
        name="lend",
    )(pair, marks)
    borrowed = [lax.ppermute(x, "row", core_pairs(nrow, q, n // 2 + 1)) for n, x in enumerate(lent)]
    prepared = []
    for p in range(q):
        source = borrowed[2 * p - 2 : 2 * p] if p else (pair, marks)
        prepared.append(
            pl.pallas_call(
                functools.partial(prepare_kernel, q, p),
                out_shape=[
                    shaped((width, side), bf16),
                    shaped((width, side), bf16),
                    shaped((side, units), bf16),
                    shaped((side, units), f32),
                    shaped((side, units), f32),
                    shaped((side, bins), bf16),
                    shaped((side, bins), f32),
                    shaped((side, width), f32),
                    shaped((side, width), f32),
                ],
                in_specs=[VMEM] * (len(source) + 4),
                out_specs=[VMEM] * 9,
                compiler_params=PARAMS,
                cost_estimate=cost(0, 0) if p else cost(6 * side * width * units, 8 * side * units),
                name="prepare",
            )(*source, w_gate, w_up, w_out, head_t)
        )

    part, tall, few = width // nrow, units // nrow, bins // ncol
    lanes = units // ncol
    short = width // ncol * tall // lanes
    fits = part % 16 == 0 and lanes == 128 and lanes % tall == 0 and bins <= lanes and short % 16 == 0
    height = 2 * ncol * part + ncol * short + part
    if fits:
        hot_shapes = [shaped((groups, height, lanes), bf16)] * q
        scratch = [pltpu.VMEM((q, groups, height, lanes), bf16)]
    else:
        hot_shapes = [shaped((width, n), bf16) for n in (units, units, units, bins)]
        scratch = []
    results = pl.pallas_call(
        functools.partial(backward_kernel, q, (nrow, ncol) if fits else None),
        out_shape=[shaped((q * side, width), f32)] + [shaped((q * side, units), bf16)] * 2 + hot_shapes,
        in_specs=[VMEM] * (7 * q + 4),
        out_specs=[VMEM] * (3 + len(hot_shapes)),
        scratch_shapes=scratch + [pltpu.VMEM((q, *piece), bf16)],
        compiler_params=PARAMS,
        cost_estimate=cost(8 * q * side * width * units, 4 * q * side * units),
        name="backward",
    )(*(x for block in prepared for x in block[:7]), w_out, head_t, far, sends)
    hot = list(results[3:])

    def d_inputs(p):
        return pl.pallas_call(
            functools.partial(input_kernel, p),
            out_shape=shaped((side, width), bf16),
            in_specs=[VMEM] * 7,
            out_specs=VMEM,
            compiler_params=PARAMS,
            cost_estimate=cost(4 * side * width * units, 4 * side * units),
            name="d_inputs",
        )(*results[:3], *prepared[p][7:], w_gate, w_up)

    d_blocks = [d_inputs(p) for p in range(q)]

    def returned(blocks):
        moved = [lax.ppermute(x, "row", core_pairs(nrow, q, n // 2 + 1)) for n, x in enumerate(blocks[1:])]
        return blocks[:1] + moved

    def placed(blocks):
        return pl.pallas_call(
            functools.partial(place_kernel, q),
            out_shape=shaped((rows, q, cols // q, width), bf16),
            in_specs=[VMEM] * (2 * q - 1),
            out_specs=VMEM,
            compiler_params=PARAMS,
            name="place",
        )(*blocks).reshape(rows, cols, width)

    factor = 1.0 / (rows * nrow)
    if not fits:
        owned = []
        hot[2] = hot[2].T
        for term in hot:
            mine = lax.psum_scatter(term, "row", scatter_dimension=0, tiled=True).astype(f32)
            owned.append(lax.psum_scatter(mine, "col", scatter_dimension=1, tiled=True) * factor)
        d_blocks = d_blocks[:1] + [half for block in d_blocks[1:] for half in (block[: side // 2], block[side // 2 :])]
        return (placed(returned(d_blocks)), *owned)

    terms = [hot[0]]
    for p in range(1, q):
        terms.append(lax.ppermute(hot[p], "row", core_pairs(nrow, q, p)))
    terms, d_blocks = lax.optimization_barrier((terms, d_blocks))
    hot = pl.pallas_call(
        functools.partial(core_sum_kernel, q, groups),
        out_shape=[shaped((height, lanes), bf16)] * groups + [shaped((side // 2, width), bf16)] * (2 * q - 2),
        in_specs=[VMEM] * (2 * q - 1),
        out_specs=[VMEM] * (groups + 2 * q - 2),
        compiler_params=PARAMS,
        name="core_sum",
    )(*terms, *d_blocks[1:])
    hot, d_blocks = hot[:groups], d_blocks[:1] + list(hot[groups:])
    terms = [hot[0]]
    for p in range(1, groups):
        terms.append(lax.ppermute(hot[p], "row", [(s, following(s // q, p, groups) * q + crossed(s % q, q)) for s in range(nrow)]))
    terms, d_blocks = lax.optimization_barrier((terms, returned(d_blocks)))
    low = 3 * part + short
    hot = pl.pallas_call(
        functools.partial(chip_sum_kernel, q, groups, ncol, (part, lanes, short, tall, few)),
        out_shape=[shaped((low, lanes), bf16)] * ncol,
        in_specs=[VMEM] * groups,
        out_specs=[VMEM] * ncol,
        scratch_shapes=[pltpu.VMEM((ncol, low, lanes), bf16)],
        compiler_params=PARAMS,
        name="chip_sum",
    )(*terms)
    terms = [hot[0]]
    for p in sorted(range(1, ncol), key=lambda p: (p != ncol // 2, -p)):
        pairs = [
            (r * ncol + c, (r - r % q + crossed(r % q, q)) * ncol + partner(c, p, ncol))
            for r in range(nrow)
            for c in range(ncol)
        ]
        terms.append(lax.ppermute(hot[p], ("row", "col"), pairs))
    *terms, d_pair = lax.optimization_barrier((*terms, placed(d_blocks)))
    gate, up, out, head = pl.pallas_call(
        functools.partial(col_sum_kernel, (part, lanes, tall, few), factor),
        out_shape=[
            shaped((part, lanes), f32),
            shaped((part, lanes), f32),
            shaped((width // ncol, tall), f32),
            shaped((part, few), f32),
        ],
        in_specs=[VMEM] * ncol,
        out_specs=[VMEM] * 4,
        compiler_params=PARAMS,
        name="col_sum",
    )(*terms)
    return d_pair, gate, up, out.T, head


def solution(mesh):
    placed = (P("row", "col", None), P("row", "col"), P(), P(), P(), P())
    return jax.shard_map(
        body,
        mesh=mesh,
        in_specs=placed,
        out_specs=(P("row", "col", None), P("row", "col"), P("row", "col"), P("row", "col"), P("row", "col")),
        check_vma=False,
    )
```

```python
import functools

import jax
import jax.numpy as jnp
from jax import lax
from jax.experimental import pallas as pl
from jax.experimental.pallas import tpu as pltpu
from jax.sharding import PartitionSpec as P

eps = 1e-05
f32 = jnp.float32
bf16 = jnp.bfloat16
HBM = pl.BlockSpec(memory_space=pltpu.HBM)
VMEM = pl.BlockSpec(memory_space=pltpu.VMEM)
PARAMS = pltpu.CompilerParams(vmem_limit_bytes=24 * 1024 * 1024)


def nn(a, b):
    return lax.dot_general(a, b, (((1,), (0,)), ((), ())), preferred_element_type=f32)


def nt(a, b):
    return lax.dot_general(a, b, (((1,), (1,)), ((), ())), preferred_element_type=f32)


def tn(a, b):
    return lax.dot_general(a, b, (((0,), (0,)), ((), ())), preferred_element_type=f32)


def normalize(flat):
    values = flat.astype(f32)
    centre = values - jnp.mean(values, axis=-1, keepdims=True)
    scale_inv = lax.rsqrt(jnp.mean(centre * centre, axis=-1, keepdims=True) + eps)
    return centre * scale_inv, scale_inv


def chunks_of(size, most):
    step = most if size % most == 0 else size
    return [(at, step) for at in range(0, size, step)]


def partner(s, p, n):
    if n & (n - 1) == 0:
        return s ^ p
    return (s + p) % n if isinstance(s, int) else lax.rem(s + p, n)


def crossed(k, q):
    return partner(k, 1, q) if q > 1 else k


def following(s, p, n):
    return (s + p) % n if isinstance(s, int) else lax.rem(s + p, n)


def joined(refs, axis):
    return jnp.concatenate([ref[...] for ref in refs], axis=axis)


def lane_packs(bins, side):
    packs = max(1, 128 // bins)
    return packs if (side // packs) % 16 == 0 else 1


def forward_kernel(q, *refs):
    sources, (pair, w_gate, w_up, w_out, w_head, marks, sends), scratch = refs[:6], refs[6:13], refs[13:]
    targets, halves, hidden, sems = scratch
    _, side, width = pair.shape
    edge = sources[0].shape[0]
    bins = w_head.shape[0]
    copies = [
        pltpu.make_async_copy(source, target, sems.at[i])
        for i, (source, target) in enumerate(zip(sources[1:], (w_gate, w_up, w_out, w_head, targets)))
    ]
    pieces = [
        pltpu.make_async_copy(
            sources[0].at[:, h * edge : (h + 1) * edge, :], pair.reshape(q, edge, edge, width).at[h], sems.at[5 + h]
        )
        for h in range(q)
    ]
    for copy in pieces + copies:
        copy.start()
    shift = edge.bit_length() - 1
    out_row = lax.broadcasted_iota(jnp.int32, (side, side), 0)
    in_row = lax.broadcasted_iota(jnp.int32, (side, side), 1)
    wanted = ((out_row & (edge - 1)) << shift) | (out_row >> shift)
    swap = jnp.where(in_row == wanted, 1.0, 0.0).astype(bf16)
    own = lax.rem(lax.axis_index("row"), q)
    for copy in pieces:
        copy.wait()
    flat = pair[...].reshape(q * side, width)
    inputs = normalize(flat)[0].astype(bf16)
    for copy in copies[:2]:
        copy.wait()
    for at, step in chunks_of(w_gate.shape[1], 256):
        w_half = w_gate[:, at : at + step] * 0.5
        for top, tall in chunks_of(q * side, 256):
            half = nn(inputs[top : top + tall], w_half)
            upper = nn(inputs[top : top + tall], w_up[:, at : at + step])
            hidden[top : top + tall, at : at + step] = (half * (1.0 + jnp.tanh(half)) * upper).astype(bf16)
    for copy in copies[2:]:
        copy.wait()
    total = flat.astype(f32) + nn(hidden[...], w_out[...])
    logit = nt(total.astype(bf16), w_head[...]).astype(bf16)
    packs = lane_packs(bins, side)
    deep = side // packs
    for h in range(q):
        piece = nn(swap, logit[h * side : (h + 1) * side])
        if packs > 1:
            piece = jnp.concatenate([piece[u * deep : (u + 1) * deep] for u in range(packs)], axis=1)
        halves[h] = piece.astype(bf16)
        mark = targets[:, h * edge : (h + 1) * edge].astype(f32)
        marks[h] = jnp.concatenate([mark, jnp.zeros((edge, width - edge), f32)], axis=1).astype(bf16)
    for p in range(q):
        sends[p] = halves[partner(own, p, q)]


def lend_kernel(q, pair, marks, *lent):
    own = lax.rem(lax.axis_index("row"), q)
    side = pair.shape[1]
    for p in range(1, q):
        first, second = lent[2 * p - 2 : 2 * p]
        block = pair[partner(own, p, q)]
        first[...] = block[: side // 2]
        second[: side // 2] = block[side // 2 :]
        second[side // 2 :] = marks[partner(own, p, q)]


def prepare_kernel(q, p, *refs):
    if p:
        first, second, refs = refs[0], refs[1], refs[2:]
        side = 2 * first.shape[0]
        edge = second.shape[0] - first.shape[0]
        flat = jnp.concatenate([first[...], second[: side // 2]], axis=0)
        mark = second[side // 2 :]
    else:
        own = lax.rem(lax.axis_index("row"), q)
        side, edge = refs[0].shape[1], refs[1].shape[1]
        flat, mark, refs = refs[0][own], refs[1][own], refs[2:]
    w_gate, w_up, w_out, w_head, inputs_t, updated_t, hidden, slope, swish, logits, onehot, normed, scale = refs
    width, bins = flat.shape[1], w_head.shape[0]
    normal, scale_inv = normalize(flat)
    normed[...] = normal
    scale[...] = jnp.broadcast_to(scale_inv, normal.shape)
    inputs = normal.astype(bf16)
    inputs_t[...] = inputs.T
    total = flat.astype(f32)
    for at, step in chunks_of(w_gate.shape[1], 256):
        span = slice(at, at + step)
        half = nn(inputs, w_gate[:, span] * 0.5)
        upper = nn(inputs, w_up[:, span])
        curve = jnp.tanh(half)
        raised = 1.0 + curve
        swished = half * raised
        hidden_part = (swished * upper).astype(bf16)
        swish[:, span] = swished
        hidden[:, span] = hidden_part
        slope[:, span] = upper * (0.5 * raised) * (1.0 + half * (1.0 - curve))
        total = total + nn(hidden_part, w_out[span, :])
    upd = total.astype(bf16)
    updated_t[...] = upd.T
    logits[...] = nt(upd, w_head[...]).astype(bf16)
    shift = edge.bit_length() - 1
    rows = lax.broadcasted_iota(jnp.int32, (side, edge), 0) >> shift
    pick = jnp.where(rows == lax.broadcasted_iota(jnp.int32, (side, edge), 1), 1.0, 0.0).astype(bf16)
    columns = lax.broadcasted_iota(jnp.int32, (side, width), 0) & (edge - 1)
    mask = columns == lax.broadcasted_iota(jnp.int32, (side, width), 1)
    lanes = lax.broadcasted_iota(jnp.int32, (side, bins), 1).astype(f32)
    picked = jnp.where(mask, nn(pick, mark), 0.0).astype(bf16)
    wanted = nn(picked, jnp.ones((width, bins), bf16))
    onehot[...] = jnp.where(wanted == lanes, 1.0, 0.0)


def backward_kernel(q, packed, *refs):
    blocks, (w_out, w_head, far, near), rest = [refs[7 * p : 7 * p + 7] for p in range(q)], refs[7 * q : 7 * q + 4], refs[7 * q + 4 :]
    (d_updated, d_gate, d_up), hot, mirrored = rest[:3], rest[3:-1], rest[-1]
    (width, side), units, bins = blocks[0][0].shape, w_out.shape[0], w_head.shape[0]
    packs = lane_packs(bins, side)
    own = lax.rem(lax.axis_index("row"), q)
    inside = lax.axis_index("row") // q == lax.axis_index("col")

    @pl.when(inside)
    def _():
        mirrored[...] = near[...]

    @pl.when(jnp.logical_not(inside))
    def _():
        mirrored[...] = far[...]

    inputs_t, updated_t, hidden, slope, swish, logits, onehot = zip(*blocks)
    mirror = jnp.concatenate([mirrored[p, :, u * bins : (u + 1) * bins] for p in range(q) for u in range(packs)], axis=0)
    summed = joined(logits, 0).astype(f32) + mirror.astype(f32)
    powers = jnp.exp(summed - jnp.max(summed, axis=-1, keepdims=True))
    probs = powers / jnp.sum(powers, axis=-1, keepdims=True)
    grad_sym = (probs - joined(onehot, 0)).astype(bf16)
    cotangent = (grad_sym.astype(f32) * 2.0).astype(bf16)
    d_upd = nn(cotangent, w_head[...])
    d_updated[...] = d_upd
    d_upd_b = d_upd.astype(bf16)
    for p in range(q):
        for top, tall in chunks_of(side, 128):
            row = slice(p * side + top, p * side + top + tall)
            for at, step in chunks_of(units, 256):
                span = slice(at, at + step)
                d_hidden = nt(d_upd_b[row], w_out[span, :])
                d_gate[row, span] = (d_hidden * slope[p][top : top + tall, span]).astype(bf16)
                d_up[row, span] = (d_hidden * swish[p][top : top + tall, span]).astype(bf16)
    depth = joined(inputs_t, 1)
    totals = (
        nn(depth, d_gate[...]),
        nn(depth, d_up[...]),
        nn(d_upd_b.T, joined(hidden, 0)),
        nn(joined(updated_t, 1), cotangent),
    )
    if not packed:
        for ref, term in zip(hot, totals):
            ref[...] = term.astype(ref.dtype)
        return
    gate_term, up_term, out_term, head_term = totals
    hot, slots = hot[:-1], hot[-1]
    nrow, ncol = packed
    groups = nrow // q
    lanes, part, tall = units // ncol, width // nrow, units // nrow
    narrow = width // ncol
    fold = lanes // tall
    short = narrow // fold
    for k in range(q):
        for a in range(groups):
            r = a * q + k
            for c in range(ncol):
                for n, term in enumerate((gate_term, up_term)):
                    block = term[r * part : (r + 1) * part, c * lanes : (c + 1) * lanes]
                    slots[k, a, (n * ncol + c) * part : (n * ncol + c + 1) * part] = block.astype(bf16)
                at = 2 * ncol * part + c * short
                block = out_term[c * narrow : (c + 1) * narrow, r * tall : (r + 1) * tall]
                block = jnp.concatenate([block[v * short : (v + 1) * short] for v in range(fold)], axis=1)
                slots[k, a, at : at + short] = block.astype(bf16)
            at = 2 * ncol * part + ncol * short
            block = head_term[r * part : (r + 1) * part, :]
            block = jnp.concatenate([block, jnp.zeros((part, lanes - bins), f32)], axis=1)
            slots[k, a, at : at + part] = block.astype(bf16)
    mine, level = lax.axis_index("row") // q, lax.axis_index("col")
    at = 2 * ncol * part + ncol * short
    lane = lax.broadcasted_iota(jnp.int32, (part, lanes), 1)
    here = (lane >= level * (bins // ncol)) & (lane < (level + 1) * (bins // ncol))
    for n in range(q):
        core = partner(own, n, q)
        for a in range(groups):
            same = jnp.where(mine == a, crossed(core, q), core)
            other = jnp.where(mine == a, core, crossed(core, q))
            for c in range(ncol):
                k = jnp.where(level == c, other, same)
                for m in (c, ncol + c):
                    hot[n][a, m * part : (m + 1) * part] = slots[k, a, m * part : (m + 1) * part]
                row = slice(2 * ncol * part + c * short, 2 * ncol * part + (c + 1) * short)
                hot[n][a, row] = slots[k, a, row]
            head = jnp.where(here, slots[other, a, at : at + part].astype(f32), slots[same, a, at : at + part].astype(f32))
            hot[n][a, at : at + part] = head.astype(bf16)


def input_kernel(p, d_updated, d_gate, d_up, normed, scale, w_gate, w_up, result):
    side = result.shape[0]
    row = slice(p * side, (p + 1) * side)
    d_inputs = nt(d_gate[row], w_gate[...]) + nt(d_up[row], w_up[...])
    normal = normed[...]
    d_norm = (
        d_inputs
        - jnp.mean(d_inputs, axis=-1, keepdims=True)
        - normal * jnp.mean(d_inputs * normal, axis=-1, keepdims=True)
    ) * scale[...]
    result[...] = (d_updated[row] + d_norm).astype(bf16)


def place_kernel(q, *refs):
    blocks, d_pair = refs[:-1], refs[-1]
    edge, _, _, width = d_pair.shape
    own = lax.rem(lax.axis_index("row"), q)
    d_pair[:, own] = blocks[0][...].reshape(edge, edge, width)
    for p in range(1, q):
        for n, half in enumerate((slice(0, edge // 2), slice(edge // 2, edge))):
            d_pair[half, partner(own, p, q)] = blocks[2 * p - 1 + n][...].reshape(edge // 2, edge, width)


def core_sum_kernel(q, groups, *rest):
    terms, blocks, hot, handed = rest[:q], rest[q : 2 * q - 1], rest[2 * q - 1 : 2 - 2 * q], rest[2 - 2 * q :]
    mine = lax.axis_index("row") // q
    for p in range(groups):
        a = following(mine, p, groups)
        total = terms[0][a].astype(f32)
        for term in terms[1:]:
            total = total + term[a].astype(f32)
        hot[p][...] = total.astype(bf16)
    for p, block in enumerate(blocks):
        half = block.shape[0] // 2
        handed[2 * p][...] = block[:half]
        handed[2 * p + 1][...] = block[half:]


def chip_sum_kernel(q, groups, ncol, shapes, *rest):
    terms, hot, slots = rest[:groups], rest[groups:-1], rest[-1]
    part, lanes, short, tall, few = shapes
    total = terms[0][...].astype(f32)
    for term in terms[1:]:
        total = total + term[...].astype(f32)
    at = 2 * ncol * part
    head = total[at + ncol * short : at + ncol * short + part]
    for c in range(ncol):
        slots[c, 0:part] = total[c * part : (c + 1) * part].astype(bf16)
        slots[c, part : 2 * part] = total[(ncol + c) * part : (ncol + c + 1) * part].astype(bf16)
        slots[c, 2 * part : 2 * part + short] = total[at + c * short : at + (c + 1) * short].astype(bf16)
        piece = jnp.concatenate([head[:, c * few : (c + 1) * few], jnp.zeros((part, lanes - few), f32)], axis=1)
        slots[c, 2 * part + short : 3 * part + short] = piece.astype(bf16)
    for p in range(ncol):
        hot[p][...] = slots[partner(lax.axis_index("col"), p, ncol)]


def col_sum_kernel(shapes, factor, *rest):
    terms, (gate, up, out, head) = rest[:-4], rest[-4:]
    part, lanes, tall, few = shapes
    total = terms[0][...].astype(f32)
    for term in terms[1:]:
        total = total + term[...].astype(f32)
    total = total * factor
    fold = lanes // tall
    short = out.shape[0] // fold
    gate[...] = total[0:part]
    up[...] = total[part : 2 * part]
    for v in range(fold):
        out[v * short : (v + 1) * short, :] = total[2 * part : 2 * part + short, v * tall : (v + 1) * tall]
    head[...] = total[2 * part + short : 3 * part + short, 0:few]


def core_pairs(nrow, q, p):
    return [(s, s - s % q + partner(s % q, p, q)) for s in range(nrow)]


def shaped(shape, kind):
    return jax.ShapeDtypeStruct(shape, kind)


def cost(flops, moved):
    return pl.CostEstimate(flops=flops, bytes_accessed=moved, transcendentals=0)


def body(pair, targets, w_gate, w_up, w_out, w_head):
    rows, cols, width = pair.shape
    units = w_gate.shape[1]
    bins = w_head.shape[1]
    nrow, ncol = lax.axis_size("row"), lax.axis_size("col")
    q = nrow // ncol
    groups = nrow // q
    side = rows * cols // q
    packs = lane_packs(bins, side)
    head_t = w_head.T
    piece = (side // packs, bins * packs)

    sources = (pair, w_gate, w_up, w_out, head_t, targets)
    pair, w_gate, w_up, w_out, head_t, marks, sends = pl.pallas_call(
        functools.partial(forward_kernel, q),
        out_shape=[shaped((q, side, width), bf16)]
        + [shaped(x.shape, bf16) for x in sources[1:5]]
        + [shaped((q, rows, width), bf16), shaped((q, *piece), bf16)],
        in_specs=[HBM] * 6,
        out_specs=[VMEM] * 7,
        scratch_shapes=[
            pltpu.VMEM((rows, cols), jnp.int32),
            pltpu.VMEM((q, *piece), bf16),
            pltpu.VMEM((q * side, units), bf16),
            pltpu.SemaphoreType.DMA((5 + q,)),
        ],
        compiler_params=PARAMS,
        name="forward",
    )(*(pltpu.with_memory_space_constraint(x, pltpu.HBM) for x in sources))

    pairs = [
        (r * ncol + c, (q * c + (partner(r % q, 1, q) if q == 2 and r // q == c else r % q)) * ncol + r // q)
        for r in range(nrow)
        for c in range(ncol)
    ]
    far = lax.ppermute(sends, ("row", "col"), pairs)
    lent = pl.pallas_call(
        functools.partial(lend_kernel, q),
        out_shape=[shaped((side // 2, width), bf16), shaped((side // 2 + rows, width), bf16)] * (q - 1),
        in_specs=[VMEM] * 2,
        out_specs=[VMEM] * (2 * q - 2),
        compiler_params=PARAMS,
        name="lend",
    )(pair, marks)
    borrowed = [lax.ppermute(x, "row", core_pairs(nrow, q, n // 2 + 1)) for n, x in enumerate(lent)]
    prepared = []
    for p in range(q):
        source = borrowed[2 * p - 2 : 2 * p] if p else (pair, marks)
        prepared.append(
            pl.pallas_call(
                functools.partial(prepare_kernel, q, p),
                out_shape=[
                    shaped((width, side), bf16),
                    shaped((width, side), bf16),
                    shaped((side, units), bf16),
                    shaped((side, units), f32),
                    shaped((side, units), f32),
                    shaped((side, bins), bf16),
                    shaped((side, bins), f32),
                    shaped((side, width), f32),
                    shaped((side, width), f32),
                ],
                in_specs=[VMEM] * (len(source) + 4),
                out_specs=[VMEM] * 9,
                compiler_params=PARAMS,
                cost_estimate=cost(0, 0) if p else cost(6 * side * width * units, 8 * side * units),
                name="prepare",
            )(*source, w_gate, w_up, w_out, head_t)
        )

    part, tall, few = width // nrow, units // nrow, bins // ncol
    lanes = units // ncol
    short = width // ncol * tall // lanes
    fits = part % 16 == 0 and lanes == 128 and lanes % tall == 0 and bins <= lanes and short % 16 == 0
    height = 2 * ncol * part + ncol * short + part
    if fits:
        hot_shapes = [shaped((groups, height, lanes), bf16)] * q
        scratch = [pltpu.VMEM((q, groups, height, lanes), bf16)]
    else:
        hot_shapes = [shaped((width, n), bf16) for n in (units, units, units, bins)]
        scratch = []
    results = pl.pallas_call(
        functools.partial(backward_kernel, q, (nrow, ncol) if fits else None),
        out_shape=[shaped((q * side, width), f32)] + [shaped((q * side, units), bf16)] * 2 + hot_shapes,
        in_specs=[VMEM] * (7 * q + 4),
        out_specs=[VMEM] * (3 + len(hot_shapes)),
        scratch_shapes=scratch + [pltpu.VMEM((q, *piece), bf16)],
        compiler_params=PARAMS,
        cost_estimate=cost(8 * q * side * width * units, 4 * q * side * units),
        name="backward",
    )(*(x for block in prepared for x in block[:7]), w_out, head_t, far, sends)
    hot = list(results[3:])

    def d_inputs(p):
        return pl.pallas_call(
            functools.partial(input_kernel, p),
            out_shape=shaped((side, width), bf16),
            in_specs=[VMEM] * 7,
            out_specs=VMEM,
            compiler_params=PARAMS,
            cost_estimate=cost(4 * side * width * units, 4 * side * units),
            name="d_inputs",
        )(*results[:3], *prepared[p][7:], w_gate, w_up)

    d_blocks = [d_inputs(p) for p in range(q)]

    def returned(blocks):
        moved = [lax.ppermute(x, "row", core_pairs(nrow, q, n // 2 + 1)) for n, x in enumerate(blocks[1:])]
        return blocks[:1] + moved

    def placed(blocks):
        return pl.pallas_call(
            functools.partial(place_kernel, q),
            out_shape=shaped((rows, q, cols // q, width), bf16),
            in_specs=[VMEM] * (2 * q - 1),
            out_specs=VMEM,
            compiler_params=PARAMS,
            name="place",
        )(*blocks).reshape(rows, cols, width)

    factor = 1.0 / (rows * nrow)
    if not fits:
        owned = []
        hot[2] = hot[2].T
        for term in hot:
            mine = lax.psum_scatter(term, "row", scatter_dimension=0, tiled=True).astype(f32)
            owned.append(lax.psum_scatter(mine, "col", scatter_dimension=1, tiled=True) * factor)
        d_blocks = d_blocks[:1] + [half for block in d_blocks[1:] for half in (block[: side // 2], block[side // 2 :])]
        return (placed(returned(d_blocks)), *owned)

    terms = [hot[0]]
    for p in range(1, q):
        terms.append(lax.ppermute(hot[p], "row", core_pairs(nrow, q, p)))
    terms, d_blocks = lax.optimization_barrier((terms, d_blocks))
    hot = pl.pallas_call(
        functools.partial(core_sum_kernel, q, groups),
        out_shape=[shaped((height, lanes), bf16)] * groups + [shaped((side // 2, width), bf16)] * (2 * q - 2),
        in_specs=[VMEM] * (2 * q - 1),
        out_specs=[VMEM] * (groups + 2 * q - 2),
        compiler_params=PARAMS,
        name="core_sum",
    )(*terms, *d_blocks[1:])
    hot, d_blocks = hot[:groups], d_blocks[:1] + list(hot[groups:])
    terms = [hot[0]]
    for p in range(1, groups):
        terms.append(lax.ppermute(hot[p], "row", [(s, following(s // q, p, groups) * q + crossed(s % q, q)) for s in range(nrow)]))
    terms, d_blocks = lax.optimization_barrier((terms, returned(d_blocks)))
    low = 3 * part + short
    hot = pl.pallas_call(
        functools.partial(chip_sum_kernel, q, groups, ncol, (part, lanes, short, tall, few)),
        out_shape=[shaped((low, lanes), bf16)] * ncol,
        in_specs=[VMEM] * groups,
        out_specs=[VMEM] * ncol,
        scratch_shapes=[pltpu.VMEM((ncol, low, lanes), bf16)],
        compiler_params=PARAMS,
        name="chip_sum",
    )(*terms)
    terms = [hot[0]]
    for p in sorted(range(1, ncol), key=lambda p: (p != ncol // 2, -p)):
        pairs = [
            (r * ncol + c, (r - r % q + crossed(r % q, q)) * ncol + partner(c, p, ncol))
            for r in range(nrow)
            for c in range(ncol)
        ]
        terms.append(lax.ppermute(hot[p], ("row", "col"), pairs))
    *terms, d_pair = lax.optimization_barrier((*terms, placed(d_blocks)))
    gate, up, out, head = pl.pallas_call(
        functools.partial(col_sum_kernel, (part, lanes, tall, few), factor),
        out_shape=[
            shaped((part, lanes), f32),
            shaped((part, lanes), f32),
            shaped((width // ncol, tall), f32),
            shaped((part, few), f32),
        ],
        in_specs=[VMEM] * ncol,
        out_specs=[VMEM] * 4,
        compiler_params=PARAMS,
        name="col_sum",
    )(*terms)
    return d_pair, gate, up, out.T, head


def solution(mesh):
    placed = (P("row", "col", None), P("row", "col"), P(), P(), P(), P())
    return jax.shard_map(
        body,
        mesh=mesh,
        in_specs=placed,
        out_specs=(P("row", "col", None), P("row", "col"), P("row", "col"), P("row", "col"), P("row", "col")),
        check_vma=False,
    )
```

```python
import functools

import jax
import jax.numpy as jnp
from jax import lax
from jax.experimental import pallas as pl
from jax.experimental.pallas import tpu as pltpu
from jax.sharding import PartitionSpec as P

eps = 1e-05
f32 = jnp.float32
bf16 = jnp.bfloat16
HBM = pl.BlockSpec(memory_space=pltpu.HBM)
VMEM = pl.BlockSpec(memory_space=pltpu.VMEM)
PARAMS = pltpu.CompilerParams(vmem_limit_bytes=24 * 1024 * 1024)


def nn(a, b):
    return lax.dot_general(a, b, (((1,), (0,)), ((), ())), preferred_element_type=f32)


def nt(a, b):
    return lax.dot_general(a, b, (((1,), (1,)), ((), ())), preferred_element_type=f32)


def tn(a, b):
    return lax.dot_general(a, b, (((0,), (0,)), ((), ())), preferred_element_type=f32)


def normalize(flat):
    values = flat.astype(f32)
    centre = values - jnp.mean(values, axis=-1, keepdims=True)
    scale_inv = lax.rsqrt(jnp.mean(centre * centre, axis=-1, keepdims=True) + eps)
    return centre * scale_inv, scale_inv


def row_sums(values):
    width = values.shape[1]
    high = values.astype(bf16)
    low = (values - high.astype(f32)).astype(bf16)
    return nn(jnp.concatenate([high, low], axis=1), jnp.ones((2 * width, width), bf16))


def normalize_rows(flat):
    width = flat.shape[1]
    centre = flat.astype(f32) - nn(flat, jnp.ones((width, width), bf16)) * (1.0 / width)
    return centre * lax.rsqrt(row_sums(centre * centre) * (1.0 / width) + eps)


def chunks_of(size, most):
    step = most if size % most == 0 else size
    return [(at, step) for at in range(0, size, step)]


def partner(s, p, n):
    if n & (n - 1) == 0:
        return s ^ p
    return (s + p) % n if isinstance(s, int) else lax.rem(s + p, n)


def crossed(k, q):
    return partner(k, 1, q) if q > 1 else k


def following(s, p, n):
    return (s + p) % n if isinstance(s, int) else lax.rem(s + p, n)


def joined(refs, axis):
    return jnp.concatenate([ref[...] for ref in refs], axis=axis)


def lane_packs(bins, side):
    packs = max(1, 128 // bins)
    return packs if (side // packs) % 16 == 0 else 1


def forward_kernel(q, *refs):
    sources, (pair, w_gate, w_up, w_out, w_head, marks, sends), scratch = refs[:6], refs[6:13], refs[13:]
    targets, halves, hidden, sems = scratch
    _, side, width = pair.shape
    edge = sources[0].shape[0]
    bins = w_head.shape[0]
    copies = [
        pltpu.make_async_copy(source, target, sems.at[i])
        for i, (source, target) in enumerate(zip(sources[1:], (w_gate, w_up, w_out, w_head, targets)))
    ]
    pieces = [
        pltpu.make_async_copy(
            sources[0].at[:, h * edge : (h + 1) * edge, :], pair.reshape(q, edge, edge, width).at[h], sems.at[5 + h]
        )
        for h in range(q)
    ]
    for copy in pieces + copies:
        copy.start()
    shift = edge.bit_length() - 1
    out_row = lax.broadcasted_iota(jnp.int32, (side, side), 0)
    in_row = lax.broadcasted_iota(jnp.int32, (side, side), 1)
    wanted = ((out_row & (edge - 1)) << shift) | (out_row >> shift)
    swap = jnp.where(in_row == wanted, 1.0, 0.0).astype(bf16)
    own = lax.rem(lax.axis_index("row"), q)
    for copy in pieces:
        copy.wait()
    flat = pair[...].reshape(q * side, width)
    inputs = normalize_rows(flat).astype(bf16)
    for copy in copies[:2]:
        copy.wait()
    for at, step in chunks_of(w_gate.shape[1], 256):
        w_half = w_gate[:, at : at + step] * 0.5
        for top, tall in chunks_of(q * side, 256):
            half = nn(inputs[top : top + tall], w_half)
            upper = nn(inputs[top : top + tall], w_up[:, at : at + step])
            hidden[top : top + tall, at : at + step] = (half * (1.0 + jnp.tanh(half)) * upper).astype(bf16)
    for copy in copies[2:]:
        copy.wait()
    total = flat.astype(f32) + nn(hidden[...], w_out[...])
    logit = nt(total.astype(bf16), w_head[...]).astype(bf16)
    packs = lane_packs(bins, side)
    deep = side // packs
    for h in range(q):
        piece = nn(swap, logit[h * side : (h + 1) * side])
        if packs > 1:
            piece = jnp.concatenate([piece[u * deep : (u + 1) * deep] for u in range(packs)], axis=1)
        halves[h] = piece.astype(bf16)
        mark = targets[:, h * edge : (h + 1) * edge].astype(f32)
        marks[h] = jnp.concatenate([mark, jnp.zeros((edge, width - edge), f32)], axis=1).astype(bf16)
    for p in range(q):
        sends[p] = halves[partner(own, p, q)]


def lend_kernel(q, pair, marks, *lent):
    own = lax.rem(lax.axis_index("row"), q)
    side = pair.shape[1]
    for p in range(1, q):
        first, second = lent[2 * p - 2 : 2 * p]
        block = pair[partner(own, p, q)]
        first[...] = block[: side // 2]
        second[: side // 2] = block[side // 2 :]
        second[side // 2 :] = marks[partner(own, p, q)]


def prepare_kernel(q, p, *refs):
    if p:
        first, second, refs = refs[0], refs[1], refs[2:]
        side = 2 * first.shape[0]
        edge = second.shape[0] - first.shape[0]
        flat = jnp.concatenate([first[...], second[: side // 2]], axis=0)
        mark = second[side // 2 :]
    else:
        own = lax.rem(lax.axis_index("row"), q)
        side, edge = refs[0].shape[1], refs[1].shape[1]
        flat, mark, refs = refs[0][own], refs[1][own], refs[2:]
    w_gate, w_up, w_out, w_head, inputs_t, updated_t, hidden, slope, swish, logits, onehot, normed, scale = refs
    width, bins = flat.shape[1], w_head.shape[0]
    normal, scale_inv = normalize(flat)
    normed[...] = normal
    scale[...] = jnp.broadcast_to(scale_inv, normal.shape)
    inputs = normal.astype(bf16)
    inputs_t[...] = inputs.T
    total = flat.astype(f32)
    for at, step in chunks_of(w_gate.shape[1], 256):
        span = slice(at, at + step)
        half = nn(inputs, w_gate[:, span] * 0.5)
        upper = nn(inputs, w_up[:, span])
        curve = jnp.tanh(half)
        raised = 1.0 + curve
        swished = half * raised
        hidden_part = (swished * upper).astype(bf16)
        swish[:, span] = swished
        hidden[:, span] = hidden_part
        slope[:, span] = upper * (0.5 * raised) * (1.0 + half * (1.0 - curve))
        total = total + nn(hidden_part, w_out[span, :])
    upd = total.astype(bf16)
    updated_t[...] = upd.T
    logits[...] = nt(upd, w_head[...]).astype(bf16)
    shift = edge.bit_length() - 1
    rows = lax.broadcasted_iota(jnp.int32, (side, edge), 0) >> shift
    pick = jnp.where(rows == lax.broadcasted_iota(jnp.int32, (side, edge), 1), 1.0, 0.0).astype(bf16)
    columns = lax.broadcasted_iota(jnp.int32, (side, width), 0) & (edge - 1)
    mask = columns == lax.broadcasted_iota(jnp.int32, (side, width), 1)
    lanes = lax.broadcasted_iota(jnp.int32, (side, bins), 1).astype(f32)
    picked = jnp.where(mask, nn(pick, mark), 0.0).astype(bf16)
    wanted = nn(picked, jnp.ones((width, bins), bf16))
    onehot[...] = jnp.where(wanted == lanes, 1.0, 0.0)


def backward_kernel(q, packed, *refs):
    blocks, (w_out, w_head, far, near), rest = [refs[7 * p : 7 * p + 7] for p in range(q)], refs[7 * q : 7 * q + 4], refs[7 * q + 4 :]
    (d_updated, d_gate, d_up), hot, mirrored = rest[:3], rest[3:-1], rest[-1]
    (width, side), units, bins = blocks[0][0].shape, w_out.shape[0], w_head.shape[0]
    packs = lane_packs(bins, side)
    own = lax.rem(lax.axis_index("row"), q)
    inside = lax.axis_index("row") // q == lax.axis_index("col")

    @pl.when(inside)
    def _():
        mirrored[...] = near[...]

    @pl.when(jnp.logical_not(inside))
    def _():
        mirrored[...] = far[...]

    inputs_t, updated_t, hidden, slope, swish, logits, onehot = zip(*blocks)
    mirror = jnp.concatenate([mirrored[p, :, u * bins : (u + 1) * bins] for p in range(q) for u in range(packs)], axis=0)
    summed = joined(logits, 0).astype(f32) + mirror.astype(f32)
    powers = jnp.exp(summed - jnp.max(summed, axis=-1, keepdims=True))
    probs = powers / row_sums(powers)
    grad_sym = (probs - joined(onehot, 0)).astype(bf16)
    cotangent = (grad_sym.astype(f32) * 2.0).astype(bf16)
    d_upd = nn(cotangent, w_head[...])
    d_updated[...] = d_upd
    d_upd_b = d_upd.astype(bf16)
    for p in range(q):
        for top, tall in chunks_of(side, 128):
            row = slice(p * side + top, p * side + top + tall)
            for at, step in chunks_of(units, 256):
                span = slice(at, at + step)
                d_hidden = nt(d_upd_b[row], w_out[span, :])
                d_gate[row, span] = (d_hidden * slope[p][top : top + tall, span]).astype(bf16)
                d_up[row, span] = (d_hidden * swish[p][top : top + tall, span]).astype(bf16)
    depth = joined(inputs_t, 1)
    totals = (
        nn(depth, d_gate[...]),
        nn(depth, d_up[...]),
        nn(d_upd_b.T, joined(hidden, 0)),
        nn(joined(updated_t, 1), cotangent),
    )
    if not packed:
        for ref, term in zip(hot, totals):
            ref[...] = term.astype(ref.dtype)
        return
    gate_term, up_term, out_term, head_term = totals
    hot, slots = hot[:-1], hot[-1]
    nrow, ncol = packed
    groups = nrow // q
    lanes, part, tall = units // ncol, width // nrow, units // nrow
    narrow = width // ncol
    fold = lanes // tall
    short = narrow // fold
    for k in range(q):
        for a in range(groups):
            r = a * q + k
            for c in range(ncol):
                for n, term in enumerate((gate_term, up_term)):
                    block = term[r * part : (r + 1) * part, c * lanes : (c + 1) * lanes]
                    slots[k, a, (n * ncol + c) * part : (n * ncol + c + 1) * part] = block.astype(bf16)
                at = 2 * ncol * part + c * short
                block = out_term[c * narrow : (c + 1) * narrow, r * tall : (r + 1) * tall]
                block = jnp.concatenate([block[v * short : (v + 1) * short] for v in range(fold)], axis=1)
                slots[k, a, at : at + short] = block.astype(bf16)
            at = 2 * ncol * part + ncol * short
            block = head_term[r * part : (r + 1) * part, :]
            block = jnp.concatenate([block, jnp.zeros((part, lanes - bins), f32)], axis=1)
            slots[k, a, at : at + part] = block.astype(bf16)
    mine, level = lax.axis_index("row") // q, lax.axis_index("col")
    at = 2 * ncol * part + ncol * short
    lane = lax.broadcasted_iota(jnp.int32, (part, lanes), 1)
    here = (lane >= level * (bins // ncol)) & (lane < (level + 1) * (bins // ncol))
    for n in range(q):
        core = partner(own, n, q)
        for a in range(groups):
            same = jnp.where(mine == a, crossed(core, q), core)
            other = jnp.where(mine == a, core, crossed(core, q))
            for c in range(ncol):
                k = jnp.where(level == c, other, same)
                for m in (c, ncol + c):
                    hot[n][a, m * part : (m + 1) * part] = slots[k, a, m * part : (m + 1) * part]
                row = slice(2 * ncol * part + c * short, 2 * ncol * part + (c + 1) * short)
                hot[n][a, row] = slots[k, a, row]
            head = jnp.where(here, slots[other, a, at : at + part].astype(f32), slots[same, a, at : at + part].astype(f32))
            hot[n][a, at : at + part] = head.astype(bf16)


def input_kernel(p, d_updated, d_gate, d_up, normed, scale, w_gate, w_up, result):
    side = result.shape[0]
    row = slice(p * side, (p + 1) * side)
    d_inputs = nt(d_gate[row], w_gate[...]) + nt(d_up[row], w_up[...])
    normal = normed[...]
    d_norm = (
        d_inputs
        - jnp.mean(d_inputs, axis=-1, keepdims=True)
        - normal * jnp.mean(d_inputs * normal, axis=-1, keepdims=True)
    ) * scale[...]
    result[...] = (d_updated[row] + d_norm).astype(bf16)


def place_kernel(q, *refs):
    blocks, d_pair = refs[:-1], refs[-1]
    edge, _, _, width = d_pair.shape
    own = lax.rem(lax.axis_index("row"), q)
    d_pair[:, own] = blocks[0][...].reshape(edge, edge, width)
    for p in range(1, q):
        for n, half in enumerate((slice(0, edge // 2), slice(edge // 2, edge))):
            d_pair[half, partner(own, p, q)] = blocks[2 * p - 1 + n][...].reshape(edge // 2, edge, width)


def core_sum_kernel(q, groups, *rest):
    terms, blocks, hot, handed = rest[:q], rest[q : 2 * q - 1], rest[2 * q - 1 : 2 - 2 * q], rest[2 - 2 * q :]
    mine = lax.axis_index("row") // q
    for p in range(groups):
        a = following(mine, p, groups)
        total = terms[0][a].astype(f32)
        for term in terms[1:]:
            total = total + term[a].astype(f32)
        hot[p][...] = total.astype(bf16)
    for p, block in enumerate(blocks):
        half = block.shape[0] // 2
        handed[2 * p][...] = block[:half]
        handed[2 * p + 1][...] = block[half:]


def chip_sum_kernel(q, groups, ncol, shapes, *rest):
    terms, hot, slots = rest[:groups], rest[groups:-1], rest[-1]
    part, lanes, short, tall, few = shapes
    total = terms[0][...].astype(f32)
    for term in terms[1:]:
        total = total + term[...].astype(f32)
    at = 2 * ncol * part
    head = total[at + ncol * short : at + ncol * short + part]
    for c in range(ncol):
        slots[c, 0:part] = total[c * part : (c + 1) * part].astype(bf16)
        slots[c, part : 2 * part] = total[(ncol + c) * part : (ncol + c + 1) * part].astype(bf16)
        slots[c, 2 * part : 2 * part + short] = total[at + c * short : at + (c + 1) * short].astype(bf16)
        piece = jnp.concatenate([head[:, c * few : (c + 1) * few], jnp.zeros((part, lanes - few), f32)], axis=1)
        slots[c, 2 * part + short : 3 * part + short] = piece.astype(bf16)
    for p in range(ncol):
        hot[p][...] = slots[partner(lax.axis_index("col"), p, ncol)]


def col_sum_kernel(shapes, factor, *rest):
    terms, (gate, up, out, head) = rest[:-4], rest[-4:]
    part, lanes, tall, few = shapes
    total = terms[0][...].astype(f32)
    for term in terms[1:]:
        total = total + term[...].astype(f32)
    total = total * factor
    fold = lanes // tall
    short = out.shape[0] // fold
    gate[...] = total[0:part]
    up[...] = total[part : 2 * part]
    for v in range(fold):
        out[v * short : (v + 1) * short, :] = total[2 * part : 2 * part + short, v * tall : (v + 1) * tall]
    head[...] = total[2 * part + short : 3 * part + short, 0:few]


def core_pairs(nrow, q, p):
    return [(s, s - s % q + partner(s % q, p, q)) for s in range(nrow)]


def shaped(shape, kind):
    return jax.ShapeDtypeStruct(shape, kind)


def cost(flops, moved):
    return pl.CostEstimate(flops=flops, bytes_accessed=moved, transcendentals=0)


def body(pair, targets, w_gate, w_up, w_out, w_head):
    rows, cols, width = pair.shape
    units = w_gate.shape[1]
    bins = w_head.shape[1]
    nrow, ncol = lax.axis_size("row"), lax.axis_size("col")
    q = nrow // ncol
    groups = nrow // q
    side = rows * cols // q
    packs = lane_packs(bins, side)
    head_t = w_head.T
    piece = (side // packs, bins * packs)

    sources = (pair, w_gate, w_up, w_out, head_t, targets)
    pair, w_gate, w_up, w_out, head_t, marks, sends = pl.pallas_call(
        functools.partial(forward_kernel, q),
        out_shape=[shaped((q, side, width), bf16)]
        + [shaped(x.shape, bf16) for x in sources[1:5]]
        + [shaped((q, rows, width), bf16), shaped((q, *piece), bf16)],
        in_specs=[HBM] * 6,
        out_specs=[VMEM] * 7,
        scratch_shapes=[
            pltpu.VMEM((rows, cols), jnp.int32),
            pltpu.VMEM((q, *piece), bf16),
            pltpu.VMEM((q * side, units), bf16),
            pltpu.SemaphoreType.DMA((5 + q,)),
        ],
        compiler_params=PARAMS,
        name="forward",
    )(*(pltpu.with_memory_space_constraint(x, pltpu.HBM) for x in sources))

    pairs = [
        (r * ncol + c, (q * c + (partner(r % q, 1, q) if q == 2 and r // q == c else r % q)) * ncol + r // q)
        for r in range(nrow)
        for c in range(ncol)
    ]
    far = lax.ppermute(sends, ("row", "col"), pairs)
    lent = pl.pallas_call(
        functools.partial(lend_kernel, q),
        out_shape=[shaped((side // 2, width), bf16), shaped((side // 2 + rows, width), bf16)] * (q - 1),
        in_specs=[VMEM] * 2,
        out_specs=[VMEM] * (2 * q - 2),
        compiler_params=PARAMS,
        name="lend",
    )(pair, marks)
    borrowed = [lax.ppermute(x, "row", core_pairs(nrow, q, n // 2 + 1)) for n, x in enumerate(lent)]
    prepared = []
    for p in range(q):
        source = borrowed[2 * p - 2 : 2 * p] if p else (pair, marks)
        prepared.append(
            pl.pallas_call(
                functools.partial(prepare_kernel, q, p),
                out_shape=[
                    shaped((width, side), bf16),
                    shaped((width, side), bf16),
                    shaped((side, units), bf16),
                    shaped((side, units), f32),
                    shaped((side, units), f32),
                    shaped((side, bins), bf16),
                    shaped((side, bins), f32),
                    shaped((side, width), f32),
                    shaped((side, width), f32),
                ],
                in_specs=[VMEM] * (len(source) + 4),
                out_specs=[VMEM] * 9,
                compiler_params=PARAMS,
                cost_estimate=cost(0, 0) if p else cost(6 * side * width * units, 8 * side * units),
                name="prepare",
            )(*source, w_gate, w_up, w_out, head_t)
        )

    part, tall, few = width // nrow, units // nrow, bins // ncol
    lanes = units // ncol
    short = width // ncol * tall // lanes
    fits = part % 16 == 0 and lanes == 128 and lanes % tall == 0 and bins <= lanes and short % 16 == 0
    height = 2 * ncol * part + ncol * short + part
    if fits:
        hot_shapes = [shaped((groups, height, lanes), bf16)] * q
        scratch = [pltpu.VMEM((q, groups, height, lanes), bf16)]
    else:
        hot_shapes = [shaped((width, n), bf16) for n in (units, units, units, bins)]
        scratch = []
    results = pl.pallas_call(
        functools.partial(backward_kernel, q, (nrow, ncol) if fits else None),
        out_shape=[shaped((q * side, width), f32)] + [shaped((q * side, units), bf16)] * 2 + hot_shapes,
        in_specs=[VMEM] * (7 * q + 4),
        out_specs=[VMEM] * (3 + len(hot_shapes)),
        scratch_shapes=scratch + [pltpu.VMEM((q, *piece), bf16)],
        compiler_params=PARAMS,
        cost_estimate=cost(8 * q * side * width * units, 4 * q * side * units),
        name="backward",
    )(*(x for block in prepared for x in block[:7]), w_out, head_t, far, sends)
    hot = list(results[3:])

    def d_inputs(p):
        return pl.pallas_call(
            functools.partial(input_kernel, p),
            out_shape=shaped((side, width), bf16),
            in_specs=[VMEM] * 7,
            out_specs=VMEM,
            compiler_params=PARAMS,
            cost_estimate=cost(4 * side * width * units, 4 * side * units),
            name="d_inputs",
        )(*results[:3], *prepared[p][7:], w_gate, w_up)

    d_blocks = [d_inputs(p) for p in range(q)]

    def returned(blocks):
        moved = [lax.ppermute(x, "row", core_pairs(nrow, q, n // 2 + 1)) for n, x in enumerate(blocks[1:])]
        return blocks[:1] + moved

    def placed(blocks):
        return pl.pallas_call(
            functools.partial(place_kernel, q),
            out_shape=shaped((rows, q, cols // q, width), bf16),
            in_specs=[VMEM] * (2 * q - 1),
            out_specs=VMEM,
            compiler_params=PARAMS,
            name="place",
        )(*blocks).reshape(rows, cols, width)

    factor = 1.0 / (rows * nrow)
    if not fits:
        owned = []
        hot[2] = hot[2].T
        for term in hot:
            mine = lax.psum_scatter(term, "row", scatter_dimension=0, tiled=True).astype(f32)
            owned.append(lax.psum_scatter(mine, "col", scatter_dimension=1, tiled=True) * factor)
        d_blocks = d_blocks[:1] + [half for block in d_blocks[1:] for half in (block[: side // 2], block[side // 2 :])]
        return (placed(returned(d_blocks)), *owned)

    terms = [hot[0]]
    for p in range(1, q):
        terms.append(lax.ppermute(hot[p], "row", core_pairs(nrow, q, p)))
    terms, d_blocks = lax.optimization_barrier((terms, d_blocks))
    hot = pl.pallas_call(
        functools.partial(core_sum_kernel, q, groups),
        out_shape=[shaped((height, lanes), bf16)] * groups + [shaped((side // 2, width), bf16)] * (2 * q - 2),
        in_specs=[VMEM] * (2 * q - 1),
        out_specs=[VMEM] * (groups + 2 * q - 2),
        compiler_params=PARAMS,
        name="core_sum",
    )(*terms, *d_blocks[1:])
    hot, d_blocks = hot[:groups], d_blocks[:1] + list(hot[groups:])
    terms = [hot[0]]
    for p in range(1, groups):
        terms.append(lax.ppermute(hot[p], "row", [(s, following(s // q, p, groups) * q + crossed(s % q, q)) for s in range(nrow)]))
    terms, d_blocks = lax.optimization_barrier((terms, returned(d_blocks)))
    low = 3 * part + short
    hot = pl.pallas_call(
        functools.partial(chip_sum_kernel, q, groups, ncol, (part, lanes, short, tall, few)),
        out_shape=[shaped((low, lanes), bf16)] * ncol,
        in_specs=[VMEM] * groups,
        out_specs=[VMEM] * ncol,
        scratch_shapes=[pltpu.VMEM((ncol, low, lanes), bf16)],
        compiler_params=PARAMS,
        name="chip_sum",
    )(*terms)
    terms = [hot[0]]
    for p in sorted(range(1, ncol), key=lambda p: (p != ncol // 2, -p)):
        pairs = [
            (r * ncol + c, (r - r % q + crossed(r % q, q)) * ncol + partner(c, p, ncol))
            for r in range(nrow)
            for c in range(ncol)
        ]
        terms.append(lax.ppermute(hot[p], ("row", "col"), pairs))
    *terms, d_pair = lax.optimization_barrier((*terms, placed(d_blocks)))
    gate, up, out, head = pl.pallas_call(
        functools.partial(col_sum_kernel, (part, lanes, tall, few), factor),
        out_shape=[
            shaped((part, lanes), f32),
            shaped((part, lanes), f32),
            shaped((width // ncol, tall), f32),
            shaped((part, few), f32),
        ],
        in_specs=[VMEM] * ncol,
        out_specs=[VMEM] * 4,
        compiler_params=PARAMS,
        name="col_sum",
    )(*terms)
    return d_pair, gate, up, out.T, head


def solution(mesh):
    placed = (P("row", "col", None), P("row", "col"), P(), P(), P(), P())
    return jax.shard_map(
        body,
        mesh=mesh,
        in_specs=placed,
        out_specs=(P("row", "col", None), P("row", "col"), P("row", "col"), P("row", "col"), P("row", "col")),
        check_vma=False,
    )
```

```python
import functools

import jax
import jax.numpy as jnp
from jax import lax
from jax.experimental import pallas as pl
from jax.experimental.pallas import tpu as pltpu
from jax.sharding import PartitionSpec as P

eps = 1e-05
f32 = jnp.float32
bf16 = jnp.bfloat16
HBM = pl.BlockSpec(memory_space=pltpu.HBM)
VMEM = pl.BlockSpec(memory_space=pltpu.VMEM)
PARAMS = pltpu.CompilerParams(vmem_limit_bytes=24 * 1024 * 1024)


def nn(a, b):
    return lax.dot_general(a, b, (((1,), (0,)), ((), ())), preferred_element_type=f32)


def nt(a, b):
    return lax.dot_general(a, b, (((1,), (1,)), ((), ())), preferred_element_type=f32)


def tn(a, b):
    return lax.dot_general(a, b, (((0,), (0,)), ((), ())), preferred_element_type=f32)


def normalize(flat):
    values = flat.astype(f32)
    centre = values - jnp.mean(values, axis=-1, keepdims=True)
    scale_inv = lax.rsqrt(jnp.mean(centre * centre, axis=-1, keepdims=True) + eps)
    return centre * scale_inv, scale_inv


def exchange(side):
    edge = 1
    while edge * edge < side:
        edge *= 2
    shift = edge.bit_length() - 1
    out_row = lax.broadcasted_iota(jnp.int32, (side, side), 0)
    in_row = lax.broadcasted_iota(jnp.int32, (side, side), 1)
    return jnp.where(in_row == (((out_row & (edge - 1)) << shift) | (out_row >> shift)), 1.0, 0.0).astype(bf16)


def chunks_of(size, most):
    step = most if size % most == 0 else size
    return [(at, step) for at in range(0, size, step)]


def partner(s, p, n):
    if n & (n - 1) == 0:
        return s ^ p
    return (s + p) % n if isinstance(s, int) else lax.rem(s + p, n)


def crossed(k, q):
    return partner(k, 1, q) if q > 1 else k


def following(s, p, n):
    return (s + p) % n if isinstance(s, int) else lax.rem(s + p, n)


def joined(refs, axis):
    return jnp.concatenate([ref[...] for ref in refs], axis=axis)


def lane_packs(bins, side):
    packs = max(1, 128 // bins)
    return packs if (side // packs) % 16 == 0 else 1


def forward_kernel(q, *refs):
    sources, (pair, w_gate, w_up, w_out, w_head, marks, sends), scratch = refs[:6], refs[6:13], refs[13:]
    targets, halves, hidden, sems = scratch
    _, side, width = pair.shape
    edge = sources[0].shape[0]
    bins = w_head.shape[0]
    copies = [
        pltpu.make_async_copy(source, target, sems.at[i])
        for i, (source, target) in enumerate(zip(sources[1:], (w_gate, w_up, w_out, w_head, targets)))
    ]
    pieces = [
        pltpu.make_async_copy(
            sources[0].at[:, h * edge : (h + 1) * edge, :], pair.reshape(q, edge, edge, width).at[h], sems.at[5 + h]
        )
        for h in range(q)
    ]
    for copy in pieces + copies:
        copy.start()
    own = lax.rem(lax.axis_index("row"), q)
    for copy in pieces:
        copy.wait()
    flat = pair[...].reshape(q * side, width)
    inputs = normalize(flat)[0].astype(bf16)
    for copy in copies[:2]:
        copy.wait()
    for at, step in chunks_of(w_gate.shape[1], 256):
        w_half = w_gate[:, at : at + step] * 0.5
        for top, tall in chunks_of(q * side, 512):
            half = nn(inputs[top : top + tall], w_half)
            upper = nn(inputs[top : top + tall], w_up[:, at : at + step])
            hidden[top : top + tall, at : at + step] = (half * (1.0 + jnp.tanh(half)) * upper).astype(bf16)
    for copy in copies[2:]:
        copy.wait()
    total = flat.astype(f32) + nn(hidden[...], w_out[...])
    logit = nt(total.astype(bf16), w_head[...]).astype(bf16)
    packs = lane_packs(bins, side)
    deep = side // packs
    for h in range(q):
        piece = logit[h * side : (h + 1) * side]
        if packs > 1:
            piece = jnp.concatenate([piece[u * deep : (u + 1) * deep] for u in range(packs)], axis=1)
        halves[h] = piece
        mark = targets[:, h * edge : (h + 1) * edge].astype(f32)
        marks[h] = jnp.concatenate([mark, jnp.zeros((edge, width - edge), f32)], axis=1).astype(bf16)
    for p in range(q):
        sends[p] = halves[partner(own, p, q)]


def lend_kernel(q, pair, marks, *lent):
    own = lax.rem(lax.axis_index("row"), q)
    side = pair.shape[1]
    for p in range(1, q):
        first, second = lent[2 * p - 2 : 2 * p]
        block = pair[partner(own, p, q)]
        first[...] = block[: side // 2]
        second[: side // 2] = block[side // 2 :]
        second[side // 2 :] = marks[partner(own, p, q)]


def prepare_kernel(q, p, *refs):
    if p:
        first, second, refs = refs[0], refs[1], refs[2:]
        side = 2 * first.shape[0]
        edge = second.shape[0] - first.shape[0]
        flat = jnp.concatenate([first[...], second[: side // 2]], axis=0)
        mark = second[side // 2 :]
    else:
        own = lax.rem(lax.axis_index("row"), q)
        side, edge = refs[0].shape[1], refs[1].shape[1]
        flat, mark, refs = refs[0][own], refs[1][own], refs[2:]
    w_gate, w_up, w_out, w_head, inputs_t, updated_t, hidden, slope, swish, logits, onehot, normed, scale = refs
    width, bins = flat.shape[1], w_head.shape[0]
    flat = nn(exchange(side), flat).astype(bf16)
    normal, scale_inv = normalize(flat)
    normed[...] = normal
    scale[...] = jnp.broadcast_to(scale_inv, normal.shape)
    inputs = normal.astype(bf16)
    inputs_t[...] = inputs.T
    total = flat.astype(f32)
    for at, step in chunks_of(w_gate.shape[1], 256):
        span = slice(at, at + step)
        half = nn(inputs, w_gate[:, span] * 0.5)
        upper = nn(inputs, w_up[:, span])
        curve = jnp.tanh(half)
        raised = 1.0 + curve
        swished = half * raised
        hidden_part = (swished * upper).astype(bf16)
        swish[:, span] = swished
        hidden[:, span] = hidden_part
        slope[:, span] = upper * (0.5 * raised) * (1.0 + half * (1.0 - curve))
        total = total + nn(hidden_part, w_out[span, :])
    upd = total.astype(bf16)
    updated_t[...] = upd.T
    logits[...] = nt(upd, w_head[...]).astype(bf16)
    shift = edge.bit_length() - 1
    rows = lax.broadcasted_iota(jnp.int32, (side, edge), 0) & (edge - 1)
    pick = jnp.where(rows == lax.broadcasted_iota(jnp.int32, (side, edge), 1), 1.0, 0.0).astype(bf16)
    columns = lax.broadcasted_iota(jnp.int32, (side, width), 0) >> shift
    mask = columns == lax.broadcasted_iota(jnp.int32, (side, width), 1)
    lanes = lax.broadcasted_iota(jnp.int32, (side, bins), 1).astype(f32)
    picked = jnp.where(mask, nn(pick, mark), 0.0).astype(bf16)
    wanted = nn(picked, jnp.ones((width, bins), bf16))
    onehot[...] = jnp.where(wanted == lanes, 1.0, 0.0)


def backward_kernel(q, packed, *refs):
    blocks, (w_out, w_head, far, near), rest = [refs[7 * p : 7 * p + 7] for p in range(q)], refs[7 * q : 7 * q + 4], refs[7 * q + 4 :]
    (d_updated, d_gate, d_up), hot, mirrored = rest[:3], rest[3:-1], rest[-1]
    (width, side), units, bins = blocks[0][0].shape, w_out.shape[0], w_head.shape[0]
    packs = lane_packs(bins, side)
    own = lax.rem(lax.axis_index("row"), q)
    inside = lax.axis_index("row") // q == lax.axis_index("col")

    @pl.when(inside)
    def _():
        mirrored[...] = near[...]

    @pl.when(jnp.logical_not(inside))
    def _():
        mirrored[...] = far[...]

    inputs_t, updated_t, hidden, slope, swish, logits, onehot = zip(*blocks)
    mirror = jnp.concatenate([mirrored[p, :, u * bins : (u + 1) * bins] for p in range(q) for u in range(packs)], axis=0)
    summed = joined(logits, 0).astype(f32) + mirror.astype(f32)
    powers = jnp.exp(summed - jnp.max(summed, axis=-1, keepdims=True))
    probs = powers / jnp.sum(powers, axis=-1, keepdims=True)
    grad_sym = (probs - joined(onehot, 0)).astype(bf16)
    cotangent = (grad_sym.astype(f32) * 2.0).astype(bf16)
    d_upd = nn(cotangent, w_head[...])
    d_updated[...] = d_upd
    d_upd_b = d_upd.astype(bf16)
    for p in range(q):
        for top, tall in chunks_of(side, 128):
            row = slice(p * side + top, p * side + top + tall)
            for at, step in chunks_of(units, 256):
                span = slice(at, at + step)
                d_hidden = nt(d_upd_b[row], w_out[span, :])
                d_gate[row, span] = (d_hidden * slope[p][top : top + tall, span]).astype(bf16)
                d_up[row, span] = (d_hidden * swish[p][top : top + tall, span]).astype(bf16)
    depth = joined(inputs_t, 1)
    totals = (
        nn(depth, d_gate[...]),
        nn(depth, d_up[...]),
        nn(d_upd_b.T, joined(hidden, 0)),
        nn(joined(updated_t, 1), cotangent),
    )
    if not packed:
        for ref, term in zip(hot, totals):
            ref[...] = term.astype(ref.dtype)
        return
    gate_term, up_term, out_term, head_term = totals
    hot, slots = hot[:-1], hot[-1]
    nrow, ncol = packed
    groups = nrow // q
    lanes, part, tall = units // ncol, width // nrow, units // nrow
    narrow = width // ncol
    fold = lanes // tall
    short = narrow // fold
    for k in range(q):
        for a in range(groups):
            r = a * q + k
            for c in range(ncol):
                for n, term in enumerate((gate_term, up_term)):
                    block = term[r * part : (r + 1) * part, c * lanes : (c + 1) * lanes]
                    slots[k, a, (n * ncol + c) * part : (n * ncol + c + 1) * part] = block.astype(bf16)
                at = 2 * ncol * part + c * short
                block = out_term[c * narrow : (c + 1) * narrow, r * tall : (r + 1) * tall]
                block = jnp.concatenate([block[v * short : (v + 1) * short] for v in range(fold)], axis=1)
                slots[k, a, at : at + short] = block.astype(bf16)
            at = 2 * ncol * part + ncol * short
            block = head_term[r * part : (r + 1) * part, :]
            block = jnp.concatenate([block, jnp.zeros((part, lanes - bins), f32)], axis=1)
            slots[k, a, at : at + part] = block.astype(bf16)
    mine, level = lax.axis_index("row") // q, lax.axis_index("col")
    at = 2 * ncol * part + ncol * short
    lane = lax.broadcasted_iota(jnp.int32, (part, lanes), 1)
    here = (lane >= level * (bins // ncol)) & (lane < (level + 1) * (bins // ncol))
    for n in range(q):
        core = partner(own, n, q)
        for a in range(groups):
            same = jnp.where(mine == a, crossed(core, q), core)
            other = jnp.where(mine == a, core, crossed(core, q))
            for c in range(ncol):
                k = jnp.where(level == c, other, same)
                for m in (c, ncol + c):
                    hot[n][a, m * part : (m + 1) * part] = slots[k, a, m * part : (m + 1) * part]
                row = slice(2 * ncol * part + c * short, 2 * ncol * part + (c + 1) * short)
                hot[n][a, row] = slots[k, a, row]
            head = jnp.where(here, slots[other, a, at : at + part].astype(f32), slots[same, a, at : at + part].astype(f32))
            hot[n][a, at : at + part] = head.astype(bf16)


def input_kernel(p, d_updated, d_gate, d_up, normed, scale, w_gate, w_up, result):
    side = result.shape[0]
    row = slice(p * side, (p + 1) * side)
    d_inputs = nt(d_gate[row], w_gate[...]) + nt(d_up[row], w_up[...])
    normal = normed[...]
    d_norm = (
        d_inputs
        - jnp.mean(d_inputs, axis=-1, keepdims=True)
        - normal * jnp.mean(d_inputs * normal, axis=-1, keepdims=True)
    ) * scale[...]
    result[...] = nn(exchange(side), (d_updated[row] + d_norm).astype(bf16)).astype(bf16)


def place_kernel(q, *refs):
    blocks, d_pair = refs[:-1], refs[-1]
    edge, _, _, width = d_pair.shape
    own = lax.rem(lax.axis_index("row"), q)
    d_pair[:, own] = blocks[0][...].reshape(edge, edge, width)
    for p in range(1, q):
        for n, half in enumerate((slice(0, edge // 2), slice(edge // 2, edge))):
            d_pair[half, partner(own, p, q)] = blocks[2 * p - 1 + n][...].reshape(edge // 2, edge, width)


def core_sum_kernel(q, groups, *rest):
    terms, blocks, hot, handed = rest[:q], rest[q : 2 * q - 1], rest[2 * q - 1 : 2 - 2 * q], rest[2 - 2 * q :]
    mine = lax.axis_index("row") // q
    for p in range(groups):
        a = following(mine, p, groups)
        total = terms[0][a].astype(f32)
        for term in terms[1:]:
            total = total + term[a].astype(f32)
        hot[p][...] = total.astype(bf16)
    for p, block in enumerate(blocks):
        half = block.shape[0] // 2
        handed[2 * p][...] = block[:half]
        handed[2 * p + 1][...] = block[half:]


def chip_sum_kernel(q, groups, ncol, shapes, *rest):
    terms, hot, slots = rest[:groups], rest[groups:-1], rest[-1]
    part, lanes, short, tall, few = shapes
    total = terms[0][...].astype(f32)
    for term in terms[1:]:
        total = total + term[...].astype(f32)
    at = 2 * ncol * part
    head = total[at + ncol * short : at + ncol * short + part]
    for c in range(ncol):
        slots[c, 0:part] = total[c * part : (c + 1) * part].astype(bf16)
        slots[c, part : 2 * part] = total[(ncol + c) * part : (ncol + c + 1) * part].astype(bf16)
        slots[c, 2 * part : 2 * part + short] = total[at + c * short : at + (c + 1) * short].astype(bf16)
        piece = jnp.concatenate([head[:, c * few : (c + 1) * few], jnp.zeros((part, lanes - few), f32)], axis=1)
        slots[c, 2 * part + short : 3 * part + short] = piece.astype(bf16)
    for p in range(ncol):
        hot[p][...] = slots[partner(lax.axis_index("col"), p, ncol)]


def col_sum_kernel(shapes, factor, *rest):
    terms, (gate, up, out, head) = rest[:-4], rest[-4:]
    part, lanes, tall, few = shapes
    total = terms[0][...].astype(f32)
    for term in terms[1:]:
        total = total + term[...].astype(f32)
    total = total * factor
    fold = lanes // tall
    short = out.shape[0] // fold
    gate[...] = total[0:part]
    up[...] = total[part : 2 * part]
    for v in range(fold):
        out[v * short : (v + 1) * short, :] = total[2 * part : 2 * part + short, v * tall : (v + 1) * tall]
    head[...] = total[2 * part + short : 3 * part + short, 0:few]


def core_pairs(nrow, q, p):
    return [(s, s - s % q + partner(s % q, p, q)) for s in range(nrow)]


def shaped(shape, kind):
    return jax.ShapeDtypeStruct(shape, kind)


def cost(flops, moved):
    return pl.CostEstimate(flops=flops, bytes_accessed=moved, transcendentals=0)


def body(pair, targets, w_gate, w_up, w_out, w_head):
    rows, cols, width = pair.shape
    units = w_gate.shape[1]
    bins = w_head.shape[1]
    nrow, ncol = lax.axis_size("row"), lax.axis_size("col")
    q = nrow // ncol
    groups = nrow // q
    side = rows * cols // q
    packs = lane_packs(bins, side)
    head_t = w_head.T
    piece = (side // packs, bins * packs)

    sources = (pair, w_gate, w_up, w_out, head_t, targets)
    pair, w_gate, w_up, w_out, head_t, marks, sends = pl.pallas_call(
        functools.partial(forward_kernel, q),
        out_shape=[shaped((q, side, width), bf16)]
        + [shaped(x.shape, bf16) for x in sources[1:5]]
        + [shaped((q, rows, width), bf16), shaped((q, *piece), bf16)],
        in_specs=[HBM] * 6,
        out_specs=[VMEM] * 7,
        scratch_shapes=[
            pltpu.VMEM((rows, cols), jnp.int32),
            pltpu.VMEM((q, *piece), bf16),
            pltpu.VMEM((q * side, units), bf16),
            pltpu.SemaphoreType.DMA((5 + q,)),
        ],
        compiler_params=PARAMS,
        name="forward",
    )(*(pltpu.with_memory_space_constraint(x, pltpu.HBM) for x in sources))

    pairs = [
        (r * ncol + c, (q * c + (partner(r % q, 1, q) if q == 2 and r // q == c else r % q)) * ncol + r // q)
        for r in range(nrow)
        for c in range(ncol)
    ]
    far = lax.ppermute(sends, ("row", "col"), pairs)
    lent = pl.pallas_call(
        functools.partial(lend_kernel, q),
        out_shape=[shaped((side // 2, width), bf16), shaped((side // 2 + rows, width), bf16)] * (q - 1),
        in_specs=[VMEM] * 2,
        out_specs=[VMEM] * (2 * q - 2),
        compiler_params=PARAMS,
        name="lend",
    )(pair, marks)
    borrowed = [lax.ppermute(x, "row", core_pairs(nrow, q, n // 2 + 1)) for n, x in enumerate(lent)]
    prepared = []
    for p in range(q):
        source = borrowed[2 * p - 2 : 2 * p] if p else (pair, marks)
        prepared.append(
            pl.pallas_call(
                functools.partial(prepare_kernel, q, p),
                out_shape=[
                    shaped((width, side), bf16),
                    shaped((width, side), bf16),
                    shaped((side, units), bf16),
                    shaped((side, units), f32),
                    shaped((side, units), f32),
                    shaped((side, bins), bf16),
                    shaped((side, bins), f32),
                    shaped((side, width), f32),
                    shaped((side, width), f32),
                ],
                in_specs=[VMEM] * (len(source) + 4),
                out_specs=[VMEM] * 9,
                compiler_params=PARAMS,
                cost_estimate=cost(0, 0) if p else cost(6 * side * width * units, 8 * side * units),
                name="prepare",
            )(*source, w_gate, w_up, w_out, head_t)
        )

    part, tall, few = width // nrow, units // nrow, bins // ncol
    lanes = units // ncol
    short = width // ncol * tall // lanes
    fits = part % 16 == 0 and lanes == 128 and lanes % tall == 0 and bins <= lanes and short % 16 == 0
    height = 2 * ncol * part + ncol * short + part
    if fits:
        hot_shapes = [shaped((groups, height, lanes), bf16)] * q
        scratch = [pltpu.VMEM((q, groups, height, lanes), bf16)]
    else:
        hot_shapes = [shaped((width, n), bf16) for n in (units, units, units, bins)]
        scratch = []
    results = pl.pallas_call(
        functools.partial(backward_kernel, q, (nrow, ncol) if fits else None),
        out_shape=[shaped((q * side, width), f32)] + [shaped((q * side, units), bf16)] * 2 + hot_shapes,
        in_specs=[VMEM] * (7 * q + 4),
        out_specs=[VMEM] * (3 + len(hot_shapes)),
        scratch_shapes=scratch + [pltpu.VMEM((q, *piece), bf16)],
        compiler_params=PARAMS,
        cost_estimate=cost(8 * q * side * width * units, 4 * q * side * units),
        name="backward",
    )(*(x for block in prepared for x in block[:7]), w_out, head_t, far, sends)
    hot = list(results[3:])

    def d_inputs(p):
        return pl.pallas_call(
            functools.partial(input_kernel, p),
            out_shape=shaped((side, width), bf16),
            in_specs=[VMEM] * 7,
            out_specs=VMEM,
            compiler_params=PARAMS,
            cost_estimate=cost(4 * side * width * units, 4 * side * units),
            name="d_inputs",
        )(*results[:3], *prepared[p][7:], w_gate, w_up)

    d_blocks = [d_inputs(p) for p in range(q)]

    def returned(blocks):
        moved = [lax.ppermute(x, "row", core_pairs(nrow, q, n // 2 + 1)) for n, x in enumerate(blocks[1:])]
        return blocks[:1] + moved

    def placed(blocks):
        return pl.pallas_call(
            functools.partial(place_kernel, q),
            out_shape=shaped((rows, q, cols // q, width), bf16),
            in_specs=[VMEM] * (2 * q - 1),
            out_specs=VMEM,
            compiler_params=PARAMS,
            name="place",
        )(*blocks).reshape(rows, cols, width)

    factor = 1.0 / (rows * nrow)
    if not fits:
        owned = []
        hot[2] = hot[2].T
        for term in hot:
            mine = lax.psum_scatter(term, "row", scatter_dimension=0, tiled=True).astype(f32)
            owned.append(lax.psum_scatter(mine, "col", scatter_dimension=1, tiled=True) * factor)
        d_blocks = d_blocks[:1] + [half for block in d_blocks[1:] for half in (block[: side // 2], block[side // 2 :])]
        return (placed(returned(d_blocks)), *owned)

    terms = [hot[0]]
    for p in range(1, q):
        terms.append(lax.ppermute(hot[p], "row", core_pairs(nrow, q, p)))
    terms, d_blocks = lax.optimization_barrier((terms, d_blocks))
    hot = pl.pallas_call(
        functools.partial(core_sum_kernel, q, groups),
        out_shape=[shaped((height, lanes), bf16)] * groups + [shaped((side // 2, width), bf16)] * (2 * q - 2),
        in_specs=[VMEM] * (2 * q - 1),
        out_specs=[VMEM] * (groups + 2 * q - 2),
        compiler_params=PARAMS,
        name="core_sum",
    )(*terms, *d_blocks[1:])
    hot, d_blocks = hot[:groups], d_blocks[:1] + list(hot[groups:])
    terms = [hot[0]]
    for p in range(1, groups):
        terms.append(lax.ppermute(hot[p], "row", [(s, following(s // q, p, groups) * q + crossed(s % q, q)) for s in range(nrow)]))
    terms, d_blocks = lax.optimization_barrier((terms, returned(d_blocks)))
    low = 3 * part + short
    hot = pl.pallas_call(
        functools.partial(chip_sum_kernel, q, groups, ncol, (part, lanes, short, tall, few)),
        out_shape=[shaped((low, lanes), bf16)] * ncol,
        in_specs=[VMEM] * groups,
        out_specs=[VMEM] * ncol,
        scratch_shapes=[pltpu.VMEM((ncol, low, lanes), bf16)],
        compiler_params=PARAMS,
        name="chip_sum",
    )(*terms)
    terms = [hot[0]]
    for p in sorted(range(1, ncol), key=lambda p: (p != ncol // 2, -p)):
        pairs = [
            (r * ncol + c, (r - r % q + crossed(r % q, q)) * ncol + partner(c, p, ncol))
            for r in range(nrow)
            for c in range(ncol)
        ]
        terms.append(lax.ppermute(hot[p], ("row", "col"), pairs))
    *terms, d_pair = lax.optimization_barrier((*terms, placed(d_blocks)))
    gate, up, out, head = pl.pallas_call(
        functools.partial(col_sum_kernel, (part, lanes, tall, few), factor),
        out_shape=[
            shaped((part, lanes), f32),
            shaped((part, lanes), f32),
            shaped((width // ncol, tall), f32),
            shaped((part, few), f32),
        ],
        in_specs=[VMEM] * ncol,
        out_specs=[VMEM] * 4,
        compiler_params=PARAMS,
        name="col_sum",
    )(*terms)
    return d_pair, gate, up, out.T, head


def solution(mesh):
    placed = (P("row", "col", None), P("row", "col"), P(), P(), P(), P())
    return jax.shard_map(
        body,
        mesh=mesh,
        in_specs=placed,
        out_specs=(P("row", "col", None), P("row", "col"), P("row", "col"), P("row", "col"), P("row", "col")),
        check_vma=False,
    )
```

```python
import functools

import jax
import jax.numpy as jnp
from jax import lax
from jax.experimental import pallas as pl
from jax.experimental.pallas import tpu as pltpu
from jax.sharding import PartitionSpec as P

eps = 1e-05
f32 = jnp.float32
bf16 = jnp.bfloat16
HBM = pl.BlockSpec(memory_space=pltpu.HBM)
VMEM = pl.BlockSpec(memory_space=pltpu.VMEM)
PARAMS = pltpu.CompilerParams(vmem_limit_bytes=24 * 1024 * 1024)


def nn(a, b):
    return lax.dot_general(a, b, (((1,), (0,)), ((), ())), preferred_element_type=f32)


def nt(a, b):
    return lax.dot_general(a, b, (((1,), (1,)), ((), ())), preferred_element_type=f32)


def tn(a, b):
    return lax.dot_general(a, b, (((0,), (0,)), ((), ())), preferred_element_type=f32)


def normalize(flat):
    values = flat.astype(f32)
    centre = values - jnp.mean(values, axis=-1, keepdims=True)
    scale_inv = lax.rsqrt(jnp.mean(centre * centre, axis=-1, keepdims=True) + eps)
    return centre * scale_inv, scale_inv


def exchange(side):
    edge = 1
    while edge * edge < side:
        edge *= 2
    shift = edge.bit_length() - 1
    out_row = lax.broadcasted_iota(jnp.int32, (side, side), 0)
    in_row = lax.broadcasted_iota(jnp.int32, (side, side), 1)
    return jnp.where(in_row == (((out_row & (edge - 1)) << shift) | (out_row >> shift)), 1.0, 0.0).astype(bf16)


def chunks_of(size, most):
    step = most if size % most == 0 else size
    return [(at, step) for at in range(0, size, step)]


def partner(s, p, n):
    if n & (n - 1) == 0:
        return s ^ p
    return (s + p) % n if isinstance(s, int) else lax.rem(s + p, n)


def crossed(k, q):
    return partner(k, 1, q) if q > 1 else k


def following(s, p, n):
    return (s + p) % n if isinstance(s, int) else lax.rem(s + p, n)


def joined(refs, axis):
    return jnp.concatenate([ref[...] for ref in refs], axis=axis)


def lane_packs(bins, side):
    packs = max(1, 128 // bins)
    return packs if (side // packs) % 16 == 0 else 1


def forward_kernel(q, *refs):
    sources, (pair, w_gate, w_up, w_out, w_head, marks, sends), scratch = refs[:6], refs[6:13], refs[13:]
    targets, halves, hidden, sems = scratch
    _, side, width = pair.shape
    edge = sources[0].shape[0]
    bins = w_head.shape[0]
    copies = [
        pltpu.make_async_copy(source, target, sems.at[i])
        for i, (source, target) in enumerate(zip(sources[1:], (w_gate, w_up, w_out, w_head, targets)))
    ]
    pieces = [
        pltpu.make_async_copy(
            sources[0].at[:, h * edge : (h + 1) * edge, :], pair.reshape(q, edge, edge, width).at[h], sems.at[5 + h]
        )
        for h in range(q)
    ]
    for copy in pieces + copies:
        copy.start()
    own = lax.rem(lax.axis_index("row"), q)
    for copy in pieces:
        copy.wait()
    flat = pair[...].reshape(q * side, width)
    inputs = normalize(flat)[0].astype(bf16)
    for copy in copies[:2]:
        copy.wait()
    for at, step in chunks_of(w_gate.shape[1], 256):
        w_half = w_gate[:, at : at + step] * 0.5
        for top, tall in chunks_of(q * side, 512):
            half = nn(inputs[top : top + tall], w_half)
            upper = nn(inputs[top : top + tall], w_up[:, at : at + step])
            hidden[top : top + tall, at : at + step] = (half * (1.0 + jnp.tanh(half)) * upper).astype(bf16)
    for copy in copies[2:]:
        copy.wait()
    total = flat.astype(f32) + nn(hidden[...], w_out[...])
    logit = nt(total.astype(bf16), w_head[...]).astype(bf16)
    packs = lane_packs(bins, side)
    deep = side // packs
    for h in range(q):
        piece = logit[h * side : (h + 1) * side]
        if packs > 1:
            piece = jnp.concatenate([piece[u * deep : (u + 1) * deep] for u in range(packs)], axis=1)
        halves[h] = piece
        mark = targets[:, h * edge : (h + 1) * edge].astype(f32)
        marks[h] = jnp.concatenate([mark, jnp.zeros((edge, width - edge), f32)], axis=1).astype(bf16)
    for p in range(q):
        sends[p] = halves[partner(own, p, q)]


def lend_kernel(q, pair, marks, *lent):
    own = lax.rem(lax.axis_index("row"), q)
    side = pair.shape[1]
    for p in range(1, q):
        first, second = lent[2 * p - 2 : 2 * p]
        block = pair[partner(own, p, q)]
        first[...] = block[: side // 2]
        second[: side // 2] = block[side // 2 :]
        second[side // 2 :] = marks[partner(own, p, q)]


def prepare_kernel(q, p, *refs):
    if p:
        first, second, refs = refs[0], refs[1], refs[2:]
        side = 2 * first.shape[0]
        edge = second.shape[0] - first.shape[0]
        flat = jnp.concatenate([first[...], second[: side // 2]], axis=0)
        mark = second[side // 2 :]
    else:
        own = lax.rem(lax.axis_index("row"), q)
        side, edge = refs[0].shape[1], refs[1].shape[1]
        flat, mark, refs = refs[0][own], refs[1][own], refs[2:]
    w_gate, w_up, w_out, w_head, inputs_t, updated_t, hidden, slope, swish, logits, onehot, normed, scale = refs
    width, bins = flat.shape[1], w_head.shape[0]
    flat = nn(exchange(side), flat).astype(bf16)
    normal, scale_inv = normalize(flat)
    normed[...] = normal
    scale[...] = jnp.broadcast_to(scale_inv, normal.shape)
    inputs = normal.astype(bf16)
    inputs_t[...] = inputs.T
    total = flat.astype(f32)
    for at, step in chunks_of(w_gate.shape[1], 256):
        span = slice(at, at + step)
        half = nn(inputs, w_gate[:, span] * 0.5)
        upper = nn(inputs, w_up[:, span])
        curve = jnp.tanh(half)
        raised = 1.0 + curve
        swished = half * raised
        hidden_part = (swished * upper).astype(bf16)
        swish[:, span] = swished
        hidden[:, span] = hidden_part
        slope[:, span] = upper * (0.5 * raised) * (1.0 + half * (1.0 - curve))
        total = total + nn(hidden_part, w_out[span, :])
    upd = total.astype(bf16)
    updated_t[...] = upd.T
    logits[...] = nt(upd, w_head[...]).astype(bf16)
    shift = edge.bit_length() - 1
    rows = lax.broadcasted_iota(jnp.int32, (side, edge), 0) & (edge - 1)
    pick = jnp.where(rows == lax.broadcasted_iota(jnp.int32, (side, edge), 1), 1.0, 0.0).astype(bf16)
    columns = lax.broadcasted_iota(jnp.int32, (side, width), 0) >> shift
    mask = columns == lax.broadcasted_iota(jnp.int32, (side, width), 1)
    lanes = lax.broadcasted_iota(jnp.int32, (side, bins), 1).astype(f32)
    picked = jnp.where(mask, nn(pick, mark), 0.0).astype(bf16)
    wanted = nn(picked, jnp.ones((width, bins), bf16))
    onehot[...] = jnp.where(wanted == lanes, 1.0, 0.0)


def backward_kernel(q, packed, *refs):
    blocks, (w_out, w_head, far, near), rest = [refs[7 * p : 7 * p + 7] for p in range(q)], refs[7 * q : 7 * q + 4], refs[7 * q + 4 :]
    (d_updated, d_gate, d_up), hot, mirrored = rest[:3], rest[3:-1], rest[-1]
    (width, side), units, bins = blocks[0][0].shape, w_out.shape[0], w_head.shape[0]
    packs = lane_packs(bins, side)
    own = lax.rem(lax.axis_index("row"), q)
    inside = lax.axis_index("row") // q == lax.axis_index("col")

    @pl.when(inside)
    def _():
        mirrored[...] = near[...]

    @pl.when(jnp.logical_not(inside))
    def _():
        mirrored[...] = far[...]

    inputs_t, updated_t, hidden, slope, swish, logits, onehot = zip(*blocks)
    mirror = jnp.concatenate([mirrored[p, :, u * bins : (u + 1) * bins] for p in range(q) for u in range(packs)], axis=0)
    summed = joined(logits, 0).astype(f32) + mirror.astype(f32)
    powers = jnp.exp(summed - jnp.max(summed, axis=-1, keepdims=True))
    probs = powers / jnp.sum(powers, axis=-1, keepdims=True)
    grad_sym = (probs - joined(onehot, 0)).astype(bf16)
    cotangent = (grad_sym.astype(f32) * 2.0).astype(bf16)
    d_upd = nn(cotangent, w_head[...])
    d_updated[...] = d_upd
    d_upd_b = d_upd.astype(bf16)
    for p in range(q):
        for top, tall in chunks_of(side, 128):
            row = slice(p * side + top, p * side + top + tall)
            for at, step in chunks_of(units, 256):
                span = slice(at, at + step)
                d_hidden = nt(d_upd_b[row], w_out[span, :])
                d_gate[row, span] = (d_hidden * slope[p][top : top + tall, span]).astype(bf16)
                d_up[row, span] = (d_hidden * swish[p][top : top + tall, span]).astype(bf16)
    depth = joined(inputs_t, 1)
    totals = (
        nn(depth, d_gate[...]),
        nn(depth, d_up[...]),
        nn(d_upd_b.T, joined(hidden, 0)),
        nn(joined(updated_t, 1), cotangent),
    )
    if not packed:
        for ref, term in zip(hot, totals):
            ref[...] = term.astype(ref.dtype)
        return
    gate_term, up_term, out_term, head_term = totals
    hot, slots = hot[:-1], hot[-1]
    nrow, ncol = packed
    groups = nrow // q
    lanes, part, tall = units // ncol, width // nrow, units // nrow
    narrow = width // ncol
    fold = lanes // tall
    short = narrow // fold
    for k in range(q):
        for a in range(groups):
            r = a * q + k
            for c in range(ncol):
                for n, term in enumerate((gate_term, up_term)):
                    block = term[r * part : (r + 1) * part, c * lanes : (c + 1) * lanes]
                    slots[k, a, (n * ncol + c) * part : (n * ncol + c + 1) * part] = block.astype(bf16)
                at = 2 * ncol * part + c * short
                block = out_term[c * narrow : (c + 1) * narrow, r * tall : (r + 1) * tall]
                block = jnp.concatenate([block[v * short : (v + 1) * short] for v in range(fold)], axis=1)
                slots[k, a, at : at + short] = block.astype(bf16)
            at = 2 * ncol * part + ncol * short
            block = head_term[r * part : (r + 1) * part, :]
            block = jnp.concatenate([block, jnp.zeros((part, lanes - bins), f32)], axis=1)
            slots[k, a, at : at + part] = block.astype(bf16)
    mine, level = lax.axis_index("row") // q, lax.axis_index("col")
    at = 2 * ncol * part + ncol * short
    lane = lax.broadcasted_iota(jnp.int32, (part, lanes), 1)
    here = (lane >= level * (bins // ncol)) & (lane < (level + 1) * (bins // ncol))
    for n in range(q):
        core = partner(own, n, q)
        for a in range(groups):
            same = jnp.where(mine == a, crossed(core, q), core)
            other = jnp.where(mine == a, core, crossed(core, q))
            for c in range(ncol):
                k = jnp.where(level == c, other, same)
                for m in (c, ncol + c):
                    hot[n][a, m * part : (m + 1) * part] = slots[k, a, m * part : (m + 1) * part]
                row = slice(2 * ncol * part + c * short, 2 * ncol * part + (c + 1) * short)
                hot[n][a, row] = slots[k, a, row]
            head = jnp.where(here, slots[other, a, at : at + part].astype(f32), slots[same, a, at : at + part].astype(f32))
            hot[n][a, at : at + part] = head.astype(bf16)


def input_kernel(p, d_updated, d_gate, d_up, normed, scale, w_gate, w_up, result):
    side = result.shape[0]
    row = slice(p * side, (p + 1) * side)
    d_inputs = nt(d_gate[row], w_gate[...]) + nt(d_up[row], w_up[...])
    normal = normed[...]
    d_norm = (
        d_inputs
        - jnp.mean(d_inputs, axis=-1, keepdims=True)
        - normal * jnp.mean(d_inputs * normal, axis=-1, keepdims=True)
    ) * scale[...]
    result[...] = (d_updated[row] + d_norm).astype(bf16)


def place_kernel(q, *refs):
    blocks, d_pair = refs[:-1], refs[-1]
    edge, _, _, width = d_pair.shape
    own = lax.rem(lax.axis_index("row"), q)
    back = exchange(edge * edge)
    for p in range(q):
        block = joined(blocks[2 * p - 1 : 2 * p + 1], 0) if p else blocks[0][...]
        d_pair[:, partner(own, p, q)] = nn(back, block).astype(bf16).reshape(edge, edge, width)


def core_sum_kernel(q, groups, *rest):
    terms, blocks, hot, handed = rest[:q], rest[q : 2 * q - 1], rest[2 * q - 1 : 2 - 2 * q], rest[2 - 2 * q :]
    mine = lax.axis_index("row") // q
    for p in range(groups):
        a = following(mine, p, groups)
        total = terms[0][a].astype(f32)
        for term in terms[1:]:
            total = total + term[a].astype(f32)
        hot[p][...] = total.astype(bf16)
    for p, block in enumerate(blocks):
        half = block.shape[0] // 2
        handed[2 * p][...] = block[:half]
        handed[2 * p + 1][...] = block[half:]


def chip_sum_kernel(q, groups, ncol, shapes, *rest):
    terms, hot, slots = rest[:groups], rest[groups:-1], rest[-1]
    part, lanes, short, tall, few = shapes
    total = terms[0][...].astype(f32)
    for term in terms[1:]:
        total = total + term[...].astype(f32)
    at = 2 * ncol * part
    head = total[at + ncol * short : at + ncol * short + part]
    for c in range(ncol):
        slots[c, 0:part] = total[c * part : (c + 1) * part].astype(bf16)
        slots[c, part : 2 * part] = total[(ncol + c) * part : (ncol + c + 1) * part].astype(bf16)
        slots[c, 2 * part : 2 * part + short] = total[at + c * short : at + (c + 1) * short].astype(bf16)
        piece = jnp.concatenate([head[:, c * few : (c + 1) * few], jnp.zeros((part, lanes - few), f32)], axis=1)
        slots[c, 2 * part + short : 3 * part + short] = piece.astype(bf16)
    for p in range(ncol):
        hot[p][...] = slots[partner(lax.axis_index("col"), p, ncol)]


def col_sum_kernel(shapes, factor, *rest):
    terms, (gate, up, out, head) = rest[:-4], rest[-4:]
    part, lanes, tall, few = shapes
    total = terms[0][...].astype(f32)
    for term in terms[1:]:
        total = total + term[...].astype(f32)
    total = total * factor
    fold = lanes // tall
    short = out.shape[0] // fold
    gate[...] = total[0:part]
    up[...] = total[part : 2 * part]
    for v in range(fold):
        out[v * short : (v + 1) * short, :] = total[2 * part : 2 * part + short, v * tall : (v + 1) * tall]
    head[...] = total[2 * part + short : 3 * part + short, 0:few]


def core_pairs(nrow, q, p):
    return [(s, s - s % q + partner(s % q, p, q)) for s in range(nrow)]


def shaped(shape, kind):
    return jax.ShapeDtypeStruct(shape, kind)


def cost(flops, moved):
    return pl.CostEstimate(flops=flops, bytes_accessed=moved, transcendentals=0)


def body(pair, targets, w_gate, w_up, w_out, w_head):
    rows, cols, width = pair.shape
    units = w_gate.shape[1]
    bins = w_head.shape[1]
    nrow, ncol = lax.axis_size("row"), lax.axis_size("col")
    q = nrow // ncol
    groups = nrow // q
    side = rows * cols // q
    packs = lane_packs(bins, side)
    head_t = w_head.T
    piece = (side // packs, bins * packs)

    sources = (pair, w_gate, w_up, w_out, head_t, targets)
    pair, w_gate, w_up, w_out, head_t, marks, sends = pl.pallas_call(
        functools.partial(forward_kernel, q),
        out_shape=[shaped((q, side, width), bf16)]
        + [shaped(x.shape, bf16) for x in sources[1:5]]
        + [shaped((q, rows, width), bf16), shaped((q, *piece), bf16)],
        in_specs=[HBM] * 6,
        out_specs=[VMEM] * 7,
        scratch_shapes=[
            pltpu.VMEM((rows, cols), jnp.int32),
            pltpu.VMEM((q, *piece), bf16),
            pltpu.VMEM((q * side, units), bf16),
            pltpu.SemaphoreType.DMA((5 + q,)),
        ],
        compiler_params=PARAMS,
        name="forward",
    )(*(pltpu.with_memory_space_constraint(x, pltpu.HBM) for x in sources))

    pairs = [
        (r * ncol + c, (q * c + (partner(r % q, 1, q) if q == 2 and r // q == c else r % q)) * ncol + r // q)
        for r in range(nrow)
        for c in range(ncol)
    ]
    far = lax.ppermute(sends, ("row", "col"), pairs)
    lent = pl.pallas_call(
        functools.partial(lend_kernel, q),
        out_shape=[shaped((side // 2, width), bf16), shaped((side // 2 + rows, width), bf16)] * (q - 1),
        in_specs=[VMEM] * 2,
        out_specs=[VMEM] * (2 * q - 2),
        compiler_params=PARAMS,
        name="lend",
    )(pair, marks)
    borrowed = [lax.ppermute(x, "row", core_pairs(nrow, q, n // 2 + 1)) for n, x in enumerate(lent)]
    prepared = []
    for p in range(q):
        source = borrowed[2 * p - 2 : 2 * p] if p else (pair, marks)
        prepared.append(
            pl.pallas_call(
                functools.partial(prepare_kernel, q, p),
                out_shape=[
                    shaped((width, side), bf16),
                    shaped((width, side), bf16),
                    shaped((side, units), bf16),
                    shaped((side, units), f32),
                    shaped((side, units), f32),
                    shaped((side, bins), bf16),
                    shaped((side, bins), f32),
                    shaped((side, width), f32),
                    shaped((side, width), f32),
                ],
                in_specs=[VMEM] * (len(source) + 4),
                out_specs=[VMEM] * 9,
                compiler_params=PARAMS,
                cost_estimate=cost(0, 0) if p else cost(6 * side * width * units, 8 * side * units),
                name="prepare",
            )(*source, w_gate, w_up, w_out, head_t)
        )

    part, tall, few = width // nrow, units // nrow, bins // ncol
    lanes = units // ncol
    short = width // ncol * tall // lanes
    fits = part % 16 == 0 and lanes == 128 and lanes % tall == 0 and bins <= lanes and short % 16 == 0
    height = 2 * ncol * part + ncol * short + part
    if fits:
        hot_shapes = [shaped((groups, height, lanes), bf16)] * q
        scratch = [pltpu.VMEM((q, groups, height, lanes), bf16)]
    else:
        hot_shapes = [shaped((width, n), bf16) for n in (units, units, units, bins)]
        scratch = []
    results = pl.pallas_call(
        functools.partial(backward_kernel, q, (nrow, ncol) if fits else None),
        out_shape=[shaped((q * side, width), f32)] + [shaped((q * side, units), bf16)] * 2 + hot_shapes,
        in_specs=[VMEM] * (7 * q + 4),
        out_specs=[VMEM] * (3 + len(hot_shapes)),
        scratch_shapes=scratch + [pltpu.VMEM((q, *piece), bf16)],
        compiler_params=PARAMS,
        cost_estimate=cost(8 * q * side * width * units, 4 * q * side * units),
        name="backward",
    )(*(x for block in prepared for x in block[:7]), w_out, head_t, far, sends)
    hot = list(results[3:])

    def d_inputs(p):
        return pl.pallas_call(
            functools.partial(input_kernel, p),
            out_shape=shaped((side, width), bf16),
            in_specs=[VMEM] * 7,
            out_specs=VMEM,
            compiler_params=PARAMS,
            cost_estimate=cost(4 * side * width * units, 4 * side * units),
            name="d_inputs",
        )(*results[:3], *prepared[p][7:], w_gate, w_up)

    d_blocks = [d_inputs(p) for p in range(q)]

    def returned(blocks):
        moved = [lax.ppermute(x, "row", core_pairs(nrow, q, n // 2 + 1)) for n, x in enumerate(blocks[1:])]
        return blocks[:1] + moved

    def placed(blocks):
        return pl.pallas_call(
            functools.partial(place_kernel, q),
            out_shape=shaped((rows, q, cols // q, width), bf16),
            in_specs=[VMEM] * (2 * q - 1),
            out_specs=VMEM,
            compiler_params=PARAMS,
            name="place",
        )(*blocks).reshape(rows, cols, width)

    factor = 1.0 / (rows * nrow)
    if not fits:
        owned = []
        hot[2] = hot[2].T
        for term in hot:
            mine = lax.psum_scatter(term, "row", scatter_dimension=0, tiled=True).astype(f32)
            owned.append(lax.psum_scatter(mine, "col", scatter_dimension=1, tiled=True) * factor)
        d_blocks = d_blocks[:1] + [half for block in d_blocks[1:] for half in (block[: side // 2], block[side // 2 :])]
        return (placed(returned(d_blocks)), *owned)

    terms = [hot[0]]
    for p in range(1, q):
        terms.append(lax.ppermute(hot[p], "row", core_pairs(nrow, q, p)))
    terms, d_blocks = lax.optimization_barrier((terms, d_blocks))
    hot = pl.pallas_call(
        functools.partial(core_sum_kernel, q, groups),
        out_shape=[shaped((height, lanes), bf16)] * groups + [shaped((side // 2, width), bf16)] * (2 * q - 2),
        in_specs=[VMEM] * (2 * q - 1),
        out_specs=[VMEM] * (groups + 2 * q - 2),
        compiler_params=PARAMS,
        name="core_sum",
    )(*terms, *d_blocks[1:])
    hot, d_blocks = hot[:groups], d_blocks[:1] + list(hot[groups:])
    terms = [hot[0]]
    for p in range(1, groups):
        terms.append(lax.ppermute(hot[p], "row", [(s, following(s // q, p, groups) * q + crossed(s % q, q)) for s in range(nrow)]))
    terms, d_blocks = lax.optimization_barrier((terms, returned(d_blocks)))
    low = 3 * part + short
    hot = pl.pallas_call(
        functools.partial(chip_sum_kernel, q, groups, ncol, (part, lanes, short, tall, few)),
        out_shape=[shaped((low, lanes), bf16)] * ncol,
        in_specs=[VMEM] * groups,
        out_specs=[VMEM] * ncol,
        scratch_shapes=[pltpu.VMEM((ncol, low, lanes), bf16)],
        compiler_params=PARAMS,
        name="chip_sum",
    )(*terms)
    terms = [hot[0]]
    for p in sorted(range(1, ncol), key=lambda p: (p != ncol // 2, -p)):
        pairs = [
            (r * ncol + c, (r - r % q + crossed(r % q, q)) * ncol + partner(c, p, ncol))
            for r in range(nrow)
            for c in range(ncol)
        ]
        terms.append(lax.ppermute(hot[p], ("row", "col"), pairs))
    *terms, d_pair = lax.optimization_barrier((*terms, placed(d_blocks)))
    gate, up, out, head = pl.pallas_call(
        functools.partial(col_sum_kernel, (part, lanes, tall, few), factor),
        out_shape=[
            shaped((part, lanes), f32),
            shaped((part, lanes), f32),
            shaped((width // ncol, tall), f32),
            shaped((part, few), f32),
        ],
        in_specs=[VMEM] * ncol,
        out_specs=[VMEM] * 4,
        compiler_params=PARAMS,
        name="col_sum",
    )(*terms)
    return d_pair, gate, up, out.T, head


def solution(mesh):
    placed = (P("row", "col", None), P("row", "col"), P(), P(), P(), P())
    return jax.shard_map(
        body,
        mesh=mesh,
        in_specs=placed,
        out_specs=(P("row", "col", None), P("row", "col"), P("row", "col"), P("row", "col"), P("row", "col")),
        check_vma=False,
    )
```
